256 devices in a mesh: seq: 8 (over x, core), tensor: 4 (over y), dp: 8 (over z).
Axes of the slice: x: 4, y: 4, z: 8, core: 2. Of those that a mesh axis runs over, the one named last changes fastest.
Arguments:
- inputs: bfloat16 [8, 2048, 3584], P('dp', 'seq'), may hold values from -6 to 6
- w_query: bfloat16 [3584, 2048], P(('seq', 'dp'), 'tensor'), may hold values from -0.09375 to 0.09375
- w_key: bfloat16 [3584, 1024], P(('seq', 'dp'), 'tensor'), may hold values from -0.09375 to 0.09375
- w_value: bfloat16 [3584, 1024], P(('seq', 'dp'), 'tensor'), may hold values from -0.09375 to 0.09375
- norm_gain: float32 [3584], replicated, may hold values from 0.1 to 1.9
- attn_grad: bfloat16 [8, 2048, 2048], P('dp', 'seq', 'tensor'), may hold values from -200 to 200
Outputs:
- grad_query: float32 [3584, 2048], P(('seq', 'dp'), 'tensor')
- grad_key: float32 [3584, 1024], P(('seq', 'dp'), 'tensor')
- grad_value: float32 [3584, 1024], P(('seq', 'dp'), 'tensor')
- input_grad: bfloat16 [8, 2048, 3584], P('dp', 'seq', 'tensor')
The draws below stay inside these ranges and needn't reach their ends.
All inputs are finite; a program needn't handle non-finite values.
Results may differ from the reference program's by a relative error of at most 0.01.
Values may be sent and summed in bfloat16 or wider, within the bound.
No kernel may reach another device: no remote copies, remote signals or barrier semaphores. Data moves between devices by JAX's collectives and lax.ppermute only.
A program may use at most 64 MiB of HBM per device.

```python
import math
import jax
import jax.numpy as jnp
from jax import lax

D = 3584
H = 8
KVH = 4
HD = 256
TOK_DEV = 256
LENGTH = 2048
WINDOW = 256
EXAMPLES = 8


def draw_attn_grad(key, part):
    split_keys = jax.random.split(jax.random.fold_in(key, 17), 3)
    full_shape = (EXAMPLES, LENGTH, H * HD)
    base_draw = jnp.clip(jax.random.normal(split_keys[0], full_shape, jnp.float32), -4.0, 4.0)
    row_scale = jnp.exp(jax.random.uniform(split_keys[1], (EXAMPLES, LENGTH, 1), jnp.float32, math.log(0.3), math.log(3.0)))
    rising = 1.0 + 2.0 * jnp.arange(LENGTH).astype(jnp.float32)[None, :, None] / (LENGTH - 1)
    col_scale = jnp.exp(jax.random.uniform(split_keys[2], (1, 1, H * HD), jnp.float32, math.log(0.3), math.log(3.0)))
    return (base_draw * row_scale * rising * col_scale).astype(jnp.bfloat16)


def block_scale(key, shape, shards, smallest, top_value):
    def one(axis_at, blocks):
        steps = jax.random.uniform(jax.random.fold_in(jax.random.fold_in(key, 6), axis_at), (blocks,), jnp.float32, smallest / len(shards), top_value / len(shards))
        return jnp.repeat(jnp.exp(steps), shape[axis_at] // blocks).reshape((-1,) + (1,) * (len(shape) - axis_at - 1))

    level = one(*shards[0])
    for cut in shards[1:]:
        level = level * one(*cut)
    return level


def centred(key, dims, scale, bound, cuts=(), kind=jnp.bfloat16):
    entries = scale * jax.random.normal(key, dims, jnp.float32)
    if cuts:
        entries = entries * block_scale(key, dims, cuts, -0.22, 0.18)
    return jnp.clip(entries, -bound, bound).astype(kind)


def setup_inputs(seed: int = 0) -> dict:
    key_of = jax.random.split(jax.random.key(seed), 7)
    return {
        "inputs": centred(key_of[0], (EXAMPLES, LENGTH, D), 1.0, 6.0, ((0, 8), (1, 8))),
        "w_query": centred(key_of[1], (D, H * HD), D ** -0.5, 0.09375, ((0, 64), (1, 4))),
        "w_key": centred(key_of[2], (D, KVH * HD), D ** -0.5, 0.09375, ((0, 64), (1, 4))),
        "w_value": centred(key_of[3], (D, KVH * HD), D ** -0.5, 0.09375, ((0, 64), (1, 4))),
        "norm_gain": jnp.clip(1.0 + 0.18 * jax.random.normal(key_of[4], (D,), jnp.float32), 0.1, 1.9),
        "attn_grad": draw_attn_grad(jax.random.fold_in(key_of[6], 71), 0),
    }


EPSILON = 1e-06
SOFTCAP = 50.0
CLIP_BOUND = 1.0
ROPE_BASE = 10000.0

def angles(positions, head_width):
    frequency = ROPE_BASE ** (-2.0 * jnp.arange(head_width // 2).astype(jnp.float32) / head_width)
    phases = positions.astype(jnp.float32)[:, None] * frequency[None, :]
    return (jnp.cos(phases)[:, None, :], jnp.sin(phases)[:, None, :])

def rotate(vectors, cosine, sine_part, direction):
    half_width = vectors.shape[-1] // 2
    first_half = vectors[..., :half_width]
    second_half = vectors[..., half_width:]
    return jnp.concatenate([first_half * cosine - direction * second_half * sine_part, second_half * cosine + direction * first_half * sine_part], -1)

def attend(queries, key_rows, value_rows, query_pos, key_pos, cotangent):
    query_count, head_count, head_width = queries.shape
    kv_heads = key_rows.shape[1]
    group_size = head_count // kv_heads
    grouped_query = queries.reshape(query_count, kv_heads, group_size, head_width).astype(jnp.float32)
    grouped_cot = cotangent.reshape(query_count, kv_heads, group_size, head_width).astype(jnp.float32)
    key_float = key_rows.astype(jnp.float32)
    value_float = value_rows.astype(jnp.float32)
    inv_scale = 1.0 / math.sqrt(head_width)
    logits = jnp.einsum('tkgd,skd->kgts', grouped_query, key_float) * inv_scale
    squash = jnp.tanh(logits / SOFTCAP)
    allowed = (key_pos[None, :] <= query_pos[:, None]) & (key_pos[None, :] > query_pos[:, None] - WINDOW) & (key_pos[None, :] >= 0)
    exp_terms = jnp.where(allowed, jnp.exp(SOFTCAP * squash), 0.0)
    softmax = exp_terms / lax.optimization_barrier(jnp.sum(exp_terms, -1, keepdims=True))
    probs_low = softmax.astype(jnp.bfloat16).astype(jnp.float32)
    dsoftmax = jnp.einsum('tkgd,skd->kgts', grouped_cot, value_float)
    value_grads = jnp.einsum('kgts,tkgd->skd', probs_low, grouped_cot)
    row_delta = lax.optimization_barrier(jnp.sum(softmax * dsoftmax, -1, keepdims=True))
    dlogits = (softmax * (dsoftmax - row_delta) * (1.0 - squash * squash) * inv_scale).astype(jnp.bfloat16).astype(jnp.float32)
    dquery = jnp.einsum('kgts,skd->tkgd', dlogits, key_float).reshape(query_count, head_count, head_width)
    key_grads = jnp.einsum('kgts,tkgd->skd', dlogits, grouped_query)
    return (dquery, key_grads, value_grads)

def example_terms(inputs_one, w_all, norm_gain, cot_one):
    seq_len = inputs_one.shape[0]
    width_q = H * HD
    width_k = KVH * HD
    widened = inputs_one.astype(jnp.float32)
    inverse_rms = lax.rsqrt(lax.optimization_barrier(jnp.mean(widened * widened, -1)) + EPSILON)
    normed = (widened * inverse_rms[:, None] * norm_gain[None, :]).astype(jnp.bfloat16)
    projected = jnp.dot(normed, w_all, preferred_element_type=jnp.float32)
    positions = jnp.arange(seq_len, dtype=jnp.int32)
    cosine, sine_part = angles(positions, HD)
    rotated_query = rotate(projected[:, :width_q].reshape(seq_len, H, HD), cosine, sine_part, 1.0).astype(jnp.bfloat16)
    rotated_keys = rotate(projected[:, width_q:width_q + width_k].reshape(seq_len, KVH, HD), cosine, sine_part, 1.0).astype(jnp.bfloat16)
    value_rows = projected[:, width_q + width_k:].reshape(seq_len, KVH, HD).astype(jnp.bfloat16)
    block_count = seq_len // TOK_DEV
    query_blocks = rotated_query.reshape(block_count, TOK_DEV, H, HD)
    key_blocks = rotated_keys.reshape(block_count, TOK_DEV, KVH, HD)
    value_blocks = value_rows.reshape(block_count, TOK_DEV, KVH, HD)
    zero_block = jnp.zeros_like(key_blocks[:1])
    key_ext = jnp.concatenate([jnp.concatenate([zero_block, key_blocks[:-1]], 0), key_blocks], 1)
    value_ext = jnp.concatenate([jnp.concatenate([zero_block, value_blocks[:-1]], 0), value_blocks], 1)
    cot_blocks = cot_one.reshape(block_count, TOK_DEV, H * HD)
    block_starts = jnp.arange(block_count, dtype=jnp.int32) * TOK_DEV

    def one_block(block_args):
        query_b, key_b, value_b, cot_b, first_row = block_args
        query_pos = first_row + jnp.arange(TOK_DEV, dtype=jnp.int32)
        key_pos = first_row - TOK_DEV + jnp.arange(2 * TOK_DEV, dtype=jnp.int32)
        return attend(query_b, key_b, value_b, query_pos, key_pos, cot_b)
    dquery, key_ext_grad, value_ext_grad = lax.map(one_block, (query_blocks, key_ext, value_ext, cot_blocks, block_starts))
    zero_grad = jnp.zeros_like(key_ext_grad[:1, :TOK_DEV])
    key_grads = key_ext_grad[:, TOK_DEV:] + jnp.concatenate([key_ext_grad[1:, :TOK_DEV], zero_grad], 0)
    value_grads = value_ext_grad[:, TOK_DEV:] + jnp.concatenate([value_ext_grad[1:, :TOK_DEV], zero_grad], 0)
    dquery = rotate(dquery.reshape(seq_len, H, HD), cosine, sine_part, -1.0)
    key_grads = rotate(key_grads.reshape(seq_len, KVH, HD), cosine, sine_part, -1.0)
    d_out = jnp.concatenate([dquery.reshape(seq_len, width_q), key_grads.reshape(seq_len, width_k), value_grads.reshape(seq_len, width_k)], 1).astype(jnp.bfloat16)
    example_grad = jnp.dot(normed.T, d_out, preferred_element_type=jnp.float32)
    dnormed = lax.dot_general(d_out, w_all, (((1,), (1,)), ((), ())), preferred_element_type=jnp.float32)
    scaled = norm_gain[None, :] * dnormed
    mean_term = lax.optimization_barrier(jnp.mean(widened * scaled, -1, keepdims=True))
    input_grad = (inverse_rms[:, None] * scaled - widened * (inverse_rms ** 3)[:, None] * mean_term).astype(jnp.bfloat16)
    return (example_grad, input_grad)

def reference(inputs, w_query, w_key, w_value, norm_gain, attn_grad):
    width_q = H * HD
    width_k = KVH * HD
    w_all = jnp.concatenate([w_query, w_key, w_value], 1)
    entry_count = D * (H + 2 * KVH) * HD

    def step_example(summed, example_args):
        inputs_one, cot_one = example_args
        example_grad, input_grad = example_terms(inputs_one, w_all, norm_gain, cot_one)
        grad_rms = jnp.sqrt(jnp.sum(example_grad * example_grad) / entry_count + EPSILON)
        factor = CLIP_BOUND / jnp.maximum(grad_rms, CLIP_BOUND)
        return (summed + factor * example_grad, input_grad)
    summed, input_grad = lax.scan(step_example, jnp.zeros((D, w_all.shape[1]), jnp.float32), (inputs, attn_grad))
    return (summed[:, :width_q], summed[:, width_q:width_q + width_k], summed[:, width_q + width_k:], input_grad)
```

```python
import functools
import math

import jax
import jax.numpy as jnp
import numpy as np
from jax import lax
from jax.experimental import pallas as pl
from jax.experimental.pallas import tpu as pltpu
from jax.sharding import PartitionSpec as P

D = 3584
H = 8
KVH = 4
HD = 256
WINDOW = 256
SLAB = D // 4
ROWS = 56
TOK = 256

EPSILON = 1e-06
SOFTCAP = 50.0
CLIP_BOUND = 1.0
ROPE_BASE = 10000.0

F32 = jnp.float32
BF16 = jnp.bfloat16
VMEM = pl.BlockSpec(memory_space=pltpu.VMEM)
SMEM = pl.BlockSpec(memory_space=pltpu.SMEM)


def call(body, outs, place, *operands, scratch=()):
    return pl.pallas_call(
        body,
        out_shape=[jax.ShapeDtypeStruct(shape, kind) for shape, kind in outs],
        in_specs=[SMEM] + [VMEM] * len(operands),
        out_specs=[VMEM] * len(outs),
        scratch_shapes=list(scratch),
        compiler_params=pltpu.CompilerParams(vmem_limit_bytes=40 * 1024 * 1024),
    )(place, *operands)


def swap(value):
    return lax.ppermute(value, "seq", [(i, i ^ 1) for i in range(8)])


def from_x(value, steps):
    return lax.ppermute(value, "seq", [((i + 2 * steps) % 8, i) for i in range(8)])


def from_y(value, steps):
    return lax.ppermute(value, "tensor", [((i + steps) % 4, i) for i in range(4)])


def from_z(value, steps):
    return lax.ppermute(value, "dp", [((i + steps) % 8, i) for i in range(8)])


def mm(a, b, contract_a=1, contract_b=0):
    return lax.dot_general(
        a, b, (((contract_a,), (contract_b,)), ((), ())), preferred_element_type=F32
    )


def norm_body(place, inputs, gain, permute, normed, moved, inverse):
    rows = inputs[...].astype(F32)
    inv = lax.rsqrt(jnp.sum(rows * rows, -1, keepdims=True) * (1.0 / D) + EPSILON)
    inverse[...] = jnp.broadcast_to(inv, inverse.shape)
    for slab in range(4):
        part = mm(inputs[:, slab * SLAB : (slab + 1) * SLAB], permute[...])
        moved[slab] = part.astype(BF16)
        normed[slab] = (part * inv * gain[slab : slab + 1, :]).astype(BF16)


def stack_body(axis, count, rows, place, *refs):
    whole = refs[-1]
    for step in range(count):
        at = lax.rem(place[axis] + step, count)
        whole[pl.ds(pl.multiple_of(at * rows, 16), rows), :] = refs[step][...]


def columns_body(place, *refs):
    mine, theirs, whole = refs[:4], refs[4:8], refs[8]
    core = place[1]
    for step in range(4):
        a = mine[step][...].T
        b = theirs[step][...].T
        first = pl.multiple_of(core * TOK, TOK)
        second = pl.multiple_of((1 - core) * TOK, TOK)
        whole[step, :, pl.ds(first, TOK)] = a
        whole[step, :, pl.ds(second, TOK)] = b


def spin(value, cosine, sine, direction):
    first, second = value[:, :128], value[:, 128:]
    return jnp.concatenate(
        [first * cosine - direction * second * sine, second * cosine + direction * first * sine], -1
    )


def project_body(place, *refs):
    own, other, cos, sin, cos2, sin2 = refs[:6]
    slabs = refs[6:10]
    strips = refs[10:17]
    half_a, half_b = refs[17:19]
    query, pair, weights = refs[19:]
    x, core, z = place[0], place[1], place[3]
    for step in range(4):
        weights[lax.rem(x + step, 4), :, :HD] = slabs[step][...]

    def put(step, ref, groups, start):
        at = pl.multiple_of(lax.rem(z + step, 8) * 112, 16)
        for k, group in enumerate(groups):
            weights[group, pl.ds(at, 112), HD:] = ref[k * 112 : (k + 1) * 112, :]

    for strip, step in zip(strips, (0, 1, 2, 3, 7, 6, 5)):
        put(step, strip, (0, 1, 2, 3), 0)
    put(4, half_a, (0, 1), 0)
    put(4, half_b, (2, 3), 2)
    for rows, block in ((own, core), (other, 1 - core)):
        total = mm(rows[0], weights[0])
        for slab in range(1, 4):
            total += mm(rows[slab], weights[slab])
        at = pl.ds(pl.multiple_of(block * TOK, TOK), TOK)
        query[at, :] = spin(total[:, :HD], cos[at, :], sin[at, :], 1.0).astype(BF16)
        pair[at, :] = spin(total[:, HD:], cos2[at, :], sin2[at, :], 1.0).astype(BF16)


def attend_body(place, query, mine, theirs, mine_before, theirs_before, cot, cos, sin,
                dquery, keep, keep_before, send, send_before, keys, values):
    first_core = place[1] == 0
    for at, a, b in ((0, mine_before, theirs_before), (TOK, mine, theirs)):
        rows = a.shape[0]
        keys[at : at + rows, :] = jnp.where(first_core, a[...], b[...])
        values[at : at + rows, :] = jnp.where(first_core, b[...], a[...])
    scale = 1.0 / math.sqrt(HD)
    q_at = lax.broadcasted_iota(jnp.int32, (TOK, 2 * TOK), 0)
    k_at = lax.broadcasted_iota(jnp.int32, (TOK, 2 * TOK), 1)
    band = (k_at <= q_at + TOK) & (k_at > q_at)
    key_parts = []
    value_parts = []
    for block in range(2):
        here = slice(block * TOK, (block + 1) * TOK)
        seen = slice(block * TOK, (block + 2) * TOK)
        q, g = query[here, :], cot[here, :]
        k, v = keys[seen, :], values[seen, :]
        squash = jnp.tanh(mm(q, k, 1, 1) * (scale / SOFTCAP))
        allowed = band
        if block == 0:
            allowed = band & ((k_at >= TOK) | (place[0] > 0))
        terms = jnp.where(allowed, jnp.exp(SOFTCAP * squash), 0.0)
        probs = terms / jnp.sum(terms, -1, keepdims=True)
        dprobs = mm(g, v, 1, 1)
        value_parts.append(mm(probs.astype(BF16), g, 0, 0))
        delta = jnp.sum(probs * dprobs, -1, keepdims=True)
        dlogits = (probs * (dprobs - delta) * (1.0 - squash * squash) * scale).astype(BF16)
        dq = mm(dlogits, k)
        dquery[here, :] = spin(dq, cos[here, :], sin[here, :], -1.0).astype(BF16)
        key_parts.append(mm(dlogits, q, 0, 0))

    def place_out(dk, dv, keep_at, send_at):
        keep_at[...] = jnp.where(first_core, dk, dv)
        send_at[...] = jnp.where(first_core, dv, dk).astype(BF16)

    place_out(key_parts[0][:TOK], value_parts[0][:TOK], keep_before, send_before)
    place_out(
        key_parts[0][TOK:] + key_parts[1][:TOK],
        value_parts[0][TOK:] + value_parts[1][:TOK],
        keep.at[:TOK, :],
        send.at[:TOK, :],
    )
    place_out(key_parts[1][TOK:], value_parts[1][TOK:], keep.at[TOK:, :], send.at[TOK:, :])


def halo_body(place, keep_before, got_before, out):
    out[...] = (keep_before[...] + got_before[...].astype(F32)).astype(BF16)


def pair_body(place, keep, got, back, cos2, sin2, dpair):
    for block in range(2):
        here = slice(block * TOK, (block + 1) * TOK)
        total = keep[here, :] + got[here, :].astype(F32)
        if block == 1:
            total += back[...].astype(F32)
        dpair[here, :] = spin(total, cos2[here, :], sin2[here, :], -1.0).astype(BF16)


def dnormed_body(place, dquery, dpair, weights, own, other, keep, send, keep_sum, send_sum):
    core = place[1]
    for rows, block, out, sums in (
        (other, 1 - core, send, send_sum),
        (own, core, keep, keep_sum),
    ):
        at = pl.ds(pl.multiple_of(block * TOK, TOK), TOK)
        dq, dp = dquery[at, :], dpair[at, :]
        total = jnp.zeros((TOK, 1), F32)
        for slab in range(4):
            part = mm(dq, weights[slab, :, :HD], 1, 1) + mm(dp, weights[slab, :, HD:], 1, 1)
            total += jnp.sum(part * rows[slab].astype(F32), -1, keepdims=True)
            out[slab] = part.astype(BF16)
        sums[...] = jnp.broadcast_to(total, sums.shape)


def split_body(place, keep, got, keep_sum, got_sum, own, own_sum, *messages):
    y = place[2]
    total = keep_sum[...] + got_sum[...]
    own_sum[...] = total
    high = total.astype(BF16)
    rest = total - high.astype(F32)
    middle = rest.astype(BF16)
    low = (rest - middle.astype(F32)).astype(BF16)
    lane = lax.broadcasted_iota(jnp.int32, total.shape, 1)
    zero = jnp.zeros_like(total)
    coded = jnp.where(
        lane == 0,
        high.astype(F32),
        jnp.where(lane == 1, middle.astype(F32), jnp.where(lane == 2, low.astype(F32), zero)),
    ).astype(BF16)
    own[...] = keep[y].astype(F32) + got[y].astype(F32)
    for step, message in enumerate(messages):
        at = lax.rem(y + 4 - (step + 1), 4)
        message[:, :SLAB] = (keep[at].astype(F32) + got[at].astype(F32)).astype(BF16)
        message[:, SLAB:] = coded


def input_body(place, own, own_sum, m1, m2, m3, moved, inverse, gain, permute, out):
    total = own[...]
    sums = own_sum[:, :1]
    for message in (m1, m2, m3):
        total += message[:, :SLAB].astype(F32)
        sums += jnp.sum(message[:, SLAB:].astype(F32), -1, keepdims=True)
    inv = inverse[:, :1]
    y = place[2]
    rows = moved[y].astype(F32)
    grad = inv * (gain[pl.ds(y, 1), :] * total) - rows * ((inv * inv) * (sums * (1.0 / D)))
    out[0] = mm(grad.astype(BF16), permute[...], 1, 1).astype(BF16)


def weights_body(place, columns, d0, d1, d2, d3, *refs):
    chunks, squares, total = refs[:8], refs[8], refs[9]
    z = place[3]
    acc = mm(columns[0], d0[...])
    for step, d in ((1, d1), (2, d2), (3, d3)):
        acc += mm(columns[step], d[...])
    total[...] = acc
    squares[...] = jnp.full(squares.shape, jnp.sum(acc * acc), F32)
    for step in range(8):
        at = lax.rem(z + 8 - step, 8)
        chunks[step][...] = total[pl.ds(pl.multiple_of(at * 112, 16), 112), :].astype(BF16)


def clip_body(place, *refs):
    halves, squares, keep, send = (refs[:8], refs[8:16]), refs[16:24], refs[24], refs[25]
    core = place[1]
    factors = []
    for total in squares:
        rms = jnp.sqrt(total[...] * (1.0 / (D * (H + 2 * KVH) * HD)) + EPSILON)
        factors.append((CLIP_BOUND / jnp.maximum(rms, CLIP_BOUND))[:1, :1])
    for half in range(2):
        total = halves[half][0][...].astype(F32) * factors[0]
        for step in range(1, 8):
            total += halves[half][step][...].astype(F32) * factors[step]
        top, bottom = total[:ROWS], total[ROWS:]
        at = slice(half * HD, (half + 1) * HD)
        keep[:, at] = jnp.where(core == 0, top, bottom)
        send[:, at] = jnp.where(core == 0, bottom, top)


def out_body(place, keep, got, grad_query, grad_key, grad_value):
    first = place[1] == 0
    mine, theirs = keep[...], got[...]
    zero = jnp.where(first, mine, theirs)
    one = jnp.where(first, theirs, mine)
    grad_query[:, :HD] = zero[:, :HD]
    grad_query[:, HD:] = one[:, :HD]
    grad_key[...] = zero[:, HD:]
    grad_value[...] = one[:, HD:]


def local(inputs, w_query, w_key, w_value, norm_gain, attn_grad):
    seq = lax.axis_index("seq").astype(jnp.int32)
    x, core = seq // 2, seq % 2
    y = lax.axis_index("tensor").astype(jnp.int32)
    z = lax.axis_index("dp").astype(jnp.int32)
    place = jnp.stack([x, core, y, z])
    first = core == 0

    low, high = w_query[:, :HD], w_query[:, HD:]
    mine = jnp.concatenate([jnp.where(first, low, high), jnp.where(first, w_key, w_value)], 1)
    theirs = jnp.concatenate([jnp.where(first, high, low), jnp.where(first, w_value, w_key)], 1)
    got = swap(theirs)
    block = jnp.concatenate([jnp.where(first, mine, got), jnp.where(first, got, mine)], 0)
    block_q, block_p = block[:, :HD], block[:, HD:]
    (strip,) = call(
        functools.partial(stack_body, 0, 4, 112),
        [((448, HD), BF16)],
        place,
        *[block_p if step == 0 else from_x(block_p, step) for step in range(4)],
    )
    ups, downs = [strip], [strip]
    for _ in range(3):
        ups.append(from_z(ups[-1], 1))
        downs.append(from_z(downs[-1], -1))
    half_a = from_z(ups[-1][:224], 1)
    half_b = from_z(downs[-1][224:], -1)
    strips = ups + downs[1:]
    (slab,) = call(
        functools.partial(stack_body, 3, 8, 112),
        [((SLAB, HD), BF16)],
        place,
        *[block_q if step == 0 else from_z(block_q, step) for step in range(8)],
    )
    slabs = [slab if step == 0 else from_x(slab, step) for step in range(4)]

    index = np.arange(SLAB)
    natural = (index % 112) // ROWS * 448 + index // 112 * ROWS + index % ROWS
    permute = (
        lax.broadcasted_iota(jnp.int32, (SLAB, SLAB), 0) == jnp.asarray(natural, jnp.int32)[None, :]
    ).astype(BF16)
    gain = norm_gain.reshape(4, 2, 8, ROWS).transpose(0, 2, 1, 3).reshape(4, SLAB)
    normed, moved, inverse = call(
        norm_body,
        [((4, TOK, SLAB), BF16), ((4, TOK, SLAB), BF16), ((TOK, 128), F32)],
        place,
        inputs[0],
        gain,
        permute,
    )
    normed_other = swap(normed)
    cot_low, cot_high = attn_grad[0][:, :HD], attn_grad[0][:, HD:]
    cot_mine = jnp.where(first, cot_low, cot_high)
    cot_got = swap(jnp.where(first, cot_high, cot_low))
    cot = jnp.concatenate(
        [jnp.where(first, cot_mine, cot_got), jnp.where(first, cot_got, cot_mine)], 0
    )

    positions = x * (2 * TOK) + jnp.arange(2 * TOK, dtype=jnp.int32)
    frequency = ROPE_BASE ** (-2.0 * jnp.arange(HD // 2).astype(F32) / HD)
    phases = positions.astype(F32)[:, None] * frequency[None, :]
    cos, sin = jnp.cos(phases), jnp.sin(phases)
    cos2, sin2 = jnp.where(first, cos, 1.0), jnp.where(first, sin, 0.0)

    query, pair, weights = call(
        project_body,
        [((2 * TOK, HD), BF16), ((2 * TOK, HD), BF16), ((4, SLAB, 2 * HD), BF16)],
        place,
        normed,
        normed_other,
        cos,
        sin,
        cos2,
        sin2,
        *slabs,
        *strips,
        half_a,
        half_b,
    )

    columns_mine = [lax.dynamic_index_in_dim(normed, x, 0, False)] + [
        from_x(lax.dynamic_index_in_dim(normed, (x + 4 - step) % 4, 0, False), step)
        for step in range(1, 4)
    ]
    columns_other = [lax.dynamic_index_in_dim(normed_other, x, 0, False)] + [
        swap(columns_mine[step]) for step in range(1, 4)
    ]
    (columns,) = call(
        columns_body, [((4, SLAB, 2 * TOK), BF16)], place, *columns_mine, *columns_other
    )

    pair_other = swap(pair)
    before = from_x(pair[TOK:], -1)
    before_other = lax.ppermute(
        pair[TOK:], "seq", [(i, ((i ^ 1) + 2) % 8) for i in range(8)]
    )
    dquery, keep, keep_before, send, send_before = call(
        attend_body,
        [
            ((2 * TOK, HD), BF16),
            ((2 * TOK, HD), F32),
            ((TOK, HD), F32),
            ((2 * TOK, HD), BF16),
            ((TOK, HD), BF16),
        ],
        place,
        query,
        pair,
        pair_other,
        before,
        before_other,
        cot,
        cos,
        sin,
        scratch=[pltpu.VMEM((3 * TOK, HD), BF16), pltpu.VMEM((3 * TOK, HD), BF16)],
    )
    got_before = swap(send_before)
    got = swap(send)
    dquery_all = [dquery] + [from_x(dquery, step) for step in range(1, 4)]
    (back,) = call(halo_body, [((TOK, HD), BF16)], place, keep_before, got_before)
    back = from_x(back, 1)
    (dpair,) = call(pair_body, [((2 * TOK, HD), BF16)], place, keep, got, back, cos2, sin2)
    dpair_all = [dpair] + [from_x(dpair, step) for step in range(1, 4)]

    keep_in, send_in, keep_sum, send_sum = call(
        dnormed_body,
        [
            ((4, TOK, SLAB), BF16),
            ((4, TOK, SLAB), BF16),
            ((TOK, 128), F32),
            ((TOK, 128), F32),
        ],
        place,
        dquery,
        dpair,
        weights,
        normed,
        normed_other,
    )
    got_in, got_sum = swap(send_in), swap(send_sum)
    own, own_sum, *messages = call(
        split_body,
        [((TOK, SLAB), F32), ((TOK, 128), F32)] + [((TOK, SLAB + 128), BF16)] * 3,
        place,
        keep_in,
        got_in,
        keep_sum,
        got_sum,
    )
    arrived = [from_y(message, step + 1) for step, message in enumerate(messages)]
    (input_grad,) = call(
        input_body,
        [((1, TOK, SLAB), BF16)],
        place,
        own,
        own_sum,
        *arrived,
        moved,
        inverse,
        gain,
        permute,
    )

    halves = []
    square = 0.0
    for parts in (dquery_all, dpair_all):
        *chunks, squares = call(
            weights_body,
            [((112, HD), BF16)] * 8 + [((8, 128), F32)],
            place,
            columns,
            *parts,
            scratch=[pltpu.VMEM((SLAB, HD), F32)],
        )
        halves += [chunk if step == 0 else from_z(chunk, step) for step, chunk in enumerate(chunks)]
        square = square + squares
    square = square + swap(square)
    square = square + from_x(square, 1) + from_x(square, 2) + from_x(square, 3)
    square = square + from_y(square, 1) + from_y(square, 2) + from_y(square, 3)
    squares = [square if step == 0 else from_z(square, step) for step in range(8)]
    keep_out, send_out = call(
        clip_body,
        [((ROWS, 2 * HD), F32), ((ROWS, 2 * HD), F32)],
        place,
        *halves,
        *squares,
    )
    got_out = swap(send_out)
    grad_query, grad_key, grad_value = call(
        out_body,
        [((ROWS, 2 * HD), F32), ((ROWS, HD), F32), ((ROWS, HD), F32)],
        place,
        keep_out,
        got_out,
    )
    return grad_query, grad_key, grad_value, input_grad


def solution(mesh):
    return jax.shard_map(
        local,
        mesh=mesh,
        in_specs=(
            P("dp", "seq", None),
            P(("seq", "dp"), "tensor"),
            P(("seq", "dp"), "tensor"),
            P(("seq", "dp"), "tensor"),
            P(),
            P("dp", "seq", "tensor"),
        ),
        out_specs=(
            P(("seq", "dp"), "tensor"),
            P(("seq", "dp"), "tensor"),
            P(("seq", "dp"), "tensor"),
            P("dp", "seq", "tensor"),
        ),
        check_vma=False,
    )
```

```python
import math

import jax
import jax.numpy as jnp
import numpy as np
from jax import lax
from jax.experimental import pallas as pl
from jax.experimental.pallas import tpu as pltpu
from jax.sharding import Mesh
from jax.sharding import PartitionSpec as P

D = 3584
H = 8
KVH = 4
HD = 256
WINDOW = 256
SLAB = D // 4
ROWS = 56
TOK = 256

EPSILON = 1e-06
SOFTCAP = 50.0
CLIP_BOUND = 1.0
ROPE_BASE = 10000.0

F32 = jnp.float32
BF16 = jnp.bfloat16
VMEM = pl.BlockSpec(memory_space=pltpu.VMEM)
SMEM = pl.BlockSpec(memory_space=pltpu.SMEM)


def call(body, outs, place, *operands, scratch=()):
    return pl.pallas_call(
        body,
        out_shape=[jax.ShapeDtypeStruct(shape, kind) for shape, kind in outs],
        in_specs=[SMEM] + [VMEM] * len(operands),
        out_specs=[VMEM] * len(outs),
        scratch_shapes=list(scratch),
        compiler_params=pltpu.CompilerParams(vmem_limit_bytes=16 * 1024 * 1024),
    )(place, *operands)


def swap(value):
    return lax.ppermute(value, "core", [(0, 1), (1, 0)])


def from_x(value, steps):
    return lax.ppermute(value, "x", [((i + steps) % 4, i) for i in range(4)])


def from_y(value, steps):
    return lax.ppermute(value, "tensor", [((i + steps) % 4, i) for i in range(4)])


def after(value, *others):
    return lax.optimization_barrier((value, *others))[0]


def code(total):
    high = total.astype(BF16)
    rest = total - high.astype(F32)
    middle = rest.astype(BF16)
    low = (rest - middle.astype(F32)).astype(BF16)
    lane = lax.broadcasted_iota(jnp.int32, total.shape, 1)
    return jnp.where(
        lane == 0,
        high.astype(F32),
        jnp.where(
            lane == 1, middle.astype(F32), jnp.where(lane == 2, low.astype(F32), jnp.zeros_like(total))
        ),
    ).astype(BF16)


def mm(a, b, contract_a=1, contract_b=0):
    return lax.dot_general(
        a, b, (((contract_a,), (contract_b,)), ((), ())), preferred_element_type=F32
    )


def norm_body(place, inputs, gain, permute, normed, moved, inverse, *apart):
    x = place[0]
    rows = inputs[...].astype(F32)
    inv = lax.rsqrt(jnp.sum(rows * rows, -1, keepdims=True) * (1.0 / D) + EPSILON)
    inverse[...] = jnp.broadcast_to(inv, inverse.shape)
    for slab in range(4):
        part = mm(inputs[:, slab * SLAB : (slab + 1) * SLAB], permute[...])
        moved[slab] = part.astype(BF16)
        normed[slab] = (part * inv * gain[slab : slab + 1, :]).astype(BF16)
    for step in range(4):
        apart[step][...] = normed[lax.rem(x + 4 - step, 4)]


def columns_body(place, *refs):
    mine, theirs, whole = refs[:4], refs[4:8], refs[8]
    x, core = place[0], place[1]
    first = pl.multiple_of(core * TOK, TOK)
    second = pl.multiple_of((1 - core) * TOK, TOK)
    for step in range(4):
        at = lax.rem(x + step, 4)
        whole[at, :, pl.ds(first, TOK)] = mine[step][...].T
        whole[at, :, pl.ds(second, TOK)] = theirs[step][...].T


def spin(value, cosine, sine, direction):
    first, second = value[:, :128], value[:, 128:]
    return jnp.concatenate(
        [first * cosine - direction * second * sine, second * cosine + direction * first * sine], -1
    )


def project_body(place, own, other, cos, sin, cos2, sin2, s0, s1, s2, s3, strip, query, pair):
    x, core = place[0], place[1]
    for rows, block in ((own, core), (other, 1 - core)):
        total_q = mm(rows[x], s0[...])
        total_p = mm(rows[0], strip[0])
        for step, slab in ((1, s1), (2, s2), (3, s3)):
            total_q += mm(rows[lax.rem(x + step, 4)], slab[...])
            total_p += mm(rows[step], strip[step])
        at = pl.ds(pl.multiple_of(block * TOK, TOK), TOK)
        query[at, :] = spin(total_q, cos[at, :], sin[at, :], 1.0).astype(BF16)
        pair[at, :] = spin(total_p, cos2[at, :], sin2[at, :], 1.0).astype(BF16)


def attend_body(place, query, mine, theirs, mine_before, theirs_before, cot, cos, sin,
                dquery, keep, keep_before, send, send_before, keys, values):
    first_core = place[1] == 0
    for at, a, b in ((0, mine_before, theirs_before), (TOK, mine, theirs)):
        rows = a.shape[0]
        keys[at : at + rows, :] = jnp.where(first_core, a[...], b[...])
        values[at : at + rows, :] = jnp.where(first_core, b[...], a[...])
    scale = 1.0 / math.sqrt(HD)
    q_at = lax.broadcasted_iota(jnp.int32, (TOK, 2 * TOK), 0)
    k_at = lax.broadcasted_iota(jnp.int32, (TOK, 2 * TOK), 1)
    band = (k_at <= q_at + TOK) & (k_at > q_at)
    key_parts = []
    value_parts = []
    for block in range(2):
        here = slice(block * TOK, (block + 1) * TOK)
        seen = slice(block * TOK, (block + 2) * TOK)
        q, g = query[here, :], cot[here, :]
        k, v = keys[seen, :], values[seen, :]
        squash = jnp.tanh(mm(q, k, 1, 1) * (scale / SOFTCAP))
        allowed = band
        if block == 0:
            allowed = band & ((k_at >= TOK) | (place[0] > 0))
        terms = jnp.where(allowed, jnp.exp(SOFTCAP * squash), 0.0)
        probs = terms / jnp.sum(terms, -1, keepdims=True)
        dprobs = mm(g, v, 1, 1)
        value_parts.append(mm(probs.astype(BF16), g, 0, 0))
        delta = jnp.sum(probs * dprobs, -1, keepdims=True)
        dlogits = (probs * (dprobs - delta) * (1.0 - squash * squash) * scale).astype(BF16)
        dq = mm(dlogits, k)
        dquery[here, :] = spin(dq, cos[here, :], sin[here, :], -1.0).astype(BF16)
        key_parts.append(mm(dlogits, q, 0, 0))

    def place_out(dk, dv, keep_at, send_at):
        keep_at[...] = jnp.where(first_core, dk, dv)
        send_at[...] = jnp.where(first_core, dv, dk).astype(BF16)

    place_out(key_parts[0][:TOK], value_parts[0][:TOK], keep_before, send_before)
    place_out(
        key_parts[0][TOK:] + key_parts[1][:TOK],
        value_parts[0][TOK:] + value_parts[1][:TOK],
        keep.at[:TOK, :],
        send.at[:TOK, :],
    )
    place_out(key_parts[1][TOK:], value_parts[1][TOK:], keep.at[TOK:, :], send.at[TOK:, :])


def halo_body(place, keep_before, got_before, out):
    out[...] = (keep_before[...] + got_before[...].astype(F32)).astype(BF16)


def pair_body(place, keep, got, back, cos2, sin2, dpair):
    for block in range(2):
        here = slice(block * TOK, (block + 1) * TOK)
        total = keep[here, :] + got[here, :].astype(F32)
        if block == 1:
            total += back[...].astype(F32)
        dpair[here, :] = spin(total, cos2[here, :], sin2[here, :], -1.0).astype(BF16)


def dnormed_body(
    place, dquery, dpair, s0, s1, s2, s3, strip, own, other, keep, send, keep_sum, send_sum
):
    x, core = place[0], place[1]
    for rows, block, out, sums in (
        (other, 1 - core, send, send_sum),
        (own, core, keep, keep_sum),
    ):
        at = pl.ds(pl.multiple_of(block * TOK, TOK), TOK)
        dq, dp = dquery[at, :], dpair[at, :]
        total = jnp.zeros((TOK, 1), F32)
        for step, slab in enumerate((s0, s1, s2, s3)):
            here = lax.rem(x + step, 4)
            part = mm(dq, slab[...], 1, 1) + mm(dp, strip[here], 1, 1)
            total += jnp.sum(part * rows[here].astype(F32), -1, keepdims=True)
            out[here] = part.astype(BF16)
        sums[...] = jnp.broadcast_to(total, sums.shape)


def split_body(place, keep, got, keep_sum, got_sum, own, own_sum, *messages):
    y = place[2]
    total = keep_sum[...] + got_sum[...]
    own_sum[...] = total
    coded = code(total)
    own[...] = keep[y].astype(F32) + got[y].astype(F32)
    for step, message in enumerate(messages):
        at = lax.rem(y + 4 - (step + 1), 4)
        message[:, :SLAB] = (keep[at].astype(F32) + got[at].astype(F32)).astype(BF16)
        message[:, SLAB:] = coded


def input_body(place, own, own_sum, m1, m2, m3, moved, inverse, gain, permute, out):
    total = own[...]
    sums = own_sum[:, :1]
    for message in (m1, m2, m3):
        total += message[:, :SLAB].astype(F32)
        sums += jnp.sum(message[:, SLAB:].astype(F32), -1, keepdims=True)
    inv = inverse[:, :1]
    y = place[2]
    rows = moved[y].astype(F32)
    grad = inv * (gain[pl.ds(y, 1), :] * total) - rows * ((inv * inv) * (sums * (1.0 / D)))
    out[0] = mm(grad.astype(BF16), permute[...], 1, 1).astype(BF16)


def weights_body(place, columns, dquery, d0, d1, d2, d3, chunks, total):
    x = place[0]
    acc = mm(columns[0], dquery[0])
    for step in range(1, 4):
        acc += mm(columns[step], dquery[step])
    square = jnp.sum(acc * acc)
    total[:, :HD] = acc
    acc = mm(columns[x], d0[...])
    for step, d in ((1, d1), (2, d2), (3, d3)):
        acc += mm(columns[lax.rem(x + step, 4)], d[...])
    square += jnp.sum(acc * acc)
    total[:, HD:] = acc
    coded = code(jnp.full((16, 2 * HD), square, F32))
    for chunk in range(8):
        chunks[chunk, :112, :] = total[chunk * 112 : (chunk + 1) * 112, :].astype(BF16)
        chunks[chunk, 112:, :] = coded


def squares_body(place, chunks, squares):
    for example in range(8):
        total = jnp.sum(chunks[example, 112:, :].astype(F32), -1, keepdims=True)
        squares[example : example + 1, :] = jnp.broadcast_to(total[:1], (1, 128))


def clip_body(place, chunks, squares, keep, send):
    core = place[1]
    rms = jnp.sqrt(squares[...] * (1.0 / (D * (H + 2 * KVH) * HD)) + EPSILON)
    factor = CLIP_BOUND / jnp.maximum(rms, CLIP_BOUND)
    total = chunks[0, :112, :].astype(F32) * factor[0:1, :1]
    for example in range(1, 8):
        total += chunks[example, :112, :].astype(F32) * factor[example : example + 1, :1]
    top, bottom = total[:ROWS], total[ROWS:]
    keep[...] = jnp.where(core == 0, top, bottom)
    send[...] = jnp.where(core == 0, bottom, top)


def out_body(place, keep, got, grad_query, grad_key, grad_value):
    first = place[1] == 0
    mine, theirs = keep[...], got[...]
    zero = jnp.where(first, mine, theirs)
    one = jnp.where(first, theirs, mine)
    grad_query[:, :HD] = zero[:, :HD]
    grad_query[:, HD:] = one[:, :HD]
    grad_key[...] = zero[:, HD:]
    grad_value[...] = one[:, HD:]


def local(inputs, w_query, w_key, w_value, norm_gain, attn_grad):
    x = lax.axis_index("x").astype(jnp.int32)
    core = lax.axis_index("core").astype(jnp.int32)
    y = lax.axis_index("tensor").astype(jnp.int32)
    z = lax.axis_index("dp").astype(jnp.int32)
    place = jnp.stack([x, core, y, z])
    first = core == 0

    low, high = w_query[:, :HD], w_query[:, HD:]
    mine = jnp.concatenate([jnp.where(first, low, high), jnp.where(first, w_key, w_value)], 1)
    theirs = jnp.concatenate([jnp.where(first, high, low), jnp.where(first, w_value, w_key)], 1)
    got = swap(theirs)
    block = jnp.concatenate([jnp.where(first, mine, got), jnp.where(first, got, mine)], 0)
    strip = lax.all_gather(block[:, HD:], ("x", "dp"), axis=0, tiled=True).reshape(4, SLAB, HD)

    index = np.arange(SLAB)
    natural = (index % 112) // ROWS * 448 + index // 112 * ROWS + index % ROWS
    permute = (
        lax.broadcasted_iota(jnp.int32, (SLAB, SLAB), 0) == jnp.asarray(natural, jnp.int32)[None, :]
    ).astype(BF16)
    gain = norm_gain.reshape(4, 2, 8, ROWS).transpose(0, 2, 1, 3).reshape(4, SLAB)
    normed, moved, inverse, *apart = call(
        norm_body,
        [((4, TOK, SLAB), BF16), ((4, TOK, SLAB), BF16), ((TOK, 128), F32)]
        + [((TOK, SLAB), BF16)] * 4,
        place,
        inputs[0],
        gain,
        permute,
    )
    columns_mine = [apart[0]] + [from_x(apart[step], step) for step in range(1, 4)]
    normed_other = swap(normed)
    columns_other = [lax.dynamic_index_in_dim(normed_other, x, 0, False)] + [
        swap(columns_mine[step]) for step in range(1, 4)
    ]
    (columns,) = call(
        columns_body, [((4, SLAB, 2 * TOK), BF16)], place, *columns_mine, *columns_other
    )

    slab = lax.all_gather(after(block[:, :HD], normed), "dp", axis=0, tiled=True)
    slabs = [slab if step == 0 else from_x(slab, step) for step in range(4)]

    cot_low, cot_high = attn_grad[0][:, :HD], attn_grad[0][:, HD:]
    cot_mine = jnp.where(first, cot_low, cot_high)
    cot_got = swap(jnp.where(first, cot_high, cot_low))
    cot = jnp.concatenate(
        [jnp.where(first, cot_mine, cot_got), jnp.where(first, cot_got, cot_mine)], 0
    )

    positions = x * (2 * TOK) + jnp.arange(2 * TOK, dtype=jnp.int32)
    frequency = ROPE_BASE ** (-2.0 * jnp.arange(HD // 2).astype(F32) / HD)
    phases = positions.astype(F32)[:, None] * frequency[None, :]
    cos, sin = jnp.cos(phases), jnp.sin(phases)
    cos2, sin2 = jnp.where(first, cos, 1.0), jnp.where(first, sin, 0.0)

    strip, columns, cot, cos, sin, cos2, sin2 = lax.optimization_barrier(
        (strip, columns, cot, cos, sin, cos2, sin2)
    )
    query, pair = call(
        project_body,
        [((2 * TOK, HD), BF16), ((2 * TOK, HD), BF16)],
        place,
        normed,
        normed_other,
        cos,
        sin,
        cos2,
        sin2,
        *slabs,
        strip,
    )
    pair_other = swap(pair)
    before = from_x(pair[TOK:], -1)
    before_other = swap(before)
    dquery, keep, keep_before, send, send_before = call(
        attend_body,
        [
            ((2 * TOK, HD), BF16),
            ((2 * TOK, HD), F32),
            ((TOK, HD), F32),
            ((2 * TOK, HD), BF16),
            ((TOK, HD), BF16),
        ],
        place,
        query,
        pair,
        pair_other,
        before,
        before_other,
        cot,
        cos,
        sin,
        scratch=[pltpu.VMEM((3 * TOK, HD), BF16), pltpu.VMEM((3 * TOK, HD), BF16)],
    )
    got_before = swap(send_before)
    got = swap(send)
    dquery_all = lax.all_gather(dquery, "x", axis=0)
    (back,) = call(halo_body, [((TOK, HD), BF16)], place, keep_before, got_before)
    back = from_x(back, 1)
    (dpair,) = call(pair_body, [((2 * TOK, HD), BF16)], place, keep, got, back, cos2, sin2)
    dpair_all = [dpair] + [from_x(dpair, step) for step in range(1, 4)]

    keep_in, send_in, keep_sum, send_sum = call(
        dnormed_body,
        [
            ((4, TOK, SLAB), BF16),
            ((4, TOK, SLAB), BF16),
            ((TOK, 128), F32),
            ((TOK, 128), F32),
        ],
        place,
        dquery,
        dpair,
        *slabs,
        strip,
        normed,
        normed_other,
    )
    got_in, got_sum = swap(send_in), swap(send_sum)
    own, own_sum, *messages = call(
        split_body,
        [((TOK, SLAB), F32), ((TOK, 128), F32)] + [((TOK, SLAB + 128), BF16)] * 3,
        place,
        keep_in,
        got_in,
        keep_sum,
        got_sum,
    )
    arrived = [from_y(message, step + 1) for step, message in enumerate(messages)]

    (chunks,) = call(
        weights_body,
        [((8, 128, 2 * HD), BF16)],
        place,
        columns,
        dquery_all,
        *dpair_all,
        scratch=[pltpu.VMEM((SLAB, 2 * HD), F32)],
    )
    chunks = after(chunks, *messages)
    chunks = lax.all_to_all(chunks, "dp", split_axis=0, concat_axis=0, tiled=True)
    (squares,) = call(squares_body, [((8, 128), F32)], place, chunks)
    for axis in ("core", "x", "tensor"):
        squares = lax.optimization_barrier(lax.psum(squares, axis))
    keep_out, send_out = call(
        clip_body,
        [((ROWS, 2 * HD), F32), ((ROWS, 2 * HD), F32)],
        place,
        chunks,
        squares,
    )
    got_out = swap(send_out)
    (input_grad,) = call(
        input_body,
        [((1, TOK, SLAB), BF16)],
        place,
        own,
        own_sum,
        *arrived,
        moved,
        inverse,
        gain,
        permute,
    )
    grad_query, grad_key, grad_value = call(
        out_body,
        [((ROWS, 2 * HD), F32), ((ROWS, HD), F32), ((ROWS, HD), F32)],
        place,
        keep_out,
        got_out,
    )
    return grad_query, grad_key, grad_value, input_grad


def solution(mesh):
    chips = Mesh(mesh.devices.reshape(4, 2, 4, 8), ("x", "core", "tensor", "dp"))
    seq = ("x", "core")
    weight = P((*seq, "dp"), "tensor")
    return jax.shard_map(
        local,
        mesh=chips,
        in_specs=(P("dp", seq, None), weight, weight, weight, P(), P("dp", seq, "tensor")),
        out_specs=(weight, weight, weight, P("dp", seq, "tensor")),
        check_vma=False,
    )
```

```python
import math

import jax
import jax.numpy as jnp
import numpy as np
from jax import lax
from jax.experimental import pallas as pl
from jax.experimental.pallas import tpu as pltpu
from jax.sharding import Mesh
from jax.sharding import PartitionSpec as P

D = 3584
H = 8
KVH = 4
HD = 256
WINDOW = 256
SLAB = D // 4
ROWS = 56
TOK = 256

EPSILON = 1e-06
SOFTCAP = 50.0
CLIP_BOUND = 1.0
ROPE_BASE = 10000.0

F32 = jnp.float32
BF16 = jnp.bfloat16
ANY = pl.BlockSpec(memory_space=pl.ANY)
SMEM = pl.BlockSpec(memory_space=pltpu.SMEM)


class Arriving:
    def __init__(self, copy, ref):
        self.copy, self.ref, self.here = copy, ref, False

    def wait(self):
        if not self.here:
            self.copy.wait()
            self.here = True

    def __getitem__(self, at):
        self.wait()
        return self.ref[at]


class Leaving:
    def __init__(self, copy, ref):
        self.copy, self.ref, self.gone = copy, ref, False

    def __getitem__(self, at):
        return self.ref[at]

    def __setitem__(self, at, value):
        self.ref[at] = value

    def leave(self):
        if not self.gone:
            self.copy.start()
            self.gone = True


def call(body, outs, place, *operands, scratch=()):
    count, made = len(operands), len(outs)

    def kernel(place_ref, *refs):
        held = refs[count + made : 2 * (count + made)]
        sems = refs[2 * (count + made)]
        rest = refs[2 * (count + made) + 1 :]
        arriving = []
        for k in range(count):
            copy = pltpu.make_async_copy(refs[k], held[k], sems.at[k])
            copy.start()
            arriving.append(Arriving(copy, held[k]))
        leaving = []
        for k in range(count, count + made):
            copy = pltpu.make_async_copy(held[k], refs[k], sems.at[k])
            leaving.append(Leaving(copy, held[k]))
        body(place_ref, *arriving, *leaving, *rest)
        for one in leaving:
            one.leave()
        for one in arriving:
            one.wait()
        for one in leaving:
            one.copy.wait()

    return pl.pallas_call(
        kernel,
        out_shape=[jax.ShapeDtypeStruct(shape, kind) for shape, kind in outs],
        in_specs=[SMEM] + [ANY] * count,
        out_specs=[ANY] * made,
        scratch_shapes=[pltpu.VMEM(one.shape, one.dtype) for one in operands]
        + [pltpu.VMEM(shape, kind) for shape, kind in outs]
        + [pltpu.SemaphoreType.DMA((count + made,))]
        + list(scratch),
        compiler_params=pltpu.CompilerParams(vmem_limit_bytes=32 * 1024 * 1024),
    )(place, *operands)


def swap(value):
    return lax.ppermute(value, "core", [(0, 1), (1, 0)])


def from_x(value, steps):
    return lax.ppermute(value, "x", [((i + steps) % 4, i) for i in range(4)])


def from_y(value, steps):
    return lax.ppermute(value, "tensor", [((i + steps) % 4, i) for i in range(4)])


def from_z(value, steps):
    return lax.ppermute(value, "dp", [((i + steps) % 8, i) for i in range(8)])


def after(value, *others):
    return lax.optimization_barrier((value, *others))[0]


def code(total):
    high = total.astype(BF16)
    rest = total - high.astype(F32)
    middle = rest.astype(BF16)
    low = (rest - middle.astype(F32)).astype(BF16)
    lane = lax.broadcasted_iota(jnp.int32, total.shape, 1)
    return jnp.where(
        lane == 0,
        high.astype(F32),
        jnp.where(
            lane == 1, middle.astype(F32), jnp.where(lane == 2, low.astype(F32), jnp.zeros_like(total))
        ),
    ).astype(BF16)


def mm(a, b, contract_a=1, contract_b=0):
    return lax.dot_general(
        a, b, (((contract_a,), (contract_b,)), ((), ())), preferred_element_type=F32
    )


def norm_body(place, inputs, permute, gain, normed, n0, n1, n2, n3, moved, inverse):
    x = place[0]
    rows = inputs[...].astype(F32)
    inv = lax.rsqrt(jnp.sum(rows * rows, -1, keepdims=True) * (1.0 / D) + EPSILON)
    inverse[...] = jnp.broadcast_to(inv, inverse.ref.shape)
    for slab in range(4):
        part = mm(inputs[:, slab * SLAB : (slab + 1) * SLAB], permute[...])
        moved[slab] = part.astype(BF16)
        normed[slab] = (part * inv * gain[slab : slab + 1, :]).astype(BF16)
    normed.leave()
    for step, one in enumerate((n0, n1, n2, n3)):
        one[...] = normed[lax.rem(x + 4 - step, 4)]
        one.leave()


def stack_body(place, own, far, up, down, up2, down2, whole):
    z = place[3]

    def put(step, rows):
        at = lax.rem(z + step, 8) * 112
        whole[pl.ds(pl.multiple_of(at, 16), 112), :] = rows

    put(0, own[...])
    put(2, up2[...])
    put(6, down2[...])
    put(4, far[...])
    put(1, up[:112, :])
    put(5, up[112:, :])
    put(7, down[:112, :])
    put(3, down[112:, :])


def columns_body(place, *refs):
    mine, theirs, whole = refs[:4], refs[4:8], refs[8]
    x, core = place[0], place[1]
    first = pl.multiple_of(core * TOK, TOK)
    second = pl.multiple_of((1 - core) * TOK, TOK)
    for step in range(4):
        at = lax.rem(x + step, 4)
        whole[at, :, pl.ds(first, TOK)] = mine[step][...].T
        whole[at, :, pl.ds(second, TOK)] = theirs[step][...].T


def spin(value, cosine, sine, direction):
    first, second = value[:, :128], value[:, 128:]
    return jnp.concatenate(
        [first * cosine - direction * second * sine, second * cosine + direction * first * sine], -1
    )


PIECES = ((0, 0, SLAB), (1, 0, SLAB), (3, 0, SLAB), (2, 0, 384), (2, 384, SLAB))


def project_body(
    place, own, s0, other, cos, sin, cos2, sin2, s1, s3, s2a, s2b, query, pair, total
):
    x, core = place[0], place[1]
    slabs = (s0, s1, s3, s2a, s2b)
    for turn, ((step, start, stop), slab) in enumerate(zip(PIECES, slabs)):
        here = lax.rem(x + step, 4)
        for half, rows in enumerate((own, other)):
            part = mm(rows[here, :, start:stop], slab[...])
            total[half] = part if turn == 0 else total[half] + part
    for half, block in ((0, core), (1, 1 - core)):
        at = pl.ds(pl.multiple_of(block * TOK, TOK), TOK)
        pair[at, :] = spin(total[half][:, HD:], cos2[at, :], sin2[at, :], 1.0).astype(BF16)
    pair.leave()
    for half, block in ((0, core), (1, 1 - core)):
        at = pl.ds(pl.multiple_of(block * TOK, TOK), TOK)
        query[at, :] = spin(total[half][:, :HD], cos[at, :], sin[at, :], 1.0).astype(BF16)


def attend_body(place, query, mine, theirs, mine_before, theirs_before, cot, cos, sin,
                dquery, keep, keep_before, send, send_before, keys, values):
    first_core = place[1] == 0
    for at, a, b in ((0, mine_before, theirs_before), (TOK, mine, theirs)):
        rows = a.ref.shape[0]
        keys[at : at + rows, :] = jnp.where(first_core, a[...], b[...])
        values[at : at + rows, :] = jnp.where(first_core, b[...], a[...])
    scale = 1.0 / math.sqrt(HD)
    q_at = lax.broadcasted_iota(jnp.int32, (TOK, 2 * TOK), 0)
    k_at = lax.broadcasted_iota(jnp.int32, (TOK, 2 * TOK), 1)
    band = (k_at <= q_at + TOK) & (k_at > q_at)
    key_parts = []
    value_parts = []
    for block in range(2):
        here = slice(block * TOK, (block + 1) * TOK)
        seen = slice(block * TOK, (block + 2) * TOK)
        q, g = query[here, :], cot[here, :]
        k, v = keys[seen, :], values[seen, :]
        squash = jnp.tanh(mm(q, k, 1, 1) * (scale / SOFTCAP))
        allowed = band
        if block == 0:
            allowed = band & ((k_at >= TOK) | (place[0] > 0))
        terms = jnp.where(allowed, jnp.exp(SOFTCAP * squash), 0.0)
        probs = terms / jnp.sum(terms, -1, keepdims=True)
        dprobs = mm(g, v, 1, 1)
        value_parts.append(mm(probs.astype(BF16), g, 0, 0))
        delta = jnp.sum(probs * dprobs, -1, keepdims=True)
        dlogits = (probs * (dprobs - delta) * (1.0 - squash * squash) * scale).astype(BF16)
        dq = mm(dlogits, k)
        dquery[here, :] = spin(dq, cos[here, :], sin[here, :], -1.0).astype(BF16)
        key_parts.append(mm(dlogits, q, 0, 0))

    def place_out(dk, dv, keep_at, send_at, here):
        keep_at[here, :] = jnp.where(first_core, dk, dv)
        send_at[here, :] = jnp.where(first_core, dv, dk).astype(BF16)

    place_out(key_parts[0][:TOK], value_parts[0][:TOK], keep_before, send_before, slice(0, TOK))
    place_out(
        key_parts[0][TOK:] + key_parts[1][:TOK],
        value_parts[0][TOK:] + value_parts[1][:TOK],
        keep,
        send,
        slice(0, TOK),
    )
    place_out(key_parts[1][TOK:], value_parts[1][TOK:], keep, send, slice(TOK, 2 * TOK))


def halo_body(place, keep_before, got_before, out):
    out[...] = (keep_before[...] + got_before[...].astype(F32)).astype(BF16)


def pair_body(place, dquery, keep, got, cos2, sin2, back, dout):
    dout[:, :HD] = dquery[...]
    for block in range(2):
        here = slice(block * TOK, (block + 1) * TOK)
        total = keep[here, :] + got[here, :].astype(F32)
        if block == 1:
            total += back[...].astype(F32)
        dout[here, HD:] = spin(total, cos2[here, :], sin2[here, :], -1.0).astype(BF16)


def dnormed_body(
    place, dout, s0, other, s1, s3, s2a, s2b, own, send, send_sum, keep, keep_sum
):
    x, core = place[0], place[1]
    for rows, block, out, sums in (
        (other, 1 - core, send, send_sum),
        (own, core, keep, keep_sum),
    ):
        d = dout[pl.ds(pl.multiple_of(block * TOK, TOK), TOK), :]
        total = jnp.zeros((TOK, 1), F32)
        for (step, start, stop), slab in zip(PIECES, (s0, s1, s3, s2a, s2b)):
            here = lax.rem(x + step, 4)
            part = mm(d, slab[...], 1, 1)
            total += jnp.sum(part * rows[here, :, start:stop].astype(F32), -1, keepdims=True)
            out[here, :, start:stop] = part.astype(BF16)
        sums[...] = jnp.broadcast_to(total, sums.ref.shape)
        out.leave()
        sums.leave()


def split_body(place, keep, got, keep_sum, got_sum, m1, m2, m3, own, own_sum):
    y = place[2]
    total = keep_sum[...] + got_sum[...]
    own_sum[...] = total
    coded = code(total)
    for step, message in enumerate((m1, m2, m3)):
        at = lax.rem(y + 4 - (step + 1), 4)
        message[:, :SLAB] = (keep[at].astype(F32) + got[at].astype(F32)).astype(BF16)
        message[:, SLAB:] = coded
        message.leave()
    own[...] = keep[y].astype(F32) + got[y].astype(F32)


def input_body(place, own, own_sum, m1, m2, m3, moved, inverse, gain, permute, out):
    total = own[...]
    sums = own_sum[:, :1]
    for message in (m1, m2, m3):
        total += message[:, :SLAB].astype(F32)
        sums += jnp.sum(message[:, SLAB:].astype(F32), -1, keepdims=True)
    inv = inverse[:, :1]
    y = place[2]
    rows = moved[y].astype(F32)
    grad = inv * (gain[pl.ds(y, 1), :] * total) - rows * ((inv * inv) * (sums * (1.0 / D)))
    out[0] = mm(grad.astype(BF16), permute[...], 1, 1).astype(BF16)


def weights_body(place, d0, columns, d1, d2, d3, squares, chunks):
    x, z = place[0], place[3]
    acc = mm(columns[x], d0[...])
    for step, d in ((1, d1), (2, d2), (3, d3)):
        acc += mm(columns[lax.rem(x + step, 4)], d[...])
    for chunk in range(8):
        chunks[chunk] = acc[chunk * 112 : (chunk + 1) * 112, :].astype(BF16)
    chunks.leave()
    row = lax.broadcasted_iota(jnp.int32, (8, 128), 0)
    squares[...] = jnp.where(row == z, jnp.sum(acc * acc), 0.0)


def clip_body(place, squares, chunks, send, keep):
    core = place[1]
    rms = jnp.sqrt(squares[...] * (1.0 / (D * (H + 2 * KVH) * HD)) + EPSILON)
    factor = CLIP_BOUND / jnp.maximum(rms, CLIP_BOUND)
    total = chunks[0].astype(F32) * factor[0:1, :1]
    for example in range(1, 8):
        total += chunks[example].astype(F32) * factor[example : example + 1, :1]
    top, bottom = total[:ROWS], total[ROWS:]
    send[...] = jnp.where(core == 0, bottom, top)
    send.leave()
    keep[...] = jnp.where(core == 0, top, bottom)


def out_body(place, keep, got, grad_query, grad_key, grad_value):
    first = place[1] == 0
    mine, theirs = keep[...], got[...]
    zero = jnp.where(first, mine, theirs)
    one = jnp.where(first, theirs, mine)
    grad_query[:, :HD] = zero[:, :HD]
    grad_query[:, HD:] = one[:, :HD]
    grad_key[...] = zero[:, HD:]
    grad_value[...] = one[:, HD:]


def local(inputs, w_query, w_key, w_value, norm_gain, attn_grad):
    x = lax.axis_index("x").astype(jnp.int32)
    core = lax.axis_index("core").astype(jnp.int32)
    y = lax.axis_index("tensor").astype(jnp.int32)
    z = lax.axis_index("dp").astype(jnp.int32)
    place = jnp.stack([x, core, y, z])
    first = core == 0

    low, high = w_query[:, :HD], w_query[:, HD:]
    mine = jnp.concatenate([jnp.where(first, low, high), jnp.where(first, w_key, w_value)], 1)
    theirs = jnp.concatenate([jnp.where(first, high, low), jnp.where(first, w_value, w_key)], 1)
    got = swap(theirs)
    block = jnp.concatenate([jnp.where(first, mine, got), jnp.where(first, got, mine)], 0)
    far = from_z(block, 4)
    up2, down2 = from_z(block, 2), from_z(block, -2)
    both = jnp.concatenate([block, far], 0)
    up, down = from_z(both, 1), from_z(both, -1)
    (slab,) = call(
        stack_body, [((SLAB, 2 * HD), BF16)], place, block, far, up, down, up2, down2
    )
    right, left = from_x(slab, 1), from_x(slab, -1)
    slabs = (slab, right, left, from_x(right[:384], 1), from_x(left[384:], -1))

    index = np.arange(SLAB)
    natural = (index % 112) // ROWS * 448 + index // 112 * ROWS + index % ROWS
    permute = (
        lax.broadcasted_iota(jnp.int32, (SLAB, SLAB), 0) == jnp.asarray(natural, jnp.int32)[None, :]
    ).astype(BF16)
    gain = norm_gain.reshape(4, 2, 8, ROWS).transpose(0, 2, 1, 3).reshape(4, SLAB)
    normed, *apart, moved, inverse = call(
        norm_body,
        [((4, TOK, SLAB), BF16)]
        + [((TOK, SLAB), BF16)] * 4
        + [((4, TOK, SLAB), BF16), ((TOK, 128), F32)],
        place,
        inputs[0],
        permute,
        gain,
    )
    columns_mine = [apart[0]] + [from_x(apart[step], step) for step in range(1, 4)]
    normed_other = swap(normed)
    columns_other = [lax.dynamic_index_in_dim(normed_other, x, 0, False)] + [
        swap(columns_mine[step]) for step in range(1, 4)
    ]
    (columns,) = call(
        columns_body, [((4, SLAB, 2 * TOK), BF16)], place, *columns_mine, *columns_other
    )

    cot_low, cot_high = attn_grad[0][:, :HD], attn_grad[0][:, HD:]
    cot_mine = jnp.where(first, cot_low, cot_high)
    cot_got = swap(jnp.where(first, cot_high, cot_low))
    cot = jnp.concatenate(
        [jnp.where(first, cot_mine, cot_got), jnp.where(first, cot_got, cot_mine)], 0
    )

    positions = x * (2 * TOK) + jnp.arange(2 * TOK, dtype=jnp.int32)
    frequency = ROPE_BASE ** (-2.0 * jnp.arange(HD // 2).astype(F32) / HD)
    phases = positions.astype(F32)[:, None] * frequency[None, :]
    cos, sin = jnp.cos(phases), jnp.sin(phases)
    cos2, sin2 = jnp.where(first, cos, 1.0), jnp.where(first, sin, 0.0)

    normed_other, columns, cot, cos, sin, cos2, sin2 = lax.optimization_barrier(
        (normed_other, columns, cot, cos, sin, cos2, sin2)
    )
    query, pair = call(
        project_body,
        [((2 * TOK, HD), BF16), ((2 * TOK, HD), BF16)],
        place,
        normed,
        slabs[0],
        normed_other,
        cos,
        sin,
        cos2,
        sin2,
        *slabs[1:],
        scratch=[pltpu.VMEM((2, TOK, 2 * HD), F32)],
    )
    pair_other = swap(pair)
    before = from_x(pair[TOK:], -1)
    before_other = swap(before)
    dquery, keep, keep_before, send, send_before = call(
        attend_body,
        [
            ((2 * TOK, HD), BF16),
            ((2 * TOK, HD), F32),
            ((TOK, HD), F32),
            ((2 * TOK, HD), BF16),
            ((TOK, HD), BF16),
        ],
        place,
        query,
        pair,
        pair_other,
        before,
        before_other,
        cot,
        cos,
        sin,
        scratch=[pltpu.VMEM((3 * TOK, HD), BF16), pltpu.VMEM((3 * TOK, HD), BF16)],
    )
    got_before = swap(send_before)
    got = swap(send)
    (back,) = call(halo_body, [((TOK, HD), BF16)], place, keep_before, got_before)
    back = from_x(back, 1)
    (dout,) = call(
        pair_body, [((2 * TOK, 2 * HD), BF16)], place, dquery, keep, got, cos2, sin2, back
    )
    dout_all = [dout] + [from_x(dout, step) for step in (1, 3, 2)]

    send_in, send_sum, keep_in, keep_sum = call(
        dnormed_body,
        [((4, TOK, SLAB), BF16), ((TOK, 128), F32)] * 2,
        place,
        after(dout, dout_all[1]),
        slabs[0],
        normed_other,
        *slabs[1:],
        normed,
    )
    got_in, got_sum = swap(send_in), swap(send_sum)
    *messages, own, own_sum = call(
        split_body,
        [((TOK, SLAB + 128), BF16)] * 3 + [((TOK, SLAB), F32), ((TOK, 128), F32)],
        place,
        keep_in,
        got_in,
        keep_sum,
        got_sum,
    )
    arrived = [from_y(message, step + 1) for step, message in enumerate(messages)]

    squares, chunks = call(
        weights_body,
        [((8, 128), F32), ((8, 112, 2 * HD), BF16)],
        place,
        after(dout, *messages),
        columns,
        dout_all[1],
        dout_all[3],
        dout_all[2],
    )
    chunks = lax.all_to_all(chunks, "dp", split_axis=0, concat_axis=0, tiled=True)
    for axis in ("core", "x", "tensor", "dp"):
        squares = lax.optimization_barrier(lax.psum(squares, axis))
    send_out, keep_out = call(
        clip_body,
        [((ROWS, 2 * HD), F32), ((ROWS, 2 * HD), F32)],
        place,
        squares,
        chunks,
    )
    got_out = swap(send_out)
    (input_grad,) = call(
        input_body,
        [((1, TOK, SLAB), BF16)],
        place,
        own,
        own_sum,
        *arrived,
        moved,
        inverse,
        gain,
        permute,
    )
    grad_query, grad_key, grad_value = call(
        out_body,
        [((ROWS, 2 * HD), F32), ((ROWS, HD), F32), ((ROWS, HD), F32)],
        place,
        keep_out,
        got_out,
    )
    return grad_query, grad_key, grad_value, input_grad


def solution(mesh):
    chips = Mesh(mesh.devices.reshape(4, 2, 4, 8), ("x", "core", "tensor", "dp"))
    seq = ("x", "core")
    weight = P((*seq, "dp"), "tensor")
    return jax.shard_map(
        local,
        mesh=chips,
        in_specs=(P("dp", seq, None), weight, weight, weight, P(), P("dp", seq, "tensor")),
        out_specs=(weight, weight, weight, P("dp", seq, "tensor")),
        check_vma=False,
    )
```

```python
import math

import jax
import jax.numpy as jnp
import numpy as np
from jax import lax
from jax.experimental import pallas as pl
from jax.experimental.pallas import tpu as pltpu
from jax.sharding import Mesh
from jax.sharding import PartitionSpec as P

D = 3584
H = 8
KVH = 4
HD = 256
WINDOW = 256
SLAB = D // 4
ROWS = 56
TOK = 256
CUT = 384

EPSILON = 1e-06
SOFTCAP = 50.0
CLIP_BOUND = 1.0
ROPE_BASE = 10000.0

F32 = jnp.float32
BF16 = jnp.bfloat16
ANY = pl.BlockSpec(memory_space=pl.ANY)
SMEM = pl.BlockSpec(memory_space=pltpu.SMEM)


class Arriving:
    def __init__(self, copy, ref):
        self.copy, self.ref, self.here = copy, ref, False

    def wait(self):
        if not self.here:
            self.copy.wait()
            self.here = True

    def __getitem__(self, at):
        self.wait()
        return self.ref[at]


class Leaving:
    def __init__(self, copy, ref):
        self.copy, self.ref, self.gone = copy, ref, False

    def __getitem__(self, at):
        return self.ref[at]

    def __setitem__(self, at, value):
        self.ref[at] = value

    def leave(self):
        if not self.gone:
            self.copy.start()
            self.gone = True


def call(body, outs, place, *operands, scratch=()):
    count, made = len(operands), len(outs)

    def kernel(place_ref, *refs):
        held = refs[count + made : 2 * (count + made)]
        sems = refs[2 * (count + made)]
        rest = refs[2 * (count + made) + 1 :]
        arriving = []
        for k in range(count):
            copy = pltpu.make_async_copy(refs[k], held[k], sems.at[k])
            copy.start()
            arriving.append(Arriving(copy, held[k]))
        leaving = []
        for k in range(count, count + made):
            copy = pltpu.make_async_copy(held[k], refs[k], sems.at[k])
            leaving.append(Leaving(copy, held[k]))
        body(place_ref, *arriving, *leaving, *rest)
        for one in leaving:
            one.leave()
        for one in arriving:
            one.wait()
        for one in leaving:
            one.copy.wait()

    return pl.pallas_call(
        kernel,
        out_shape=[jax.ShapeDtypeStruct(shape, kind) for shape, kind in outs],
        in_specs=[SMEM] + [ANY] * count,
        out_specs=[ANY] * made,
        scratch_shapes=[pltpu.VMEM(one.shape, one.dtype) for one in operands]
        + [pltpu.VMEM(shape, kind) for shape, kind in outs]
        + [pltpu.SemaphoreType.DMA((count + made,))]
        + list(scratch),
        compiler_params=pltpu.CompilerParams(vmem_limit_bytes=16 * 1024 * 1024),
    )(place, *operands)


def swap(value):
    return lax.ppermute(value, "core", [(0, 1), (1, 0)])


def from_x(value, steps):
    return lax.ppermute(value, "x", [((i + steps) % 4, i) for i in range(4)])


def from_y(value, steps):
    return lax.ppermute(value, "tensor", [((i + steps) % 4, i) for i in range(4)])


def from_z(value, steps):
    return lax.ppermute(value, "dp", [((i + steps) % 8, i) for i in range(8)])


def after(value, *others):
    return lax.optimization_barrier((value, *others))[0]


def code(total):
    high = total.astype(BF16)
    rest = total - high.astype(F32)
    middle = rest.astype(BF16)
    low = (rest - middle.astype(F32)).astype(BF16)
    lane = lax.broadcasted_iota(jnp.int32, total.shape, 1)
    return jnp.where(
        lane == 0,
        high.astype(F32),
        jnp.where(
            lane == 1, middle.astype(F32), jnp.where(lane == 2, low.astype(F32), jnp.zeros_like(total))
        ),
    ).astype(BF16)


def mm(a, b, contract_a=1, contract_b=0):
    return lax.dot_general(
        a, b, (((contract_a,), (contract_b,)), ((), ())), preferred_element_type=F32
    )


def norm_body(place, permute, gain, inputs, normed, n0, q1, q2, q3, moved, inverse, moved_gain):
    x, y = place[0], place[2]
    wide = gain[...]
    high = wide.astype(BF16)
    middle = (wide - high.astype(F32)).astype(BF16)
    low = (wide - high.astype(F32) - middle.astype(F32)).astype(BF16)
    moved_gain[...] = mm(high, permute[...]) + mm(middle, permute[...]) + mm(low, permute[...])
    rows = inputs[...].astype(F32)
    inv = lax.rsqrt(jnp.sum(rows * rows, -1, keepdims=True) * (1.0 / D) + EPSILON)
    inverse[...] = jnp.broadcast_to(inv, inverse.ref.shape)
    for slab in range(4):
        part = mm(inputs[:, slab * SLAB : (slab + 1) * SLAB], permute[...])
        moved[slab] = part.astype(BF16)
        normed[slab] = (part * inv * moved_gain[slab : slab + 1, :]).astype(BF16)
    normed.leave()
    quarter = pl.ds(pl.multiple_of(y * 64, 64), 64)
    for step, one in ((1, q1), (2, q2), (3, q3)):
        one[...] = normed[lax.rem(x + 4 - step, 4), quarter, :]
        one.leave()
    n0[...] = normed[x]


def stack_body(place, own, far, up2, down2, up, down, top, bottom, whole):
    z = place[3]

    def put(step, rows):
        at = lax.rem(z + step, 8) * 112
        whole[pl.ds(pl.multiple_of(at, 16), 112), :] = rows

    put(0, own[...])
    put(4, far[...])
    put(2, up2[...])
    put(6, down2[...])
    put(1, up[:112, :])
    put(5, up[112:, :])
    put(7, down[:112, :])
    put(3, down[112:, :])
    top[...] = whole[:CUT, :]
    bottom[...] = whole[CUT:, :]


def columns_body(place, *refs):
    own, other, mine, theirs, whole, rows = refs[0], refs[1], refs[2:6], refs[6:10], refs[10], refs[11]
    x, core, y = place[0], place[1], place[2]
    for first, block, parts in ((own, core, mine), (other, 1 - core, theirs)):
        rows[x, pl.ds(pl.multiple_of(block * TOK, TOK), TOK), :] = first[...]
        for turn in range(4):
            at = pl.ds(pl.multiple_of(block * TOK + lax.rem(y + turn, 4) * 64, 64), 64)
            for step in range(1, 4):
                rows[lax.rem(x + step, 4), at, :] = parts[turn][(step - 1) * 64 : step * 64, :]
    for slab in range(4):
        whole[slab] = rows[slab].T


def spin(value, cosine, sine, direction):
    first, second = value[:, :128], value[:, 128:]
    return jnp.concatenate(
        [first * cosine - direction * second * sine, second * cosine + direction * first * sine], -1
    )


PIECES = tuple((step, start, stop) for step in (0, 1, 3, 2) for start, stop in ((0, CUT), (CUT, SLAB)))


def project_body(place, own, s0, s1, other, s2, s3, s4, s5, total, last):
    x = place[0]
    for turn, ((step, start, stop), slab) in enumerate(zip(PIECES, (s0, s1, s2, s3, s4, s5))):
        here = lax.rem(x + step, 4)
        for half, rows in enumerate((own, other)):
            part = mm(rows[here, :, start:stop], slab[...])
            total[half] = part if turn == 0 else total[half] + part
    for half, rows in enumerate((own, other)):
        last[half] = rows[lax.rem(x + 2, 4)]


def finish_body(place, last, s6, s7, total, cos2, sin2, cos, sin, pair, query):
    core = place[1]
    sums = []
    for half in range(2):
        sums.append(total[half] + mm(last[half, :, :CUT], s6[...]) + mm(last[half, :, CUT:], s7[...]))
    for half, block in ((0, core), (1, 1 - core)):
        at = pl.ds(pl.multiple_of(block * TOK, TOK), TOK)
        pair[at, :] = spin(sums[half][:, HD:], cos2[at, :], sin2[at, :], 1.0).astype(BF16)
    pair.leave()
    for half, block in ((0, core), (1, 1 - core)):
        at = pl.ds(pl.multiple_of(block * TOK, TOK), TOK)
        query[at, :] = spin(sums[half][:, :HD], cos[at, :], sin[at, :], 1.0).astype(BF16)


def attend_body(place, query, mine, theirs, mine_before, theirs_before, cot, cos, sin,
                dquery, keep, keep_before, send, send_before, keys, values):
    first_core = place[1] == 0
    for at, a, b in ((0, mine_before, theirs_before), (TOK, mine, theirs)):
        rows = a.ref.shape[0]
        keys[at : at + rows, :] = jnp.where(first_core, a[...], b[...])
        values[at : at + rows, :] = jnp.where(first_core, b[...], a[...])
    scale = 1.0 / math.sqrt(HD)
    q_at = lax.broadcasted_iota(jnp.int32, (TOK, 2 * TOK), 0)
    k_at = lax.broadcasted_iota(jnp.int32, (TOK, 2 * TOK), 1)
    band = (k_at <= q_at + TOK) & (k_at > q_at)
    key_parts = []
    value_parts = []
    for block in range(2):
        here = slice(block * TOK, (block + 1) * TOK)
        seen = slice(block * TOK, (block + 2) * TOK)
        q, g = query[here, :], cot[here, :]
        k, v = keys[seen, :], values[seen, :]
        squash = jnp.tanh(mm(q, k, 1, 1) * (scale / SOFTCAP))
        allowed = band
        if block == 0:
            allowed = band & ((k_at >= TOK) | (place[0] > 0))
        terms = jnp.where(allowed, jnp.exp(SOFTCAP * squash), 0.0)
        probs = terms / jnp.sum(terms, -1, keepdims=True)
        dprobs = mm(g, v, 1, 1)
        value_parts.append(mm(probs.astype(BF16), g, 0, 0))
        delta = jnp.sum(probs * dprobs, -1, keepdims=True)
        dlogits = (probs * (dprobs - delta) * (1.0 - squash * squash) * scale).astype(BF16)
        dq = mm(dlogits, k)
        dquery[here, :] = spin(dq, cos[here, :], sin[here, :], -1.0).astype(BF16)
        key_parts.append(mm(dlogits, q, 0, 0))

    def place_out(dk, dv, keep_at, send_at, here):
        keep_at[here, :] = jnp.where(first_core, dk, dv)
        send_at[here, :] = jnp.where(first_core, dv, dk).astype(BF16)

    place_out(key_parts[0][:TOK], value_parts[0][:TOK], keep_before, send_before, slice(0, TOK))
    place_out(
        key_parts[0][TOK:] + key_parts[1][:TOK],
        value_parts[0][TOK:] + value_parts[1][:TOK],
        keep,
        send,
        slice(0, TOK),
    )
    place_out(key_parts[1][TOK:], value_parts[1][TOK:], keep, send, slice(TOK, 2 * TOK))


def halo_body(place, keep_before, got_before, out):
    out[...] = (keep_before[...] + got_before[...].astype(F32)).astype(BF16)


def pair_body(place, dquery, keep, got, cos2, sin2, back, dout):
    dout[:, :HD] = dquery[...]
    for block in range(2):
        here = slice(block * TOK, (block + 1) * TOK)
        total = keep[here, :] + got[here, :].astype(F32)
        if block == 1:
            total += back[...].astype(F32)
        dout[here, HD:] = spin(total, cos2[here, :], sin2[here, :], -1.0).astype(BF16)


def dnormed_body(
    place, dout, s0, s1, other, s2, s3, s4, s5, s6, s7, own, send, send_sum, keep, keep_sum
):
    x, core = place[0], place[1]
    for rows, block, out, sums in (
        (other, 1 - core, send, send_sum),
        (own, core, keep, keep_sum),
    ):
        d = dout[pl.ds(pl.multiple_of(block * TOK, TOK), TOK), :]
        total = jnp.zeros((TOK, 1), F32)
        for (step, start, stop), slab in zip(PIECES, (s0, s1, s2, s3, s4, s5, s6, s7)):
            here = lax.rem(x + step, 4)
            part = mm(d, slab[...], 1, 1)
            total += jnp.sum(part * rows[here, :, start:stop].astype(F32), -1, keepdims=True)
            out[here, :, start:stop] = part.astype(BF16)
        sums[...] = jnp.broadcast_to(total, sums.ref.shape)
        out.leave()
        sums.leave()


def split_body(place, keep, got, keep_sum, got_sum, m1, m2, m3, own, own_sum):
    y = place[2]
    total = keep_sum[...] + got_sum[...]
    own_sum[...] = total
    coded = code(total)
    for step, message in enumerate((m1, m2, m3)):
        at = lax.rem(y + 4 - (step + 1), 4)
        message[:, :SLAB] = (keep[at].astype(F32) + got[at].astype(F32)).astype(BF16)
        message[:, SLAB:] = coded
        message.leave()
    own[...] = keep[y].astype(F32) + got[y].astype(F32)


def input_body(place, own, own_sum, m1, m2, m3, moved, inverse, gain, permute, out):
    total = own[...]
    sums = own_sum[:, :1]
    for message in (m1, m2, m3):
        total += message[:, :SLAB].astype(F32)
        sums += jnp.sum(message[:, SLAB:].astype(F32), -1, keepdims=True)
    inv = inverse[:, :1]
    y = place[2]
    rows = moved[y].astype(F32)
    grad = inv * (gain[pl.ds(y, 1), :] * total) - rows * ((inv * inv) * (sums * (1.0 / D)))
    out[0] = mm(grad.astype(BF16), permute[...], 1, 1).astype(BF16)


def weights_body(place, d0, columns, d1, d2, d3, squares, chunks):
    x, z = place[0], place[3]
    acc = mm(columns[x], d0[...])
    for step, d in ((1, d1), (2, d2), (3, d3)):
        acc += mm(columns[lax.rem(x + step, 4)], d[...])
    for chunk in range(8):
        chunks[chunk] = acc[chunk * 112 : (chunk + 1) * 112, :].astype(BF16)
    chunks.leave()
    row = lax.broadcasted_iota(jnp.int32, (8, 128), 0)
    squares[...] = jnp.where(row == z, jnp.sum(acc * acc), 0.0)


def local(inputs, w_query, w_key, w_value, norm_gain, attn_grad):
    x = lax.axis_index("x").astype(jnp.int32)
    core = lax.axis_index("core").astype(jnp.int32)
    y = lax.axis_index("tensor").astype(jnp.int32)
    z = lax.axis_index("dp").astype(jnp.int32)
    place = jnp.stack([x, core, y, z])
    first = core == 0

    low, high = w_query[:, :HD], w_query[:, HD:]
    mine = jnp.concatenate([jnp.where(first, low, high), jnp.where(first, w_key, w_value)], 1)
    theirs = jnp.concatenate([jnp.where(first, high, low), jnp.where(first, w_value, w_key)], 1)
    got = swap(theirs)
    block = jnp.concatenate([jnp.where(first, mine, got), jnp.where(first, got, mine)], 0)
    far = from_z(block, 4)
    up2, down2 = from_z(block, 2), from_z(block, -2)
    far, up2, down2 = lax.optimization_barrier((far, up2, down2))
    both = jnp.concatenate([block, far], 0)
    up, down = from_z(both, 1), from_z(both, -1)
    top, bottom = call(
        stack_body,
        [((CUT, 2 * HD), BF16), ((SLAB - CUT, 2 * HD), BF16)],
        place,
        block,
        far,
        up2,
        down2,
        up,
        down,
        scratch=[pltpu.VMEM((SLAB, 2 * HD), BF16)],
    )
    near = (from_x(top, 1), from_x(bottom, 1), from_x(top, -1), from_x(bottom, -1))
    near = lax.optimization_barrier(near)
    slabs = (top, bottom, *near, from_x(near[0], 1), from_x(near[3], -1))

    index = np.arange(SLAB)
    natural = (index % 112) // ROWS * 448 + index // 112 * ROWS + index % ROWS
    permute = (
        lax.broadcasted_iota(jnp.int32, (SLAB, SLAB), 0) == jnp.asarray(natural, jnp.int32)[None, :]
    ).astype(BF16)
    normed, own_columns, *quarters, moved, inverse, gain = call(
        norm_body,
        [((4, TOK, SLAB), BF16), ((TOK, SLAB), BF16)]
        + [((TOK // 4, SLAB), BF16)] * 3
        + [((4, TOK, SLAB), BF16), ((TOK, 128), F32), ((4, SLAB), F32)],
        place,
        permute,
        norm_gain.reshape(4, SLAB),
        after(inputs[0], far),
    )
    normed_other = swap(normed)
    bundle = jnp.concatenate([from_x(one, step + 1) for step, one in enumerate(quarters)], 0)
    bundles = lax.optimization_barrier(
        (bundle, from_y(bundle, 1), from_y(bundle, 2), from_y(bundle, 3))
    )
    (columns,) = call(
        columns_body,
        [((4, SLAB, 2 * TOK), BF16)],
        place,
        own_columns,
        swap(own_columns),
        *bundles,
        *[swap(one) for one in bundles],
        scratch=[pltpu.VMEM((4, 2 * TOK, SLAB), BF16)],
    )

    cot_low, cot_high = attn_grad[0][:, :HD], attn_grad[0][:, HD:]
    cot_mine = jnp.where(first, cot_low, cot_high)
    cot_got = swap(jnp.where(first, cot_high, cot_low))
    cot = jnp.concatenate(
        [jnp.where(first, cot_mine, cot_got), jnp.where(first, cot_got, cot_mine)], 0
    )

    positions = x * (2 * TOK) + jnp.arange(2 * TOK, dtype=jnp.int32)
    frequency = ROPE_BASE ** (-2.0 * jnp.arange(HD // 2).astype(F32) / HD)
    phases = positions.astype(F32)[:, None] * frequency[None, :]
    cos, sin = jnp.cos(phases), jnp.sin(phases)
    cos2, sin2 = jnp.where(first, cos, 1.0), jnp.where(first, sin, 0.0)

    normed_other, cos, sin, cos2, sin2 = lax.optimization_barrier(
        (normed_other, cos, sin, cos2, sin2)
    )
    cot = after(cot, columns)
    total, last = call(
        project_body,
        [((2, TOK, 2 * HD), F32), ((2, TOK, SLAB), BF16)],
        place,
        normed,
        *slabs[:2],
        normed_other,
        *slabs[2:6],
    )
    pair, query = call(
        finish_body,
        [((2 * TOK, HD), BF16), ((2 * TOK, HD), BF16)],
        place,
        last,
        *slabs[6:],
        total,
        cos2,
        sin2,
        cos,
        sin,
    )
    pair_other = swap(pair)
    before = from_x(pair[TOK:], -1)
    before_other = swap(before)
    dquery, keep, keep_before, send, send_before = call(
        attend_body,
        [
            ((2 * TOK, HD), BF16),
            ((2 * TOK, HD), F32),
            ((TOK, HD), F32),
            ((2 * TOK, HD), BF16),
            ((TOK, HD), BF16),
        ],
        place,
        query,
        pair,
        pair_other,
        before,
        before_other,
        cot,
        cos,
        sin,
        scratch=[pltpu.VMEM((3 * TOK, HD), BF16), pltpu.VMEM((3 * TOK, HD), BF16)],
    )
    got_before = swap(send_before)
    got = swap(send)
    (back,) = call(halo_body, [((TOK, HD), BF16)], place, keep_before, got_before)
    back = from_x(back, 1)
    (dout,) = call(
        pair_body, [((2 * TOK, 2 * HD), BF16)], place, dquery, keep, got, cos2, sin2, back
    )
    dout_1, dout_3 = lax.optimization_barrier((from_x(dout, 1), from_x(dout, 3)))
    dout_2 = from_x(dout, 2)

    send_in, send_sum, keep_in, keep_sum = call(
        dnormed_body,
        [((4, TOK, SLAB), BF16), ((TOK, 128), F32)] * 2,
        place,
        dout,
        *slabs[:2],
        normed_other,
        *slabs[2:],
        normed,
    )
    got_in, got_sum = swap(send_in), swap(send_sum)
    *messages, own, own_sum = call(
        split_body,
        [((TOK, SLAB + 128), BF16)] * 3 + [((TOK, SLAB), F32), ((TOK, 128), F32)],
        place,
        keep_in,
        got_in,
        keep_sum,
        after(got_sum, dout_1, dout_3),
    )
    arrived = [from_y(message, step + 1) for step, message in enumerate(messages)]

    squares, chunks = call(
        weights_body,
        [((8, 128), F32), ((8, 112, 2 * HD), BF16)],
        place,
        after(dout, arrived[0]),
        columns,
        dout_1,
        dout_2,
        dout_3,
    )
    chunks = lax.all_to_all(chunks, "dp", split_axis=0, concat_axis=0, tiled=True)
    for axis in ("core", "x", "tensor"):
        squares = lax.optimization_barrier(lax.psum(squares, axis))
    chunks = after(chunks, squares)
    upper, lower = chunks[:, :ROWS], chunks[:, ROWS:]
    (input_grad,) = call(
        input_body,
        [((1, TOK, SLAB), BF16)],
        place,
        own,
        own_sum,
        *arrived,
        moved,
        inverse,
        gain,
        permute,
    )
    squares = lax.psum(after(squares, input_grad), "dp")
    rms = jnp.sqrt(squares[:, :1] * (1.0 / (D * (H + 2 * KVH) * HD)) + EPSILON)
    factor = (CLIP_BOUND / jnp.maximum(rms, CLIP_BOUND))[:, :, None]
    mine_out = jnp.where(first, upper, lower)
    got_out = swap(jnp.where(first, lower, upper))
    mine_out, got_out = (
        jnp.sum(one.astype(F32) * factor, 0) for one in (mine_out, got_out)
    )
    zero = jnp.where(first, mine_out, got_out)
    one = jnp.where(first, got_out, mine_out)
    grad_query = jnp.concatenate([zero[:, :HD], one[:, :HD]], 1)
    grad_key, grad_value = zero[:, HD:], one[:, HD:]
    return grad_query, grad_key, grad_value, input_grad


def solution(mesh):
    chips = Mesh(mesh.devices.reshape(4, 2, 4, 8), ("x", "core", "tensor", "dp"))
    seq = ("x", "core")
    weight = P((*seq, "dp"), "tensor")
    return jax.shard_map(
        local,
        mesh=chips,
        in_specs=(P("dp", seq, None), weight, weight, weight, P(), P("dp", seq, "tensor")),
        out_specs=(weight, weight, weight, P("dp", seq, "tensor")),
        check_vma=False,
    )
```

```python
import math

import jax
import jax.numpy as jnp
import numpy as np
from jax import lax
from jax.experimental import pallas as pl
from jax.experimental.pallas import tpu as pltpu
from jax.sharding import Mesh
from jax.sharding import PartitionSpec as P

D = 3584
H = 8
KVH = 4
HD = 256
WINDOW = 256
SLAB = D // 4
ROWS = 56
TOK = 256
CUT = 384

EPSILON = 1e-06
SOFTCAP = 50.0
CLIP_BOUND = 1.0
ROPE_BASE = 10000.0

F32 = jnp.float32
BF16 = jnp.bfloat16
ANY = pl.BlockSpec(memory_space=pl.ANY)
SMEM = pl.BlockSpec(memory_space=pltpu.SMEM)


class Arriving:
    def __init__(self, copy, ref):
        self.copy, self.ref, self.here = copy, ref, False

    def wait(self):
        if not self.here:
            self.copy.wait()
            self.here = True

    def __getitem__(self, at):
        self.wait()
        return self.ref[at]


class Leaving:
    def __init__(self, copy, ref):
        self.copy, self.ref, self.gone = copy, ref, False

    def __getitem__(self, at):
        return self.ref[at]

    def __setitem__(self, at, value):
        self.ref[at] = value

    def leave(self):
        if not self.gone:
            self.copy.start()
            self.gone = True


def call(body, outs, place, *operands, scratch=(), room=16):
    count, made = len(operands), len(outs)

    def kernel(place_ref, *refs):
        held = refs[count + made : 2 * (count + made)]
        sems = refs[2 * (count + made)]
        rest = refs[2 * (count + made) + 1 :]
        arriving = []
        for k in range(count):
            copy = pltpu.make_async_copy(refs[k], held[k], sems.at[k])
            copy.start()
            arriving.append(Arriving(copy, held[k]))
        leaving = []
        for k in range(count, count + made):
            copy = pltpu.make_async_copy(held[k], refs[k], sems.at[k])
            leaving.append(Leaving(copy, held[k]))
        body(place_ref, *arriving, *leaving, *rest)
        for one in leaving:
            one.leave()
        for one in arriving:
            one.wait()
        for one in leaving:
            one.copy.wait()

    return pl.pallas_call(
        kernel,
        out_shape=[jax.ShapeDtypeStruct(shape, kind) for shape, kind in outs],
        in_specs=[SMEM] + [ANY] * count,
        out_specs=[ANY] * made,
        scratch_shapes=[pltpu.VMEM(one.shape, one.dtype) for one in operands]
        + [pltpu.VMEM(shape, kind) for shape, kind in outs]
        + [pltpu.SemaphoreType.DMA((count + made,))]
        + list(scratch),
        compiler_params=pltpu.CompilerParams(vmem_limit_bytes=room * 1024 * 1024),
    )(place, *operands)


def swap(value):
    return lax.ppermute(value, "core", [(0, 1), (1, 0)])


def from_x(value, steps):
    return lax.ppermute(value, "x", [((i + steps) % 4, i) for i in range(4)])


def from_y(value, steps):
    return lax.ppermute(value, "tensor", [((i + steps) % 4, i) for i in range(4)])


def from_z(value, steps):
    return lax.ppermute(value, "dp", [((i + steps) % 8, i) for i in range(8)])


def after(value, *others):
    return lax.optimization_barrier((value, *others))[0]


def code(total):
    high = total.astype(BF16)
    rest = total - high.astype(F32)
    middle = rest.astype(BF16)
    low = (rest - middle.astype(F32)).astype(BF16)
    lane = lax.broadcasted_iota(jnp.int32, total.shape, 1)
    return jnp.where(
        lane == 0,
        high.astype(F32),
        jnp.where(
            lane == 1, middle.astype(F32), jnp.where(lane == 2, low.astype(F32), jnp.zeros_like(total))
        ),
    ).astype(BF16)


def mm(a, b, contract_a=1, contract_b=0):
    return lax.dot_general(
        a, b, (((contract_a,), (contract_b,)), ((), ())), preferred_element_type=F32
    )


def norm_body(place, permute, gain, inputs, normed, n0, q1, q2, q3, moved, inverse, moved_gain):
    x, y = place[0], place[2]
    wide = gain[...]
    high = wide.astype(BF16)
    middle = (wide - high.astype(F32)).astype(BF16)
    low = (wide - high.astype(F32) - middle.astype(F32)).astype(BF16)
    moved_gain[...] = mm(high, permute[...]) + mm(middle, permute[...]) + mm(low, permute[...])
    rows = inputs[...].astype(F32)
    inv = lax.rsqrt(jnp.sum(rows * rows, -1, keepdims=True) * (1.0 / D) + EPSILON)
    inverse[...] = jnp.broadcast_to(inv, inverse.ref.shape)
    for slab in range(4):
        part = mm(inputs[:, slab * SLAB : (slab + 1) * SLAB], permute[...])
        moved[slab] = part.astype(BF16)
        normed[slab] = (part * inv * moved_gain[slab : slab + 1, :]).astype(BF16)
    normed.leave()
    quarter = pl.ds(pl.multiple_of(y * 64, 64), 64)
    for step, one in ((1, q1), (2, q2), (3, q3)):
        one[...] = normed[lax.rem(x + 4 - step, 4), quarter, :]
        one.leave()
    n0[...] = normed[x]


def stack_body(place, own, far, up2, down2, up, down, top, bottom, whole):
    z = place[3]

    def put(step, rows):
        at = lax.rem(z + step, 8) * 112
        whole[pl.ds(pl.multiple_of(at, 16), 112), :] = rows

    put(0, own[...])
    put(4, far[...])
    put(2, up2[...])
    put(6, down2[...])
    put(1, up[:112, :])
    put(5, up[112:, :])
    put(7, down[:112, :])
    put(3, down[112:, :])
    top[...] = whole[:CUT, :]
    bottom[...] = whole[CUT:, :]


def columns_body(place, *refs):
    own, other, mine, theirs, whole, rows = refs[0], refs[1], refs[2:6], refs[6:10], refs[10], refs[11]
    x, core, y = place[0], place[1], place[2]
    for first, block, parts in ((own, core, mine), (other, 1 - core, theirs)):
        rows[x, pl.ds(pl.multiple_of(block * TOK, TOK), TOK), :] = first[...]
        for turn in range(4):
            at = pl.ds(pl.multiple_of(block * TOK + lax.rem(y + turn, 4) * 64, 64), 64)
            for step in range(1, 4):
                rows[lax.rem(x + step, 4), at, :] = parts[turn][(step - 1) * 64 : step * 64, :]
    for slab in range(4):
        whole[slab] = rows[slab].T


def spin(value, cosine, sine, direction):
    first, second = value[:, :128], value[:, 128:]
    return jnp.concatenate(
        [first * cosine - direction * second * sine, second * cosine + direction * first * sine], -1
    )


PIECES = tuple((step, start, stop) for step in (0, 1, 3, 2) for start, stop in ((0, CUT), (CUT, SLAB)))


def project_body(place, own, s0, s1, other, s2, s3, s4, s5, total, last):
    x = place[0]
    for turn, ((step, start, stop), slab) in enumerate(zip(PIECES, (s0, s1, s2, s3, s4, s5))):
        here = lax.rem(x + step, 4)
        for half, rows in enumerate((own, other)):
            part = mm(rows[here, :, start:stop], slab[...])
            total[half] = part if turn == 0 else total[half] + part
    for half, rows in enumerate((own, other)):
        last[half] = rows[lax.rem(x + 2, 4)]


def finish_body(place, last, s6, s7, total, cos2, sin2, cos, sin, pair, query):
    core = place[1]
    sums = []
    for half in range(2):
        sums.append(total[half] + mm(last[half, :, :CUT], s6[...]) + mm(last[half, :, CUT:], s7[...]))
    for half, block in ((0, core), (1, 1 - core)):
        at = pl.ds(pl.multiple_of(block * TOK, TOK), TOK)
        pair[at, :] = spin(sums[half][:, HD:], cos2[at, :], sin2[at, :], 1.0).astype(BF16)
    pair.leave()
    for half, block in ((0, core), (1, 1 - core)):
        at = pl.ds(pl.multiple_of(block * TOK, TOK), TOK)
        query[at, :] = spin(sums[half][:, :HD], cos[at, :], sin[at, :], 1.0).astype(BF16)


def attend_body(place, query, mine, theirs, mine_before, theirs_before, cot, cos, sin,
                dquery, keep, keep_before, send, send_before, keys, values):
    first_core = place[1] == 0
    for at, a, b in ((0, mine_before, theirs_before), (TOK, mine, theirs)):
        rows = a.ref.shape[0]
        keys[at : at + rows, :] = jnp.where(first_core, a[...], b[...])
        values[at : at + rows, :] = jnp.where(first_core, b[...], a[...])
    scale = 1.0 / math.sqrt(HD)
    q_at = lax.broadcasted_iota(jnp.int32, (TOK, 2 * TOK), 0)
    k_at = lax.broadcasted_iota(jnp.int32, (TOK, 2 * TOK), 1)
    band = (k_at <= q_at + TOK) & (k_at > q_at)
    key_parts = []
    value_parts = []
    for block in range(2):
        here = slice(block * TOK, (block + 1) * TOK)
        seen = slice(block * TOK, (block + 2) * TOK)
        q, g = query[here, :], cot[here, :]
        k, v = keys[seen, :], values[seen, :]
        squash = jnp.tanh(mm(q, k, 1, 1) * (scale / SOFTCAP))
        allowed = band
        if block == 0:
            allowed = band & ((k_at >= TOK) | (place[0] > 0))
        terms = jnp.where(allowed, jnp.exp(SOFTCAP * squash), 0.0)
        probs = terms / jnp.sum(terms, -1, keepdims=True)
        dprobs = mm(g, v, 1, 1)
        value_parts.append(mm(probs.astype(BF16), g, 0, 0))
        delta = jnp.sum(probs * dprobs, -1, keepdims=True)
        dlogits = (probs * (dprobs - delta) * (1.0 - squash * squash) * scale).astype(BF16)
        dq = mm(dlogits, k)
        dquery[here, :] = spin(dq, cos[here, :], sin[here, :], -1.0).astype(BF16)
        key_parts.append(mm(dlogits, q, 0, 0))

    def place_out(dk, dv, keep_at, send_at, here):
        keep_at[here, :] = jnp.where(first_core, dk, dv)
        send_at[here, :] = jnp.where(first_core, dv, dk).astype(BF16)

    place_out(key_parts[0][:TOK], value_parts[0][:TOK], keep_before, send_before, slice(0, TOK))
    place_out(
        key_parts[0][TOK:] + key_parts[1][:TOK],
        value_parts[0][TOK:] + value_parts[1][:TOK],
        keep,
        send,
        slice(0, TOK),
    )
    place_out(key_parts[1][TOK:], value_parts[1][TOK:], keep, send, slice(TOK, 2 * TOK))


def halo_body(place, keep_before, got_before, out):
    out[...] = (keep_before[...] + got_before[...].astype(F32)).astype(BF16)


def pair_body(place, dquery, keep, got, cos2, sin2, back, dout):
    dout[:, :HD] = dquery[...]
    for block in range(2):
        here = slice(block * TOK, (block + 1) * TOK)
        total = keep[here, :] + got[here, :].astype(F32)
        if block == 1:
            total += back[...].astype(F32)
        dout[here, HD:] = spin(total, cos2[here, :], sin2[here, :], -1.0).astype(BF16)


def dnormed_body(
    place, dout, s0, s1, other, s2, s3, s4, s5, s6, s7, own, send, send_sum, keep, keep_sum
):
    x, core = place[0], place[1]
    for rows, block, out, sums in (
        (other, 1 - core, send, send_sum),
        (own, core, keep, keep_sum),
    ):
        d = dout[pl.ds(pl.multiple_of(block * TOK, TOK), TOK), :]
        total = jnp.zeros((TOK, 1), F32)
        for (step, start, stop), slab in zip(PIECES, (s0, s1, s2, s3, s4, s5, s6, s7)):
            here = lax.rem(x + step, 4)
            part = mm(d, slab[...], 1, 1)
            total += jnp.sum(part * rows[here, :, start:stop].astype(F32), -1, keepdims=True)
            out[here, :, start:stop] = part.astype(BF16)
        sums[...] = jnp.broadcast_to(total, sums.ref.shape)
        out.leave()
        sums.leave()


def split_body(place, keep, got, keep_sum, got_sum, m1, m2, m3, own, own_sum):
    y = place[2]
    total = keep_sum[...] + got_sum[...]
    own_sum[...] = total
    coded = code(total)
    for step, message in enumerate((m1, m2, m3)):
        at = lax.rem(y + 4 - (step + 1), 4)
        message[:, :SLAB] = (keep[at].astype(F32) + got[at].astype(F32)).astype(BF16)
        message[:, SLAB:] = coded
        message.leave()
    own[...] = keep[y].astype(F32) + got[y].astype(F32)


def input_body(place, own, own_sum, m1, m2, m3, moved, inverse, gain, permute, out):
    total = own[...]
    sums = own_sum[:, :1]
    for message in (m1, m2, m3):
        total += message[:, :SLAB].astype(F32)
        sums += jnp.sum(message[:, SLAB:].astype(F32), -1, keepdims=True)
    inv = inverse[:, :1]
    y = place[2]
    rows = moved[y].astype(F32)
    grad = inv * (gain[pl.ds(y, 1), :] * total) - rows * ((inv * inv) * (sums * (1.0 / D)))
    out[0] = mm(grad.astype(BF16), permute[...], 1, 1).astype(BF16)


def weights_body(place, d0, columns, d1, d2, d3, squares, chunks):
    x, z = place[0], place[3]
    acc = mm(columns[x], d0[...])
    for step, d in ((1, d1), (2, d2), (3, d3)):
        acc += mm(columns[lax.rem(x + step, 4)], d[...])
    for chunk in range(8):
        chunks[chunk] = acc[chunk * 112 : (chunk + 1) * 112, :].astype(BF16)
    chunks.leave()
    row = lax.broadcasted_iota(jnp.int32, (8, 128), 0)
    squares[...] = jnp.where(row == z, jnp.sum(acc * acc), 0.0)


def local(inputs, w_query, w_key, w_value, norm_gain, attn_grad):
    x = lax.axis_index("x").astype(jnp.int32)
    core = lax.axis_index("core").astype(jnp.int32)
    y = lax.axis_index("tensor").astype(jnp.int32)
    z = lax.axis_index("dp").astype(jnp.int32)
    place = jnp.stack([x, core, y, z])
    first = core == 0

    low, high = w_query[:, :HD], w_query[:, HD:]
    mine = jnp.concatenate([jnp.where(first, low, high), jnp.where(first, w_key, w_value)], 1)
    theirs = jnp.concatenate([jnp.where(first, high, low), jnp.where(first, w_value, w_key)], 1)
    got = swap(theirs)
    block = jnp.concatenate([jnp.where(first, mine, got), jnp.where(first, got, mine)], 0)
    far = from_z(block, 4)
    up2, down2 = from_z(block, 2), from_z(block, -2)
    far, up2, down2 = lax.optimization_barrier((far, up2, down2))
    both = jnp.concatenate([block, far], 0)
    up, down = from_z(both, 1), from_z(both, -1)

    index = np.arange(SLAB)
    natural = (index % 112) // ROWS * 448 + index // 112 * ROWS + index % ROWS
    permute = (
        lax.broadcasted_iota(jnp.int32, (SLAB, SLAB), 0) == jnp.asarray(natural, jnp.int32)[None, :]
    ).astype(BF16)
    normed, own_columns, *quarters, moved, inverse, gain = call(
        norm_body,
        [((4, TOK, SLAB), BF16), ((TOK, SLAB), BF16)]
        + [((TOK // 4, SLAB), BF16)] * 3
        + [((4, TOK, SLAB), BF16), ((TOK, 128), F32), ((4, SLAB), F32)],
        place,
        permute,
        norm_gain.reshape(4, SLAB),
        after(inputs[0], far),
        room=60,
    )
    top, bottom = call(
        stack_body,
        [((CUT, 2 * HD), BF16), ((SLAB - CUT, 2 * HD), BF16)],
        place,
        after(block, normed),
        far,
        up2,
        down2,
        up,
        down,
        scratch=[pltpu.VMEM((SLAB, 2 * HD), BF16)],
    )
    *quarters, normed_late, _, _ = lax.optimization_barrier((*quarters, normed, up, down))
    bundle = jnp.concatenate([from_x(one, step + 1) for step, one in enumerate(quarters)], 0)
    normed_other = swap(normed_late)
    near = (from_x(top, 1), from_x(bottom, 1), from_x(top, -1), from_x(bottom, -1))
    *near, bundle_1, bundle_3 = lax.optimization_barrier(
        (*near, from_y(bundle, 1), from_y(bundle, 3))
    )
    slabs = (top, bottom, *near, from_x(near[0], 1), from_x(near[3], -1))
    bundles = (bundle, bundle_1, from_y(bundle, 2), bundle_3)
    theirs = [swap(one) for one in bundles]
    theirs_own = swap(own_columns)
    (columns,) = call(
        columns_body,
        [((4, SLAB, 2 * TOK), BF16)],
        place,
        own_columns,
        theirs_own,
        *bundles,
        *theirs,
        scratch=[pltpu.VMEM((4, 2 * TOK, SLAB), BF16)],
    )

    cot_low, cot_high = attn_grad[0][:, :HD], attn_grad[0][:, HD:]
    cot_mine = jnp.where(first, cot_low, cot_high)
    cot_got = swap(jnp.where(first, cot_high, cot_low))
    cot = jnp.concatenate(
        [jnp.where(first, cot_mine, cot_got), jnp.where(first, cot_got, cot_mine)], 0
    )

    positions = x * (2 * TOK) + jnp.arange(2 * TOK, dtype=jnp.int32)
    frequency = ROPE_BASE ** (-2.0 * jnp.arange(HD // 2).astype(F32) / HD)
    phases = positions.astype(F32)[:, None] * frequency[None, :]
    cos, sin = jnp.cos(phases), jnp.sin(phases)
    cos2, sin2 = jnp.where(first, cos, 1.0), jnp.where(first, sin, 0.0)

    normed_other, cos, sin, cos2, sin2 = lax.optimization_barrier(
        (normed_other, cos, sin, cos2, sin2)
    )
    cot = after(cot, theirs_own, *theirs)
    total, last = call(
        project_body,
        [((2, TOK, 2 * HD), F32), ((2, TOK, SLAB), BF16)],
        place,
        normed,
        *slabs[:2],
        normed_other,
        *slabs[2:6],
    )
    pair, query = call(
        finish_body,
        [((2 * TOK, HD), BF16), ((2 * TOK, HD), BF16)],
        place,
        last,
        *slabs[6:],
        total,
        cos2,
        sin2,
        cos,
        sin,
    )
    pair_other = swap(pair)
    before = from_x(pair[TOK:], -1)
    before_other = swap(before)
    dquery, keep, keep_before, send, send_before = call(
        attend_body,
        [
            ((2 * TOK, HD), BF16),
            ((2 * TOK, HD), F32),
            ((TOK, HD), F32),
            ((2 * TOK, HD), BF16),
            ((TOK, HD), BF16),
        ],
        place,
        query,
        pair,
        pair_other,
        before,
        before_other,
        cot,
        cos,
        sin,
        scratch=[pltpu.VMEM((3 * TOK, HD), BF16), pltpu.VMEM((3 * TOK, HD), BF16)],
    )
    got_before = swap(send_before)
    got = swap(send)
    (back,) = call(halo_body, [((TOK, HD), BF16)], place, keep_before, got_before)
    back = from_x(back, 1)
    (dout,) = call(
        pair_body, [((2 * TOK, 2 * HD), BF16)], place, dquery, keep, got, cos2, sin2, back
    )
    dout_1, dout_2, dout_3 = (from_x(dout, step) for step in (1, 2, 3))

    send_in, send_sum, keep_in, keep_sum = call(
        dnormed_body,
        [((4, TOK, SLAB), BF16), ((TOK, 128), F32)] * 2,
        place,
        dout,
        *slabs[:2],
        normed_other,
        *slabs[2:],
        normed,
    )
    got_in, got_sum = swap(send_in), swap(send_sum)
    *messages, own, own_sum = call(
        split_body,
        [((TOK, SLAB + 128), BF16)] * 3 + [((TOK, SLAB), F32), ((TOK, 128), F32)],
        place,
        keep_in,
        got_in,
        keep_sum,
        got_sum,
    )
    arrived = [from_y(message, step + 1) for step, message in enumerate(messages)]

    squares, chunks = call(
        weights_body,
        [((8, 128), F32), ((8, 112, 2 * HD), BF16)],
        place,
        after(dout, *messages),
        columns,
        dout_1,
        dout_2,
        dout_3,
    )
    chunks = lax.all_to_all(chunks, "dp", split_axis=0, concat_axis=0, tiled=True)
    for axis, size, step in (
        ("core", 2, 1),
        ("x", 4, 1),
        ("x", 4, 2),
        ("tensor", 4, 1),
        ("tensor", 4, 2),
        ("dp", 8, 1),
        ("dp", 8, 2),
        ("dp", 8, 4),
    ):
        pairs = [(i, i ^ step) for i in range(size)]
        squares = squares + lax.ppermute(squares, axis, pairs)
    (input_grad,) = call(
        input_body,
        [((1, TOK, SLAB), BF16)],
        place,
        own,
        own_sum,
        *arrived,
        moved,
        inverse,
        gain,
        permute,
    )
    chunks = after(chunks, squares, input_grad)
    upper, lower = chunks[:, :ROWS], chunks[:, ROWS:]
    rms = jnp.sqrt(squares[:, :1] * (1.0 / (D * (H + 2 * KVH) * HD)) + EPSILON)
    factor = (CLIP_BOUND / jnp.maximum(rms, CLIP_BOUND))[:, :, None]
    mine_out = jnp.where(first, upper, lower)
    got_out = swap(jnp.where(first, lower, upper))
    mine_out, got_out = (
        jnp.sum(one.astype(F32) * factor, 0) for one in (mine_out, got_out)
    )
    zero = jnp.where(first, mine_out, got_out)
    one = jnp.where(first, got_out, mine_out)
    grad_query = jnp.concatenate([zero[:, :HD], one[:, :HD]], 1)
    grad_key, grad_value = zero[:, HD:], one[:, HD:]
    return grad_query, grad_key, grad_value, input_grad


def solution(mesh):
    chips = Mesh(mesh.devices.reshape(4, 2, 4, 8), ("x", "core", "tensor", "dp"))
    seq = ("x", "core")
    weight = P((*seq, "dp"), "tensor")
    return jax.shard_map(
        local,
        mesh=chips,
        in_specs=(P("dp", seq, None), weight, weight, weight, P(), P("dp", seq, "tensor")),
        out_specs=(weight, weight, weight, P("dp", seq, "tensor")),
        check_vma=False,
    )
```

```python
import math

import jax
import jax.numpy as jnp
import numpy as np
from jax import lax
from jax.experimental import pallas as pl
from jax.experimental.pallas import tpu as pltpu
from jax.sharding import Mesh
from jax.sharding import PartitionSpec as P

D = 3584
H = 8
KVH = 4
HD = 256
WINDOW = 256
SLAB = D // 4
ROWS = 56
TOK = 256
CUT = 384

EPSILON = 1e-06
SOFTCAP = 50.0
CLIP_BOUND = 1.0
ROPE_BASE = 10000.0

F32 = jnp.float32
BF16 = jnp.bfloat16
ANY = pl.BlockSpec(memory_space=pl.ANY)
SMEM = pl.BlockSpec(memory_space=pltpu.SMEM)


class Arriving:
    def __init__(self, copy, ref):
        self.copy, self.ref, self.here = copy, ref, False

    def wait(self):
        if not self.here:
            self.copy.wait()
            self.here = True

    def __getitem__(self, at):
        self.wait()
        return self.ref[at]


class Leaving:
    def __init__(self, copy, ref):
        self.copy, self.ref, self.gone = copy, ref, False

    def __getitem__(self, at):
        return self.ref[at]

    def __setitem__(self, at, value):
        self.ref[at] = value

    def leave(self):
        if not self.gone:
            self.copy.start()
            self.gone = True


def call(body, outs, place, *operands, scratch=(), room=16):
    count, made = len(operands), len(outs)

    def kernel(place_ref, *refs):
        held = refs[count + made : 2 * (count + made)]
        sems = refs[2 * (count + made)]
        rest = refs[2 * (count + made) + 1 :]
        arriving = []
        for k in range(count):
            copy = pltpu.make_async_copy(refs[k], held[k], sems.at[k])
            copy.start()
            arriving.append(Arriving(copy, held[k]))
        leaving = []
        for k in range(count, count + made):
            copy = pltpu.make_async_copy(held[k], refs[k], sems.at[k])
            leaving.append(Leaving(copy, held[k]))
        body(place_ref, *arriving, *leaving, *rest)
        for one in leaving:
            one.leave()
        for one in arriving:
            one.wait()
        for one in leaving:
            one.copy.wait()

    return pl.pallas_call(
        kernel,
        out_shape=[jax.ShapeDtypeStruct(shape, kind) for shape, kind in outs],
        in_specs=[SMEM] + [ANY] * count,
        out_specs=[ANY] * made,
        scratch_shapes=[pltpu.VMEM(one.shape, one.dtype) for one in operands]
        + [pltpu.VMEM(shape, kind) for shape, kind in outs]
        + [pltpu.SemaphoreType.DMA((count + made,))]
        + list(scratch),
        compiler_params=pltpu.CompilerParams(vmem_limit_bytes=room * 1024 * 1024),
    )(place, *operands)


def swap(value):
    return lax.ppermute(value, "core", [(0, 1), (1, 0)])


def from_x(value, steps):
    return lax.ppermute(value, "x", [((i + steps) % 4, i) for i in range(4)])


def from_y(value, steps):
    return lax.ppermute(value, "tensor", [((i + steps) % 4, i) for i in range(4)])


def from_z(value, steps):
    return lax.ppermute(value, "dp", [((i + steps) % 8, i) for i in range(8)])


def after(value, *others):
    return lax.optimization_barrier((value, *others))[0]


def code(total):
    high = total.astype(BF16)
    rest = total - high.astype(F32)
    middle = rest.astype(BF16)
    low = (rest - middle.astype(F32)).astype(BF16)
    lane = lax.broadcasted_iota(jnp.int32, total.shape, 1)
    return jnp.where(
        lane == 0,
        high.astype(F32),
        jnp.where(
            lane == 1, middle.astype(F32), jnp.where(lane == 2, low.astype(F32), jnp.zeros_like(total))
        ),
    ).astype(BF16)


def mm(a, b, contract_a=1, contract_b=0):
    return lax.dot_general(
        a, b, (((contract_a,), (contract_b,)), ((), ())), preferred_element_type=F32
    )


def norm_body(place, permute, gain, inputs, normed, n0, q1, q2, q3, moved, inverse, moved_gain):
    x, y = place[0], place[2]
    wide = gain[...]
    high = wide.astype(BF16)
    middle = (wide - high.astype(F32)).astype(BF16)
    low = (wide - high.astype(F32) - middle.astype(F32)).astype(BF16)
    moved_gain[...] = mm(high, permute[...]) + mm(middle, permute[...]) + mm(low, permute[...])
    rows = inputs[...].astype(F32)
    inv = lax.rsqrt(jnp.sum(rows * rows, -1, keepdims=True) * (1.0 / D) + EPSILON)
    inverse[...] = jnp.broadcast_to(inv, inverse.ref.shape)
    for slab in range(4):
        part = mm(inputs[:, slab * SLAB : (slab + 1) * SLAB], permute[...])
        moved[slab] = part.astype(BF16)
        normed[slab] = (part * inv * moved_gain[slab : slab + 1, :]).astype(BF16)
    normed.leave()
    quarter = pl.ds(pl.multiple_of(y * 64, 64), 64)
    for step, one in ((1, q1), (2, q2), (3, q3)):
        one[...] = normed[lax.rem(x + 4 - step, 4), quarter, :]
        one.leave()
    n0[...] = normed[x]


def stack_body(place, own, far, up2, down2, up, down, top, bottom, whole):
    z = place[3]

    def put(step, rows):
        at = lax.rem(z + step, 8) * 112
        whole[pl.ds(pl.multiple_of(at, 16), 112), :] = rows

    put(0, own[...])
    put(4, far[...])
    put(2, up2[...])
    put(6, down2[...])
    put(1, up[:112, :])
    put(5, up[112:, :])
    put(7, down[:112, :])
    put(3, down[112:, :])
    top[...] = whole[:CUT, :]
    bottom[...] = whole[CUT:, :]


def columns_body(place, *refs):
    own, other, mine, theirs, whole, rows = refs[0], refs[1], refs[2:6], refs[6:10], refs[10], refs[11]
    x, core, y = place[0], place[1], place[2]
    for first, block, parts in ((own, core, mine), (other, 1 - core, theirs)):
        rows[x, pl.ds(pl.multiple_of(block * TOK, TOK), TOK), :] = first[...]
        for turn in range(4):
            at = pl.ds(pl.multiple_of(block * TOK + lax.rem(y + turn, 4) * 64, 64), 64)
            for step in range(1, 4):
                rows[lax.rem(x + step, 4), at, :] = parts[turn][(step - 1) * 64 : step * 64, :]
    for slab in range(4):
        whole[slab] = rows[slab].T


def spin(value, cosine, sine, direction):
    first, second = value[:, :128], value[:, 128:]
    return jnp.concatenate(
        [first * cosine - direction * second * sine, second * cosine + direction * first * sine], -1
    )


PIECES = tuple((step, start, stop) for step in (0, 1, 3, 2) for start, stop in ((0, CUT), (CUT, SLAB)))


def project_body(place, own, s0, s1, other, s2, s3, s4, s5, total, last):
    x = place[0]
    for turn, ((step, start, stop), slab) in enumerate(zip(PIECES, (s0, s1, s2, s3, s4, s5))):
        here = lax.rem(x + step, 4)
        for half, rows in enumerate((own, other)):
            part = mm(rows[here, :, start:stop], slab[...])
            total[half] = part if turn == 0 else total[half] + part
    for half, rows in enumerate((own, other)):
        last[half] = rows[lax.rem(x + 2, 4)]


def finish_body(place, last, s6, s7, total, cos2, sin2, cos, sin, pair, query):
    core = place[1]
    sums = []
    for half in range(2):
        sums.append(total[half] + mm(last[half, :, :CUT], s6[...]) + mm(last[half, :, CUT:], s7[...]))
    for half, block in ((0, core), (1, 1 - core)):
        at = pl.ds(pl.multiple_of(block * TOK, TOK), TOK)
        pair[at, :] = spin(sums[half][:, HD:], cos2[at, :], sin2[at, :], 1.0).astype(BF16)
    pair.leave()
    for half, block in ((0, core), (1, 1 - core)):
        at = pl.ds(pl.multiple_of(block * TOK, TOK), TOK)
        query[at, :] = spin(sums[half][:, :HD], cos[at, :], sin[at, :], 1.0).astype(BF16)


def attend_body(place, query, mine, theirs, mine_before, theirs_before, cot, cos, sin,
                dquery, keep, keep_before, send, send_before, keys, values):
    first_core = place[1] == 0
    for at, a, b in ((0, mine_before, theirs_before), (TOK, mine, theirs)):
        rows = a.ref.shape[0]
        keys[at : at + rows, :] = jnp.where(first_core, a[...], b[...])
        values[at : at + rows, :] = jnp.where(first_core, b[...], a[...])
    scale = 1.0 / math.sqrt(HD)
    q_at = lax.broadcasted_iota(jnp.int32, (TOK, 2 * TOK), 0)
    k_at = lax.broadcasted_iota(jnp.int32, (TOK, 2 * TOK), 1)
    band = (k_at <= q_at + TOK) & (k_at > q_at)
    key_parts = []
    value_parts = []
    for block in range(2):
        here = slice(block * TOK, (block + 1) * TOK)
        seen = slice(block * TOK, (block + 2) * TOK)
        q, g = query[here, :], cot[here, :]
        k, v = keys[seen, :], values[seen, :]
        squash = jnp.tanh(mm(q, k, 1, 1) * (scale / SOFTCAP))
        allowed = band
        if block == 0:
            allowed = band & ((k_at >= TOK) | (place[0] > 0))
        terms = jnp.where(allowed, jnp.exp(SOFTCAP * squash), 0.0)
        probs = terms / jnp.sum(terms, -1, keepdims=True)
        dprobs = mm(g, v, 1, 1)
        value_parts.append(mm(probs.astype(BF16), g, 0, 0))
        delta = jnp.sum(probs * dprobs, -1, keepdims=True)
        dlogits = (probs * (dprobs - delta) * (1.0 - squash * squash) * scale).astype(BF16)
        dq = mm(dlogits, k)
        dquery[here, :] = spin(dq, cos[here, :], sin[here, :], -1.0).astype(BF16)
        key_parts.append(mm(dlogits, q, 0, 0))

    def place_out(dk, dv, keep_at, send_at, here):
        keep_at[here, :] = jnp.where(first_core, dk, dv)
        send_at[here, :] = jnp.where(first_core, dv, dk).astype(BF16)

    place_out(key_parts[0][:TOK], value_parts[0][:TOK], keep_before, send_before, slice(0, TOK))
    place_out(
        key_parts[0][TOK:] + key_parts[1][:TOK],
        value_parts[0][TOK:] + value_parts[1][:TOK],
        keep,
        send,
        slice(0, TOK),
    )
    place_out(key_parts[1][TOK:], value_parts[1][TOK:], keep, send, slice(TOK, 2 * TOK))


def halo_body(place, keep_before, got_before, out):
    out[...] = (keep_before[...] + got_before[...].astype(F32)).astype(BF16)


def pair_body(place, dquery, keep, got, cos2, sin2, back, dout):
    dout[:, :HD] = dquery[...]
    for block in range(2):
        here = slice(block * TOK, (block + 1) * TOK)
        total = keep[here, :] + got[here, :].astype(F32)
        if block == 1:
            total += back[...].astype(F32)
        dout[here, HD:] = spin(total, cos2[here, :], sin2[here, :], -1.0).astype(BF16)


def dnormed_body(
    place, dout, s0, s1, other, s2, s3, s4, s5, s6, s7, own, send, send_sum, keep, keep_sum
):
    x, core = place[0], place[1]
    for rows, block, out, sums in (
        (other, 1 - core, send, send_sum),
        (own, core, keep, keep_sum),
    ):
        d = dout[pl.ds(pl.multiple_of(block * TOK, TOK), TOK), :]
        total = jnp.zeros((TOK, 1), F32)
        for (step, start, stop), slab in zip(PIECES, (s0, s1, s2, s3, s4, s5, s6, s7)):
            here = lax.rem(x + step, 4)
            part = mm(d, slab[...], 1, 1)
            total += jnp.sum(part * rows[here, :, start:stop].astype(F32), -1, keepdims=True)
            out[here, :, start:stop] = part.astype(BF16)
        sums[...] = jnp.broadcast_to(total, sums.ref.shape)
        out.leave()
        sums.leave()


def split_body(place, keep, got, keep_sum, got_sum, m1, m2, m3, own, own_sum):
    y = place[2]
    total = keep_sum[...] + got_sum[...]
    own_sum[...] = total
    coded = code(total)
    for step, message in enumerate((m1, m2, m3)):
        at = lax.rem(y + 4 - (step + 1), 4)
        message[:, :SLAB] = (keep[at].astype(F32) + got[at].astype(F32)).astype(BF16)
        message[:, SLAB:] = coded
        message.leave()
    own[...] = keep[y].astype(F32) + got[y].astype(F32)


def input_body(place, own, own_sum, m1, m2, m3, moved, inverse, gain, permute, out):
    total = own[...]
    sums = own_sum[:, :1]
    for message in (m1, m2, m3):
        total += message[:, :SLAB].astype(F32)
        sums += jnp.sum(message[:, SLAB:].astype(F32), -1, keepdims=True)
    inv = inverse[:, :1]
    y = place[2]
    rows = moved[y].astype(F32)
    grad = inv * (gain[pl.ds(y, 1), :] * total) - rows * ((inv * inv) * (sums * (1.0 / D)))
    out[0] = mm(grad.astype(BF16), permute[...], 1, 1).astype(BF16)


def weights_body(place, d0, columns, d1, d2, d3, squares, chunks):
    x, z = place[0], place[3]
    acc = mm(columns[x], d0[...])
    for step, d in ((1, d1), (2, d2), (3, d3)):
        acc += mm(columns[lax.rem(x + step, 4)], d[...])
    for chunk in range(8):
        chunks[chunk] = acc[chunk * 112 : (chunk + 1) * 112, :].astype(BF16)
    chunks.leave()
    row = lax.broadcasted_iota(jnp.int32, (8, 128), 0)
    squares[...] = jnp.where(row == z, jnp.sum(acc * acc), 0.0)


def local(inputs, w_query, w_key, w_value, norm_gain, attn_grad):
    x = lax.axis_index("x").astype(jnp.int32)
    core = lax.axis_index("core").astype(jnp.int32)
    y = lax.axis_index("tensor").astype(jnp.int32)
    z = lax.axis_index("dp").astype(jnp.int32)
    place = jnp.stack([x, core, y, z])
    first = core == 0

    low, high = w_query[:, :HD], w_query[:, HD:]
    mine = jnp.concatenate([jnp.where(first, low, high), jnp.where(first, w_key, w_value)], 1)
    theirs = jnp.concatenate([jnp.where(first, high, low), jnp.where(first, w_value, w_key)], 1)
    got = swap(theirs)
    block = jnp.concatenate([jnp.where(first, mine, got), jnp.where(first, got, mine)], 0)
    far = from_z(block, 4)
    up2, down2 = from_z(block, 2), from_z(block, -2)
    far, up2, down2 = lax.optimization_barrier((far, up2, down2))
    both = jnp.concatenate([block, far], 0)
    up, down = from_z(both, 1), from_z(both, -1)

    index = np.arange(SLAB)
    natural = (index % 112) // ROWS * 448 + index // 112 * ROWS + index % ROWS
    permute = (
        lax.broadcasted_iota(jnp.int32, (SLAB, SLAB), 0) == jnp.asarray(natural, jnp.int32)[None, :]
    ).astype(BF16)
    normed, own_columns, *quarters, moved, inverse, gain = call(
        norm_body,
        [((4, TOK, SLAB), BF16), ((TOK, SLAB), BF16)]
        + [((TOK // 4, SLAB), BF16)] * 3
        + [((4, TOK, SLAB), BF16), ((TOK, 128), F32), ((4, SLAB), F32)],
        place,
        permute,
        norm_gain.reshape(4, SLAB),
        after(inputs[0], far),
        room=60,
    )
    top, bottom = call(
        stack_body,
        [((CUT, 2 * HD), BF16), ((SLAB - CUT, 2 * HD), BF16)],
        place,
        after(block, normed),
        far,
        up2,
        down2,
        up,
        down,
        scratch=[pltpu.VMEM((SLAB, 2 * HD), BF16)],
    )
    normed_late = after(normed, up, down)
    *quarters, _, _ = lax.optimization_barrier((*quarters, top, bottom))
    bundle = jnp.concatenate([from_x(one, step + 1) for step, one in enumerate(quarters)], 0)
    normed_other = swap(normed_late)
    near = (from_x(top, 1), from_x(bottom, 1), from_x(top, -1), from_x(bottom, -1))
    near = lax.optimization_barrier(near)
    slabs = (top, bottom, *near, from_x(near[0], 1), from_x(near[3], -1))
    bundles = (bundle, from_y(bundle, 1), from_y(bundle, 2), from_y(bundle, 3))
    theirs = [swap(one) for one in bundles]
    theirs_own = swap(own_columns)
    (columns,) = call(
        columns_body,
        [((4, SLAB, 2 * TOK), BF16)],
        place,
        own_columns,
        theirs_own,
        *bundles,
        *theirs,
        scratch=[pltpu.VMEM((4, 2 * TOK, SLAB), BF16)],
    )

    cot_low, cot_high = attn_grad[0][:, :HD], attn_grad[0][:, HD:]
    cot_mine = jnp.where(first, cot_low, cot_high)
    cot_got = swap(jnp.where(first, cot_high, cot_low))
    cot = jnp.concatenate(
        [jnp.where(first, cot_mine, cot_got), jnp.where(first, cot_got, cot_mine)], 0
    )

    positions = x * (2 * TOK) + jnp.arange(2 * TOK, dtype=jnp.int32)
    frequency = ROPE_BASE ** (-2.0 * jnp.arange(HD // 2).astype(F32) / HD)
    phases = positions.astype(F32)[:, None] * frequency[None, :]
    cos, sin = jnp.cos(phases), jnp.sin(phases)
    cos2, sin2 = jnp.where(first, cos, 1.0), jnp.where(first, sin, 0.0)

    normed_other, cos, sin, cos2, sin2, _ = lax.optimization_barrier(
        (normed_other, cos, sin, cos2, sin2, bundle)
    )
    cot = after(cot, theirs_own, *theirs)
    total, last = call(
        project_body,
        [((2, TOK, 2 * HD), F32), ((2, TOK, SLAB), BF16)],
        place,
        normed,
        *slabs[:2],
        normed_other,
        *slabs[2:6],
    )
    pair, query = call(
        finish_body,
        [((2 * TOK, HD), BF16), ((2 * TOK, HD), BF16)],
        place,
        last,
        *slabs[6:],
        total,
        cos2,
        sin2,
        cos,
        sin,
    )
    pair_other = swap(pair)
    before = from_x(pair[TOK:], -1)
    before_other = swap(before)
    dquery, keep, keep_before, send, send_before = call(
        attend_body,
        [
            ((2 * TOK, HD), BF16),
            ((2 * TOK, HD), F32),
            ((TOK, HD), F32),
            ((2 * TOK, HD), BF16),
            ((TOK, HD), BF16),
        ],
        place,
        query,
        pair,
        pair_other,
        before,
        before_other,
        cot,
        cos,
        sin,
        scratch=[pltpu.VMEM((3 * TOK, HD), BF16), pltpu.VMEM((3 * TOK, HD), BF16)],
    )
    got_before = swap(send_before)
    got = swap(send)
    (back,) = call(halo_body, [((TOK, HD), BF16)], place, keep_before, got_before)
    back = from_x(back, 1)
    (dout,) = call(
        pair_body, [((2 * TOK, 2 * HD), BF16)], place, dquery, keep, got, cos2, sin2, back
    )
    dout_1, dout_2, dout_3 = (from_x(dout, step) for step in (1, 2, 3))

    send_in, send_sum, keep_in, keep_sum = call(
        dnormed_body,
        [((4, TOK, SLAB), BF16), ((TOK, 128), F32)] * 2,
        place,
        dout,
        *slabs[:2],
        normed_other,
        *slabs[2:],
        normed,
    )
    got_in, got_sum = swap(send_in), swap(send_sum)
    *messages, own, own_sum = call(
        split_body,
        [((TOK, SLAB + 128), BF16)] * 3 + [((TOK, SLAB), F32), ((TOK, 128), F32)],
        place,
        keep_in,
        got_in,
        keep_sum,
        got_sum,
    )
    arrived = [from_y(message, step + 1) for step, message in enumerate(messages)]

    squares, chunks = call(
        weights_body,
        [((8, 128), F32), ((8, 112, 2 * HD), BF16)],
        place,
        dout,
        columns,
        dout_1,
        dout_2,
        dout_3,
    )
    chunks = lax.all_to_all(after(chunks, arrived[0], arrived[2]), "dp", split_axis=0, concat_axis=0, tiled=True)
    for axis in ("core", "x", "tensor"):
        squares = lax.optimization_barrier(lax.psum(squares, axis))
    (input_grad,) = call(
        input_body,
        [((1, TOK, SLAB), BF16)],
        place,
        own,
        own_sum,
        *arrived,
        moved,
        inverse,
        gain,
        permute,
    )
    chunks = after(chunks, squares, input_grad)
    for step in (1, 2, 4):
        squares = squares + lax.ppermute(squares, "dp", [(i, i ^ step) for i in range(8)])
    upper, lower = chunks[:, :ROWS], chunks[:, ROWS:]
    rms = jnp.sqrt(squares[:, :1] * (1.0 / (D * (H + 2 * KVH) * HD)) + EPSILON)
    factor = (CLIP_BOUND / jnp.maximum(rms, CLIP_BOUND))[:, :, None]
    mine_out = jnp.where(first, upper, lower)
    got_out = swap(jnp.where(first, lower, upper))
    mine_out, got_out = (
        jnp.sum(one.astype(F32) * factor, 0) for one in (mine_out, got_out)
    )
    zero = jnp.where(first, mine_out, got_out)
    one = jnp.where(first, got_out, mine_out)
    grad_query = jnp.concatenate([zero[:, :HD], one[:, :HD]], 1)
    grad_key, grad_value = zero[:, HD:], one[:, HD:]
    return grad_query, grad_key, grad_value, input_grad


def solution(mesh):
    chips = Mesh(mesh.devices.reshape(4, 2, 4, 8), ("x", "core", "tensor", "dp"))
    seq = ("x", "core")
    weight = P((*seq, "dp"), "tensor")
    return jax.shard_map(
        local,
        mesh=chips,
        in_specs=(P("dp", seq, None), weight, weight, weight, P(), P("dp", seq, "tensor")),
        out_specs=(weight, weight, weight, P("dp", seq, "tensor")),
        check_vma=False,
    )
```

```python
import math

import jax
import jax.numpy as jnp
import numpy as np
from jax import lax
from jax.experimental import pallas as pl
from jax.experimental.pallas import tpu as pltpu
from jax.sharding import Mesh
from jax.sharding import PartitionSpec as P

D = 3584
H = 8
KVH = 4
HD = 256
WINDOW = 256
SLAB = D // 4
ROWS = 56
TOK = 256
CUT = 384

EPSILON = 1e-06
SOFTCAP = 50.0
CLIP_BOUND = 1.0
ROPE_BASE = 10000.0

F32 = jnp.float32
BF16 = jnp.bfloat16
ANY = pl.BlockSpec(memory_space=pl.ANY)
SMEM = pl.BlockSpec(memory_space=pltpu.SMEM)


class Arriving:
    def __init__(self, copy, ref):
        self.copy, self.ref, self.here = copy, ref, False

    def wait(self):
        if not self.here:
            self.copy.wait()
            self.here = True

    def __getitem__(self, at):
        self.wait()
        return self.ref[at]


class Leaving:
    def __init__(self, copy, ref):
        self.copy, self.ref, self.gone = copy, ref, False

    def __getitem__(self, at):
        return self.ref[at]

    def __setitem__(self, at, value):
        self.ref[at] = value

    def leave(self):
        if not self.gone:
            self.copy.start()
            self.gone = True


def call(body, outs, place, *operands, scratch=(), room=16):
    count, made = len(operands), len(outs)

    def kernel(place_ref, *refs):
        held = refs[count + made : 2 * (count + made)]
        sems = refs[2 * (count + made)]
        rest = refs[2 * (count + made) + 1 :]
        arriving = []
        for k in range(count):
            copy = pltpu.make_async_copy(refs[k], held[k], sems.at[k])
            copy.start()
            arriving.append(Arriving(copy, held[k]))
        leaving = []
        for k in range(count, count + made):
            copy = pltpu.make_async_copy(held[k], refs[k], sems.at[k])
            leaving.append(Leaving(copy, held[k]))
        body(place_ref, *arriving, *leaving, *rest)
        for one in leaving:
            one.leave()
        for one in arriving:
            one.wait()
        for one in leaving:
            one.copy.wait()

    return pl.pallas_call(
        kernel,
        out_shape=[jax.ShapeDtypeStruct(shape, kind) for shape, kind in outs],
        in_specs=[SMEM] + [ANY] * count,
        out_specs=[ANY] * made,
        scratch_shapes=[pltpu.VMEM(one.shape, one.dtype) for one in operands]
        + [pltpu.VMEM(shape, kind) for shape, kind in outs]
        + [pltpu.SemaphoreType.DMA((count + made,))]
        + list(scratch),
        compiler_params=pltpu.CompilerParams(vmem_limit_bytes=room * 1024 * 1024),
    )(place, *operands)


def swap(value):
    return lax.ppermute(value, "core", [(0, 1), (1, 0)])


def from_x(value, steps):
    return lax.ppermute(value, "x", [((i + steps) % 4, i) for i in range(4)])


def from_y(value, steps):
    return lax.ppermute(value, "tensor", [((i + steps) % 4, i) for i in range(4)])


def from_z(value, steps):
    return lax.ppermute(value, "dp", [((i + steps) % 8, i) for i in range(8)])


def after(value, *others):
    return lax.optimization_barrier((value, *others))[0]


def code(total):
    high = total.astype(BF16)
    rest = total - high.astype(F32)
    middle = rest.astype(BF16)
    low = (rest - middle.astype(F32)).astype(BF16)
    lane = lax.broadcasted_iota(jnp.int32, total.shape, 1)
    return jnp.where(
        lane == 0,
        high.astype(F32),
        jnp.where(
            lane == 1, middle.astype(F32), jnp.where(lane == 2, low.astype(F32), jnp.zeros_like(total))
        ),
    ).astype(BF16)


def mm(a, b, contract_a=1, contract_b=0):
    return lax.dot_general(
        a, b, (((contract_a,), (contract_b,)), ((), ())), preferred_element_type=F32
    )


def norm_body(place, permute, gain, inputs, normed, n0, q1, q2, q3, moved, inverse, moved_gain):
    x, y = place[0], place[2]
    wide = gain[...]
    high = wide.astype(BF16)
    middle = (wide - high.astype(F32)).astype(BF16)
    low = (wide - high.astype(F32) - middle.astype(F32)).astype(BF16)
    moved_gain[...] = mm(high, permute[...]) + mm(middle, permute[...]) + mm(low, permute[...])
    rows = inputs[...].astype(F32)
    inv = lax.rsqrt(jnp.sum(rows * rows, -1, keepdims=True) * (1.0 / D) + EPSILON)
    inverse[...] = jnp.broadcast_to(inv, inverse.ref.shape)
    for slab in range(4):
        part = mm(inputs[:, slab * SLAB : (slab + 1) * SLAB], permute[...])
        moved[slab] = part.astype(BF16)
        normed[slab] = (part * inv * moved_gain[slab : slab + 1, :]).astype(BF16)
    normed.leave()
    quarter = pl.ds(pl.multiple_of(y * 64, 64), 64)
    for step, one in ((1, q1), (2, q2), (3, q3)):
        one[...] = normed[lax.rem(x + 4 - step, 4), quarter, :]
        one.leave()
    n0[...] = normed[x]


def stack_body(place, own, far, up2, down2, up, down, top, bottom, whole):
    z = place[3]

    def put(step, rows):
        at = lax.rem(z + step, 8) * 112
        whole[pl.ds(pl.multiple_of(at, 16), 112), :] = rows

    put(0, own[...])
    put(4, far[...])
    put(2, up2[...])
    put(6, down2[...])
    put(1, up[:112, :])
    put(5, up[112:, :])
    put(7, down[:112, :])
    put(3, down[112:, :])
    top[...] = whole[:CUT, :]
    bottom[...] = whole[CUT:, :]


def columns_body(place, *refs):
    own, other, mine, theirs, whole, rows = refs[0], refs[1], refs[2:6], refs[6:10], refs[10], refs[11]
    x, core, y = place[0], place[1], place[2]
    for first, block, parts in ((own, core, mine), (other, 1 - core, theirs)):
        rows[x, pl.ds(pl.multiple_of(block * TOK, TOK), TOK), :] = first[...]
        for turn in range(4):
            at = pl.ds(pl.multiple_of(block * TOK + lax.rem(y + turn, 4) * 64, 64), 64)
            for step in range(1, 4):
                rows[lax.rem(x + step, 4), at, :] = parts[turn][(step - 1) * 64 : step * 64, :]
    for slab in range(4):
        whole[slab] = rows[slab].T


def spin(value, cosine, sine, direction):
    first, second = value[:, :128], value[:, 128:]
    return jnp.concatenate(
        [first * cosine - direction * second * sine, second * cosine + direction * first * sine], -1
    )


PIECES = tuple((step, start, stop) for step in (0, 1, 3, 2) for start, stop in ((0, CUT), (CUT, SLAB)))


def project_body(place, own, s0, s1, other, s2, s3, s4, s5, total, last):
    x = place[0]
    for turn, ((step, start, stop), slab) in enumerate(zip(PIECES, (s0, s1, s2, s3, s4, s5))):
        here = lax.rem(x + step, 4)
        for half, rows in enumerate((own, other)):
            part = mm(rows[here, :, start:stop], slab[...])
            total[half] = part if turn == 0 else total[half] + part
    for half, rows in enumerate((own, other)):
        last[half] = rows[lax.rem(x + 2, 4)]


def finish_body(place, last, s6, s7, total, cos2, sin2, cos, sin, pair, query):
    core = place[1]
    sums = []
    for half in range(2):
        sums.append(total[half] + mm(last[half, :, :CUT], s6[...]) + mm(last[half, :, CUT:], s7[...]))
    for half, block in ((0, core), (1, 1 - core)):
        at = pl.ds(pl.multiple_of(block * TOK, TOK), TOK)
        pair[at, :] = spin(sums[half][:, HD:], cos2[at, :], sin2[at, :], 1.0).astype(BF16)
    pair.leave()
    for half, block in ((0, core), (1, 1 - core)):
        at = pl.ds(pl.multiple_of(block * TOK, TOK), TOK)
        query[at, :] = spin(sums[half][:, :HD], cos[at, :], sin[at, :], 1.0).astype(BF16)


def attend_body(place, query, mine, theirs, mine_before, theirs_before, cot, cos, sin,
                dquery, keep, keep_before, send, send_before, keys, values):
    first_core = place[1] == 0
    for at, a, b in ((0, mine_before, theirs_before), (TOK, mine, theirs)):
        rows = a.ref.shape[0]
        keys[at : at + rows, :] = jnp.where(first_core, a[...], b[...])
        values[at : at + rows, :] = jnp.where(first_core, b[...], a[...])
    scale = 1.0 / math.sqrt(HD)
    q_at = lax.broadcasted_iota(jnp.int32, (TOK, 2 * TOK), 0)
    k_at = lax.broadcasted_iota(jnp.int32, (TOK, 2 * TOK), 1)
    band = (k_at <= q_at + TOK) & (k_at > q_at)
    key_parts = []
    value_parts = []
    for block in range(2):
        here = slice(block * TOK, (block + 1) * TOK)
        seen = slice(block * TOK, (block + 2) * TOK)
        q, g = query[here, :], cot[here, :]
        k, v = keys[seen, :], values[seen, :]
        squash = jnp.tanh(mm(q, k, 1, 1) * (scale / SOFTCAP))
        allowed = band
        if block == 0:
            allowed = band & ((k_at >= TOK) | (place[0] > 0))
        terms = jnp.where(allowed, jnp.exp(SOFTCAP * squash), 0.0)
        probs = terms / jnp.sum(terms, -1, keepdims=True)
        dprobs = mm(g, v, 1, 1)
        value_parts.append(mm(probs.astype(BF16), g, 0, 0))
        delta = jnp.sum(probs * dprobs, -1, keepdims=True)
        dlogits = (probs * (dprobs - delta) * (1.0 - squash * squash) * scale).astype(BF16)
        dq = mm(dlogits, k)
        dquery[here, :] = spin(dq, cos[here, :], sin[here, :], -1.0).astype(BF16)
        key_parts.append(mm(dlogits, q, 0, 0))

    def place_out(dk, dv, keep_at, send_at, here):
        keep_at[here, :] = jnp.where(first_core, dk, dv)
        send_at[here, :] = jnp.where(first_core, dv, dk).astype(BF16)

    place_out(key_parts[0][:TOK], value_parts[0][:TOK], keep_before, send_before, slice(0, TOK))
    place_out(
        key_parts[0][TOK:] + key_parts[1][:TOK],
        value_parts[0][TOK:] + value_parts[1][:TOK],
        keep,
        send,
        slice(0, TOK),
    )
    place_out(key_parts[1][TOK:], value_parts[1][TOK:], keep, send, slice(TOK, 2 * TOK))


def halo_body(place, keep_before, got_before, out):
    out[...] = (keep_before[...] + got_before[...].astype(F32)).astype(BF16)


def pair_body(place, dquery, keep, got, cos2, sin2, back, dout):
    dout[:, :HD] = dquery[...]
    for block in range(2):
        here = slice(block * TOK, (block + 1) * TOK)
        total = keep[here, :] + got[here, :].astype(F32)
        if block == 1:
            total += back[...].astype(F32)
        dout[here, HD:] = spin(total, cos2[here, :], sin2[here, :], -1.0).astype(BF16)


def dnormed_body(
    place, dout, s0, s1, other, s2, s3, s4, s5, s6, s7, own, send, send_sum, keep, keep_sum
):
    x, core = place[0], place[1]
    for rows, block, out, sums in (
        (other, 1 - core, send, send_sum),
        (own, core, keep, keep_sum),
    ):
        d = dout[pl.ds(pl.multiple_of(block * TOK, TOK), TOK), :]
        total = jnp.zeros((TOK, 1), F32)
        for (step, start, stop), slab in zip(PIECES, (s0, s1, s2, s3, s4, s5, s6, s7)):
            here = lax.rem(x + step, 4)
            part = mm(d, slab[...], 1, 1)
            total += jnp.sum(part * rows[here, :, start:stop].astype(F32), -1, keepdims=True)
            out[here, :, start:stop] = part.astype(BF16)
        sums[...] = jnp.broadcast_to(total, sums.ref.shape)
        out.leave()
        sums.leave()


def split_body(place, keep, got, keep_sum, got_sum, m1, m2, m3, own, own_sum):
    y = place[2]
    total = keep_sum[...] + got_sum[...]
    own_sum[...] = total
    coded = code(total)
    for step, message in enumerate((m1, m2, m3)):
        at = lax.rem(y + 4 - (step + 1), 4)
        message[:, :SLAB] = (keep[at].astype(F32) + got[at].astype(F32)).astype(BF16)
        message[:, SLAB:] = coded
        message.leave()
    own[...] = keep[y].astype(F32) + got[y].astype(F32)


def input_body(place, own, own_sum, m1, m2, m3, moved, inverse, gain, permute, out):
    total = own[...]
    sums = own_sum[:, :1]
    for message in (m1, m2, m3):
        total += message[:, :SLAB].astype(F32)
        sums += jnp.sum(message[:, SLAB:].astype(F32), -1, keepdims=True)
    inv = inverse[:, :1]
    y = place[2]
    rows = moved[y].astype(F32)
    grad = inv * (gain[pl.ds(y, 1), :] * total) - rows * ((inv * inv) * (sums * (1.0 / D)))
    out[0] = mm(grad.astype(BF16), permute[...], 1, 1).astype(BF16)


def weights_body(place, d0, columns, d1, d2, d3, squares, chunks):
    x, z = place[0], place[3]
    acc = mm(columns[x], d0[...])
    for step, d in ((1, d1), (2, d2), (3, d3)):
        acc += mm(columns[lax.rem(x + step, 4)], d[...])
    for chunk in range(8):
        chunks[chunk] = acc[chunk * 112 : (chunk + 1) * 112, :].astype(BF16)
    chunks.leave()
    row = lax.broadcasted_iota(jnp.int32, (8, 128), 0)
    squares[...] = jnp.where(row == z, jnp.sum(acc * acc), 0.0)


def local(inputs, w_query, w_key, w_value, norm_gain, attn_grad):
    x = lax.axis_index("x").astype(jnp.int32)
    core = lax.axis_index("core").astype(jnp.int32)
    y = lax.axis_index("tensor").astype(jnp.int32)
    z = lax.axis_index("dp").astype(jnp.int32)
    place = jnp.stack([x, core, y, z])
    first = core == 0

    low, high = w_query[:, :HD], w_query[:, HD:]
    mine = jnp.concatenate([jnp.where(first, low, high), jnp.where(first, w_key, w_value)], 1)
    theirs = jnp.concatenate([jnp.where(first, high, low), jnp.where(first, w_value, w_key)], 1)
    got = swap(theirs)
    block = jnp.concatenate([jnp.where(first, mine, got), jnp.where(first, got, mine)], 0)
    index = np.arange(SLAB)
    natural = (index % 112) // ROWS * 448 + index // 112 * ROWS + index % ROWS
    permute = (
        lax.broadcasted_iota(jnp.int32, (SLAB, SLAB), 0) == jnp.asarray(natural, jnp.int32)[None, :]
    ).astype(BF16)
    far = from_z(block, 4)
    up2, down2 = from_z(block, 2), from_z(block, -2)
    far, up2, down2, permute = lax.optimization_barrier((far, up2, down2, permute))
    both = jnp.concatenate([block, far], 0)
    up, down = from_z(both, 1), from_z(both, -1)

    normed, own_columns, *quarters, moved, inverse, gain = call(
        norm_body,
        [((4, TOK, SLAB), BF16), ((TOK, SLAB), BF16)]
        + [((TOK // 4, SLAB), BF16)] * 3
        + [((4, TOK, SLAB), BF16), ((TOK, 128), F32), ((4, SLAB), F32)],
        place,
        permute,
        norm_gain.reshape(4, SLAB),
        after(inputs[0], far),
        room=60,
    )
    *quarters, normed_late, _, _ = lax.optimization_barrier((*quarters, normed, up, down))
    quarters = lax.optimization_barrier(
        tuple(from_x(one, step + 1) for step, one in enumerate(quarters))
    )
    normed_other = swap(normed_late)
    top, bottom = call(
        stack_body,
        [((CUT, 2 * HD), BF16), ((SLAB - CUT, 2 * HD), BF16)],
        place,
        after(block, normed, *quarters),
        far,
        up2,
        down2,
        up,
        down,
        scratch=[pltpu.VMEM((SLAB, 2 * HD), BF16)],
    )
    bundle = jnp.concatenate(quarters, 0)
    near = (from_x(top, 1), from_x(bottom, 1), from_x(top, -1), from_x(bottom, -1))
    *near, bundle_1, bundle_3 = lax.optimization_barrier(
        (*near, from_y(bundle, 1), from_y(bundle, 3))
    )
    slabs = (top, bottom, *near, from_x(near[0], 1), from_x(near[3], -1))
    bundles = (bundle, bundle_1, from_y(bundle, 2), bundle_3)
    theirs = [swap(one) for one in bundles]
    theirs_own = swap(own_columns)
    (columns,) = call(
        columns_body,
        [((4, SLAB, 2 * TOK), BF16)],
        place,
        own_columns,
        theirs_own,
        *bundles,
        *theirs,
        scratch=[pltpu.VMEM((4, 2 * TOK, SLAB), BF16)],
    )

    cot_low, cot_high = attn_grad[0][:, :HD], attn_grad[0][:, HD:]
    cot_mine = jnp.where(first, cot_low, cot_high)
    cot_got = swap(jnp.where(first, cot_high, cot_low))
    cot = jnp.concatenate(
        [jnp.where(first, cot_mine, cot_got), jnp.where(first, cot_got, cot_mine)], 0
    )

    positions = x * (2 * TOK) + jnp.arange(2 * TOK, dtype=jnp.int32)
    frequency = ROPE_BASE ** (-2.0 * jnp.arange(HD // 2).astype(F32) / HD)
    phases = positions.astype(F32)[:, None] * frequency[None, :]
    cos, sin = jnp.cos(phases), jnp.sin(phases)
    cos2, sin2 = jnp.where(first, cos, 1.0), jnp.where(first, sin, 0.0)

    normed_other, cos, sin, cos2, sin2 = lax.optimization_barrier(
        (normed_other, cos, sin, cos2, sin2)
    )
    cot = after(cot, theirs_own, *theirs)
    total, last = call(
        project_body,
        [((2, TOK, 2 * HD), F32), ((2, TOK, SLAB), BF16)],
        place,
        normed,
        *slabs[:2],
        normed_other,
        *slabs[2:6],
    )
    pair, query = call(
        finish_body,
        [((2 * TOK, HD), BF16), ((2 * TOK, HD), BF16)],
        place,
        last,
        *slabs[6:],
        total,
        cos2,
        sin2,
        cos,
        sin,
    )
    pair_other = swap(pair)
    before = from_x(pair[TOK:], -1)
    before_other = swap(before)
    dquery, keep, keep_before, send, send_before = call(
        attend_body,
        [
            ((2 * TOK, HD), BF16),
            ((2 * TOK, HD), F32),
            ((TOK, HD), F32),
            ((2 * TOK, HD), BF16),
            ((TOK, HD), BF16),
        ],
        place,
        query,
        pair,
        pair_other,
        before,
        before_other,
        cot,
        cos,
        sin,
        scratch=[pltpu.VMEM((3 * TOK, HD), BF16), pltpu.VMEM((3 * TOK, HD), BF16)],
    )
    got_before = swap(send_before)
    got = swap(send)
    (back,) = call(halo_body, [((TOK, HD), BF16)], place, keep_before, got_before)
    back = from_x(back, 1)
    (dout,) = call(
        pair_body, [((2 * TOK, 2 * HD), BF16)], place, dquery, keep, got, cos2, sin2, back
    )
    dout_1, dout_2, dout_3 = (from_x(dout, step) for step in (1, 2, 3))

    send_in, send_sum, keep_in, keep_sum = call(
        dnormed_body,
        [((4, TOK, SLAB), BF16), ((TOK, 128), F32)] * 2,
        place,
        dout,
        *slabs[:2],
        normed_other,
        *slabs[2:],
        normed,
    )
    got_in, got_sum = swap(send_in), swap(send_sum)
    *messages, own, own_sum = call(
        split_body,
        [((TOK, SLAB + 128), BF16)] * 3 + [((TOK, SLAB), F32), ((TOK, 128), F32)],
        place,
        keep_in,
        got_in,
        keep_sum,
        got_sum,
    )
    arrived = [from_y(message, step + 1) for step, message in enumerate(messages)]

    squares, chunks = call(
        weights_body,
        [((8, 128), F32), ((8, 112, 2 * HD), BF16)],
        place,
        dout,
        columns,
        dout_1,
        dout_2,
        dout_3,
    )
    chunks = lax.all_to_all(after(chunks, *arrived), "dp", split_axis=0, concat_axis=0, tiled=True)
    squares = squares + swap(squares)
    squares = squares + sum(lax.optimization_barrier(tuple(from_x(squares, k) for k in range(1, 4))))
    squares = squares + sum(lax.optimization_barrier(tuple(from_y(squares, k) for k in range(1, 4))))
    squares = squares + sum(lax.optimization_barrier(tuple(from_z(squares, k) for k in range(1, 8))))
    own, squares = lax.optimization_barrier((own, squares))
    (input_grad,) = call(
        input_body,
        [((1, TOK, SLAB), BF16)],
        place,
        own,
        own_sum,
        *arrived,
        moved,
        inverse,
        gain,
        permute,
    )
    chunks = after(chunks, input_grad)
    upper, lower = chunks[:, :ROWS], chunks[:, ROWS:]
    rms = jnp.sqrt(squares[:, :1] * (1.0 / (D * (H + 2 * KVH) * HD)) + EPSILON)
    factor = (CLIP_BOUND / jnp.maximum(rms, CLIP_BOUND))[:, :, None]
    mine_out = jnp.where(first, upper, lower)
    got_out = swap(jnp.where(first, lower, upper))
    mine_out, got_out = (
        jnp.sum(one.astype(F32) * factor, 0) for one in (mine_out, got_out)
    )
    zero = jnp.where(first, mine_out, got_out)
    one = jnp.where(first, got_out, mine_out)
    grad_query = jnp.concatenate([zero[:, :HD], one[:, :HD]], 1)
    grad_key, grad_value = zero[:, HD:], one[:, HD:]
    return grad_query, grad_key, grad_value, input_grad


def solution(mesh):
    chips = Mesh(mesh.devices.reshape(4, 2, 4, 8), ("x", "core", "tensor", "dp"))
    seq = ("x", "core")
    weight = P((*seq, "dp"), "tensor")
    return jax.shard_map(
        local,
        mesh=chips,
        in_specs=(P("dp", seq, None), weight, weight, weight, P(), P("dp", seq, "tensor")),
        out_specs=(weight, weight, weight, P("dp", seq, "tensor")),
        check_vma=False,
    )
```

```python
import math

import jax
import jax.numpy as jnp
import numpy as np
from jax import lax
from jax.experimental import pallas as pl
from jax.experimental.pallas import tpu as pltpu
from jax.sharding import Mesh
from jax.sharding import PartitionSpec as P

D = 3584
H = 8
KVH = 4
HD = 256
WINDOW = 256
SLAB = D // 4
ROWS = 56
TOK = 256
CUT = 384

EPSILON = 1e-06
SOFTCAP = 50.0
CLIP_BOUND = 1.0
ROPE_BASE = 10000.0

F32 = jnp.float32
BF16 = jnp.bfloat16
ANY = pl.BlockSpec(memory_space=pl.ANY)
SMEM = pl.BlockSpec(memory_space=pltpu.SMEM)


class Arriving:
    def __init__(self, copy, ref):
        self.copy, self.ref, self.here = copy, ref, False

    def wait(self):
        if not self.here:
            self.copy.wait()
            self.here = True

    def __getitem__(self, at):
        self.wait()
        return self.ref[at]


class Leaving:
    def __init__(self, copy, ref):
        self.copy, self.ref, self.gone = copy, ref, False

    def __getitem__(self, at):
        return self.ref[at]

    def __setitem__(self, at, value):
        self.ref[at] = value

    def leave(self):
        if not self.gone:
            self.copy.start()
            self.gone = True


def call(body, outs, place, *operands, scratch=(), room=16):
    count, made = len(operands), len(outs)

    def kernel(place_ref, *refs):
        held = refs[count + made : 2 * (count + made)]
        sems = refs[2 * (count + made)]
        rest = refs[2 * (count + made) + 1 :]
        arriving = []
        for k in range(count):
            copy = pltpu.make_async_copy(refs[k], held[k], sems.at[k])
            copy.start()
            arriving.append(Arriving(copy, held[k]))
        leaving = []
        for k in range(count, count + made):
            copy = pltpu.make_async_copy(held[k], refs[k], sems.at[k])
            leaving.append(Leaving(copy, held[k]))
        body(place_ref, *arriving, *leaving, *rest)
        for one in leaving:
            one.leave()
        for one in arriving:
            one.wait()
        for one in leaving:
            one.copy.wait()

    return pl.pallas_call(
        kernel,
        out_shape=[jax.ShapeDtypeStruct(shape, kind) for shape, kind in outs],
        in_specs=[SMEM] + [ANY] * count,
        out_specs=[ANY] * made,
        scratch_shapes=[pltpu.VMEM(one.shape, one.dtype) for one in operands]
        + [pltpu.VMEM(shape, kind) for shape, kind in outs]
        + [pltpu.SemaphoreType.DMA((count + made,))]
        + list(scratch),
        compiler_params=pltpu.CompilerParams(vmem_limit_bytes=room * 1024 * 1024),
    )(place, *operands)


def swap(value):
    return lax.ppermute(value, "core", [(0, 1), (1, 0)])


def from_x(value, steps):
    return lax.ppermute(value, "x", [((i + steps) % 4, i) for i in range(4)])


def from_y(value, steps):
    return lax.ppermute(value, "tensor", [((i + steps) % 4, i) for i in range(4)])


def from_z(value, steps):
    return lax.ppermute(value, "dp", [((i + steps) % 8, i) for i in range(8)])


def after(value, *others):
    return lax.optimization_barrier((value, *others))[0]


def code(total):
    high = total.astype(BF16)
    rest = total - high.astype(F32)
    middle = rest.astype(BF16)
    low = (rest - middle.astype(F32)).astype(BF16)
    lane = lax.broadcasted_iota(jnp.int32, total.shape, 1)
    return jnp.where(
        lane == 0,
        high.astype(F32),
        jnp.where(
            lane == 1, middle.astype(F32), jnp.where(lane == 2, low.astype(F32), jnp.zeros_like(total))
        ),
    ).astype(BF16)


def mm(a, b, contract_a=1, contract_b=0):
    return lax.dot_general(
        a, b, (((contract_a,), (contract_b,)), ((), ())), preferred_element_type=F32
    )


def norm_body(place, permute, gain, inputs, normed, n0, q1, q2, q3, moved, inverse, moved_gain):
    x, y = place[0], place[2]
    wide = gain[...]
    high = wide.astype(BF16)
    middle = (wide - high.astype(F32)).astype(BF16)
    low = (wide - high.astype(F32) - middle.astype(F32)).astype(BF16)
    moved_gain[...] = mm(high, permute[...]) + mm(middle, permute[...]) + mm(low, permute[...])
    rows = inputs[...].astype(F32)
    inv = lax.rsqrt(jnp.sum(rows * rows, -1, keepdims=True) * (1.0 / D) + EPSILON)
    inverse[...] = jnp.broadcast_to(inv, inverse.ref.shape)
    for slab in range(4):
        part = mm(inputs[:, slab * SLAB : (slab + 1) * SLAB], permute[...])
        moved[slab] = part.astype(BF16)
        normed[slab] = (part * inv * moved_gain[slab : slab + 1, :]).astype(BF16)
    normed.leave()
    quarter = pl.ds(pl.multiple_of(y * 64, 64), 64)
    for step, one in ((1, q1), (2, q2), (3, q3)):
        one[...] = normed[lax.rem(x + 4 - step, 4), quarter, :]
        one.leave()
    n0[...] = normed[x]


def stack_body(place, own, far, up2, down2, up, down, top, bottom, whole):
    z = place[3]

    def put(step, rows):
        at = lax.rem(z + step, 8) * 112
        whole[pl.ds(pl.multiple_of(at, 16), 112), :] = rows

    put(0, own[...])
    put(4, far[...])
    put(2, up2[...])
    put(6, down2[...])
    put(1, up[:112, :])
    put(5, up[112:, :])
    put(7, down[:112, :])
    put(3, down[112:, :])
    top[...] = whole[:CUT, :]
    bottom[...] = whole[CUT:, :]


def columns_body(place, *refs):
    own, other, mine, theirs, whole, rows = refs[0], refs[1], refs[2:6], refs[6:10], refs[10], refs[11]
    x, core, y = place[0], place[1], place[2]
    for first, block, parts in ((own, core, mine), (other, 1 - core, theirs)):
        rows[x, pl.ds(pl.multiple_of(block * TOK, TOK), TOK), :] = first[...]
        for turn in range(4):
            at = pl.ds(pl.multiple_of(block * TOK + lax.rem(y + turn, 4) * 64, 64), 64)
            for step in range(1, 4):
                rows[lax.rem(x + step, 4), at, :] = parts[turn][(step - 1) * 64 : step * 64, :]
    for slab in range(4):
        whole[slab] = rows[slab].T


def spin(value, cosine, sine, direction):
    first, second = value[:, :128], value[:, 128:]
    return jnp.concatenate(
        [first * cosine - direction * second * sine, second * cosine + direction * first * sine], -1
    )


PIECES = tuple((step, start, stop) for step in (0, 1, 3, 2) for start, stop in ((0, CUT), (CUT, SLAB)))


def project_body(place, own, s0, s1, other, s2, s3, s4, s5, total, last):
    x = place[0]
    for turn, ((step, start, stop), slab) in enumerate(zip(PIECES, (s0, s1, s2, s3, s4, s5))):
        here = lax.rem(x + step, 4)
        for half, rows in enumerate((own, other)):
            part = mm(rows[here, :, start:stop], slab[...])
            total[half] = part if turn == 0 else total[half] + part
    for half, rows in enumerate((own, other)):
        last[half] = rows[lax.rem(x + 2, 4)]


def finish_body(place, last, s6, s7, total, cos2, sin2, cos, sin, pair, query):
    core = place[1]
    sums = []
    for half in range(2):
        sums.append(total[half] + mm(last[half, :, :CUT], s6[...]) + mm(last[half, :, CUT:], s7[...]))
    for half, block in ((0, core), (1, 1 - core)):
        at = pl.ds(pl.multiple_of(block * TOK, TOK), TOK)
        pair[at, :] = spin(sums[half][:, HD:], cos2[at, :], sin2[at, :], 1.0).astype(BF16)
    pair.leave()
    for half, block in ((0, core), (1, 1 - core)):
        at = pl.ds(pl.multiple_of(block * TOK, TOK), TOK)
        query[at, :] = spin(sums[half][:, :HD], cos[at, :], sin[at, :], 1.0).astype(BF16)


def attend_body(place, query, mine, theirs, mine_before, theirs_before, cot, cos, sin,
                dquery, keep, keep_before, send, send_before, keys, values):
    first_core = place[1] == 0
    for at, a, b in ((0, mine_before, theirs_before), (TOK, mine, theirs)):
        rows = a.ref.shape[0]
        keys[at : at + rows, :] = jnp.where(first_core, a[...], b[...])
        values[at : at + rows, :] = jnp.where(first_core, b[...], a[...])
    scale = 1.0 / math.sqrt(HD)
    q_at = lax.broadcasted_iota(jnp.int32, (TOK, 2 * TOK), 0)
    k_at = lax.broadcasted_iota(jnp.int32, (TOK, 2 * TOK), 1)
    band = (k_at <= q_at + TOK) & (k_at > q_at)
    key_parts = []
    value_parts = []
    for block in range(2):
        here = slice(block * TOK, (block + 1) * TOK)
        seen = slice(block * TOK, (block + 2) * TOK)
        q, g = query[here, :], cot[here, :]
        k, v = keys[seen, :], values[seen, :]
        squash = jnp.tanh(mm(q, k, 1, 1) * (scale / SOFTCAP))
        allowed = band
        if block == 0:
            allowed = band & ((k_at >= TOK) | (place[0] > 0))
        terms = jnp.where(allowed, jnp.exp(SOFTCAP * squash), 0.0)
        probs = terms / jnp.sum(terms, -1, keepdims=True)
        dprobs = mm(g, v, 1, 1)
        value_parts.append(mm(probs.astype(BF16), g, 0, 0))
        delta = jnp.sum(probs * dprobs, -1, keepdims=True)
        dlogits = (probs * (dprobs - delta) * (1.0 - squash * squash) * scale).astype(BF16)
        dq = mm(dlogits, k)
        dquery[here, :] = spin(dq, cos[here, :], sin[here, :], -1.0).astype(BF16)
        key_parts.append(mm(dlogits, q, 0, 0))

    def place_out(dk, dv, keep_at, send_at, here):
        keep_at[here, :] = jnp.where(first_core, dk, dv)
        send_at[here, :] = jnp.where(first_core, dv, dk).astype(BF16)

    place_out(key_parts[0][:TOK], value_parts[0][:TOK], keep_before, send_before, slice(0, TOK))
    place_out(
        key_parts[0][TOK:] + key_parts[1][:TOK],
        value_parts[0][TOK:] + value_parts[1][:TOK],
        keep,
        send,
        slice(0, TOK),
    )
    place_out(key_parts[1][TOK:], value_parts[1][TOK:], keep, send, slice(TOK, 2 * TOK))


def halo_body(place, keep_before, got_before, out):
    out[...] = (keep_before[...] + got_before[...].astype(F32)).astype(BF16)


def pair_body(place, dquery, keep, got, cos2, sin2, back, dout):
    dout[:, :HD] = dquery[...]
    for block in range(2):
        here = slice(block * TOK, (block + 1) * TOK)
        total = keep[here, :] + got[here, :].astype(F32)
        if block == 1:
            total += back[...].astype(F32)
        dout[here, HD:] = spin(total, cos2[here, :], sin2[here, :], -1.0).astype(BF16)


def dnormed_body(
    place, dout, s0, s1, other, s2, s3, s4, s5, s6, s7, own, send, send_sum, keep, keep_sum
):
    x, core = place[0], place[1]
    for rows, block, out, sums in (
        (other, 1 - core, send, send_sum),
        (own, core, keep, keep_sum),
    ):
        d = dout[pl.ds(pl.multiple_of(block * TOK, TOK), TOK), :]
        total = jnp.zeros((TOK, 1), F32)
        for (step, start, stop), slab in zip(PIECES, (s0, s1, s2, s3, s4, s5, s6, s7)):
            here = lax.rem(x + step, 4)
            part = mm(d, slab[...], 1, 1)
            total += jnp.sum(part * rows[here, :, start:stop].astype(F32), -1, keepdims=True)
            out[here, :, start:stop] = part.astype(BF16)
        sums[...] = jnp.broadcast_to(total, sums.ref.shape)
        out.leave()
        sums.leave()


def split_body(place, keep, got, keep_sum, got_sum, m1, m2, m3, own, own_sum):
    y = place[2]
    total = keep_sum[...] + got_sum[...]
    own_sum[...] = total
    coded = code(total)
    for step, message in enumerate((m1, m2, m3)):
        at = lax.rem(y + 4 - (step + 1), 4)
        message[:, :SLAB] = (keep[at].astype(F32) + got[at].astype(F32)).astype(BF16)
        message[:, SLAB:] = coded
        message.leave()
    own[...] = keep[y].astype(F32) + got[y].astype(F32)


def input_body(place, own, own_sum, m1, m2, m3, moved, inverse, gain, permute, out):
    total = own[...]
    sums = own_sum[:, :1]
    for message in (m1, m2, m3):
        total += message[:, :SLAB].astype(F32)
        sums += jnp.sum(message[:, SLAB:].astype(F32), -1, keepdims=True)
    inv = inverse[:, :1]
    y = place[2]
    rows = moved[y].astype(F32)
    grad = inv * (gain[pl.ds(y, 1), :] * total) - rows * ((inv * inv) * (sums * (1.0 / D)))
    out[0] = mm(grad.astype(BF16), permute[...], 1, 1).astype(BF16)


def weights_body(place, d0, columns, d1, d2, d3, squares, chunks):
    x, z = place[0], place[3]
    acc = mm(columns[x], d0[...])
    for step, d in ((1, d1), (2, d2), (3, d3)):
        acc += mm(columns[lax.rem(x + step, 4)], d[...])
    for chunk in range(8):
        chunks[chunk] = acc[chunk * 112 : (chunk + 1) * 112, :].astype(BF16)
    chunks.leave()
    row = lax.broadcasted_iota(jnp.int32, (8, 128), 0)
    squares[...] = jnp.where(row == z, jnp.sum(acc * acc), 0.0)


def local(inputs, w_query, w_key, w_value, norm_gain, attn_grad):
    x = lax.axis_index("x").astype(jnp.int32)
    core = lax.axis_index("core").astype(jnp.int32)
    y = lax.axis_index("tensor").astype(jnp.int32)
    z = lax.axis_index("dp").astype(jnp.int32)
    place = jnp.stack([x, core, y, z])
    first = core == 0

    low, high = w_query[:, :HD], w_query[:, HD:]
    mine = jnp.concatenate([jnp.where(first, low, high), jnp.where(first, w_key, w_value)], 1)
    theirs = jnp.concatenate([jnp.where(first, high, low), jnp.where(first, w_value, w_key)], 1)
    got = swap(theirs)
    block = jnp.concatenate([jnp.where(first, mine, got), jnp.where(first, got, mine)], 0)
    index = np.arange(SLAB)
    natural = (index % 112) // ROWS * 448 + index // 112 * ROWS + index % ROWS
    permute = (
        lax.broadcasted_iota(jnp.int32, (SLAB, SLAB), 0) == jnp.asarray(natural, jnp.int32)[None, :]
    ).astype(BF16)
    far = from_z(block, 4)
    up2, down2 = from_z(block, 2), from_z(block, -2)
    far, up2, down2, permute = lax.optimization_barrier((far, up2, down2, permute))
    both = jnp.concatenate([block, far], 0)
    up, down = from_z(both, 1), from_z(both, -1)

    normed, own_columns, *quarters, moved, inverse, gain = call(
        norm_body,
        [((4, TOK, SLAB), BF16), ((TOK, SLAB), BF16)]
        + [((TOK // 4, SLAB), BF16)] * 3
        + [((4, TOK, SLAB), BF16), ((TOK, 128), F32), ((4, SLAB), F32)],
        place,
        permute,
        norm_gain.reshape(4, SLAB),
        after(inputs[0], far),
        room=60,
    )
    top, bottom = call(
        stack_body,
        [((CUT, 2 * HD), BF16), ((SLAB - CUT, 2 * HD), BF16)],
        place,
        after(block, normed),
        far,
        up2,
        down2,
        up,
        down,
        scratch=[pltpu.VMEM((SLAB, 2 * HD), BF16)],
    )
    *quarters, _, _ = lax.optimization_barrier((*quarters, up, down))
    bundle = jnp.concatenate([from_x(one, step + 1) for step, one in enumerate(quarters)], 0)
    near = (from_x(top, 1), from_x(bottom, 1), from_x(top, -1), from_x(bottom, -1))
    near = lax.optimization_barrier(near)
    normed_other = swap(after(normed, *near))
    slabs = (top, bottom, *near, from_x(near[0], 1), from_x(near[3], -1))
    bundles = (bundle, from_y(bundle, 1), from_y(bundle, 2), from_y(bundle, 3))
    theirs = [swap(one) for one in bundles]
    theirs_own = swap(own_columns)
    (columns,) = call(
        columns_body,
        [((4, SLAB, 2 * TOK), BF16)],
        place,
        own_columns,
        theirs_own,
        *bundles,
        *theirs,
        scratch=[pltpu.VMEM((4, 2 * TOK, SLAB), BF16)],
    )

    cot_low, cot_high = attn_grad[0][:, :HD], attn_grad[0][:, HD:]
    cot_mine = jnp.where(first, cot_low, cot_high)
    cot_got = swap(jnp.where(first, cot_high, cot_low))
    cot = jnp.concatenate(
        [jnp.where(first, cot_mine, cot_got), jnp.where(first, cot_got, cot_mine)], 0
    )

    positions = x * (2 * TOK) + jnp.arange(2 * TOK, dtype=jnp.int32)
    frequency = ROPE_BASE ** (-2.0 * jnp.arange(HD // 2).astype(F32) / HD)
    phases = positions.astype(F32)[:, None] * frequency[None, :]
    cos, sin = jnp.cos(phases), jnp.sin(phases)
    cos2, sin2 = jnp.where(first, cos, 1.0), jnp.where(first, sin, 0.0)

    normed_other, cos, sin, cos2, sin2 = lax.optimization_barrier(
        (normed_other, cos, sin, cos2, sin2)
    )
    cot = after(cot, *bundles)
    total, last = call(
        project_body,
        [((2, TOK, 2 * HD), F32), ((2, TOK, SLAB), BF16)],
        place,
        normed,
        *slabs[:2],
        normed_other,
        *slabs[2:6],
    )
    pair, query = call(
        finish_body,
        [((2 * TOK, HD), BF16), ((2 * TOK, HD), BF16)],
        place,
        last,
        *slabs[6:],
        total,
        cos2,
        sin2,
        cos,
        sin,
    )
    pair_other = swap(pair)
    before = from_x(pair[TOK:], -1)
    before_other = swap(before)
    dquery, keep, keep_before, send, send_before = call(
        attend_body,
        [
            ((2 * TOK, HD), BF16),
            ((2 * TOK, HD), F32),
            ((TOK, HD), F32),
            ((2 * TOK, HD), BF16),
            ((TOK, HD), BF16),
        ],
        place,
        query,
        pair,
        pair_other,
        before,
        before_other,
        cot,
        cos,
        sin,
        scratch=[pltpu.VMEM((3 * TOK, HD), BF16), pltpu.VMEM((3 * TOK, HD), BF16)],
    )
    got_before = swap(send_before)
    got = after(swap(send), theirs_own, *theirs)
    (back,) = call(halo_body, [((TOK, HD), BF16)], place, keep_before, got_before)
    back = from_x(back, 1)
    (dout,) = call(
        pair_body, [((2 * TOK, 2 * HD), BF16)], place, dquery, keep, got, cos2, sin2, back
    )
    dout_1, dout_2, dout_3 = (from_x(dout, step) for step in (1, 2, 3))

    send_in, send_sum, keep_in, keep_sum = call(
        dnormed_body,
        [((4, TOK, SLAB), BF16), ((TOK, 128), F32)] * 2,
        place,
        dout,
        *slabs[:2],
        normed_other,
        *slabs[2:],
        normed,
    )
    got_in, got_sum = swap(send_in), swap(send_sum)
    *messages, own, own_sum = call(
        split_body,
        [((TOK, SLAB + 128), BF16)] * 3 + [((TOK, SLAB), F32), ((TOK, 128), F32)],
        place,
        keep_in,
        got_in,
        keep_sum,
        got_sum,
    )
    arrived = [from_y(message, step + 1) for step, message in enumerate(messages)]

    squares, chunks = call(
        weights_body,
        [((8, 128), F32), ((8, 112, 2 * HD), BF16)],
        place,
        dout,
        columns,
        dout_1,
        dout_2,
        dout_3,
    )
    chunks = lax.all_to_all(after(chunks, *arrived), "dp", split_axis=0, concat_axis=0, tiled=True)
    for axis in ("core", "x", "tensor"):
        squares = lax.optimization_barrier(lax.psum(squares, axis))
    (input_grad,) = call(
        input_body,
        [((1, TOK, SLAB), BF16)],
        place,
        own,
        own_sum,
        *arrived,
        moved,
        inverse,
        gain,
        permute,
        room=60,
    )
    chunks, squares = lax.optimization_barrier((chunks, squares))
    spread = jnp.broadcast_to(squares[None], (8, 8, 128))
    spread = lax.all_to_all(spread, "dp", split_axis=0, concat_axis=0, tiled=True)
    squares = jnp.sum(after(spread, input_grad), 0)
    upper, lower = chunks[:, :ROWS], chunks[:, ROWS:]
    rms = jnp.sqrt(squares[:, :1] * (1.0 / (D * (H + 2 * KVH) * HD)) + EPSILON)
    factor = (CLIP_BOUND / jnp.maximum(rms, CLIP_BOUND))[:, :, None]
    mine_out = jnp.where(first, upper, lower)
    got_out = swap(jnp.where(first, lower, upper))
    mine_out, got_out = (
        jnp.sum(one.astype(F32) * factor, 0) for one in (mine_out, got_out)
    )
    zero = jnp.where(first, mine_out, got_out)
    one = jnp.where(first, got_out, mine_out)
    grad_query = jnp.concatenate([zero[:, :HD], one[:, :HD]], 1)
    grad_key, grad_value = zero[:, HD:], one[:, HD:]
    return grad_query, grad_key, grad_value, input_grad


def solution(mesh):
    chips = Mesh(mesh.devices.reshape(4, 2, 4, 8), ("x", "core", "tensor", "dp"))
    seq = ("x", "core")
    weight = P((*seq, "dp"), "tensor")
    return jax.shard_map(
        local,
        mesh=chips,
        in_specs=(P("dp", seq, None), weight, weight, weight, P(), P("dp", seq, "tensor")),
        out_specs=(weight, weight, weight, P("dp", seq, "tensor")),
        check_vma=False,
    )
```

```python
import math

import jax
import jax.numpy as jnp
import numpy as np
from jax import lax
from jax.experimental import pallas as pl
from jax.experimental.pallas import tpu as pltpu
from jax.sharding import Mesh
from jax.sharding import PartitionSpec as P

D = 3584
H = 8
KVH = 4
HD = 256
WINDOW = 256
SLAB = D // 4
ROWS = 56
TOK = 256
CUT = 384

EPSILON = 1e-06
SOFTCAP = 50.0
CLIP_BOUND = 1.0
ROPE_BASE = 10000.0

F32 = jnp.float32
BF16 = jnp.bfloat16
ANY = pl.BlockSpec(memory_space=pl.ANY)
SMEM = pl.BlockSpec(memory_space=pltpu.SMEM)


class Arriving:
    def __init__(self, copy, ref):
        self.copy, self.ref, self.here = copy, ref, False

    def wait(self):
        if not self.here:
            self.copy.wait()
            self.here = True

    def __getitem__(self, at):
        self.wait()
        return self.ref[at]


class Leaving:
    def __init__(self, copy, ref):
        self.copy, self.ref, self.gone = copy, ref, False

    def __getitem__(self, at):
        return self.ref[at]

    def __setitem__(self, at, value):
        self.ref[at] = value

    def leave(self):
        if not self.gone:
            self.copy.start()
            self.gone = True


def call(body, outs, place, *operands, scratch=(), room=16):
    count, made = len(operands), len(outs)

    def kernel(place_ref, *refs):
        held = refs[count + made : 2 * (count + made)]
        sems = refs[2 * (count + made)]
        rest = refs[2 * (count + made) + 1 :]
        arriving = []
        for k in range(count):
            copy = pltpu.make_async_copy(refs[k], held[k], sems.at[k])
            copy.start()
            arriving.append(Arriving(copy, held[k]))
        leaving = []
        for k in range(count, count + made):
            copy = pltpu.make_async_copy(held[k], refs[k], sems.at[k])
            leaving.append(Leaving(copy, held[k]))
        body(place_ref, *arriving, *leaving, *rest)
        for one in leaving:
            one.leave()
        for one in arriving:
            one.wait()
        for one in leaving:
            one.copy.wait()

    return pl.pallas_call(
        kernel,
        out_shape=[jax.ShapeDtypeStruct(shape, kind) for shape, kind in outs],
        in_specs=[SMEM] + [ANY] * count,
        out_specs=[ANY] * made,
        scratch_shapes=[pltpu.VMEM(one.shape, one.dtype) for one in operands]
        + [pltpu.VMEM(shape, kind) for shape, kind in outs]
        + [pltpu.SemaphoreType.DMA((count + made,))]
        + list(scratch),
        compiler_params=pltpu.CompilerParams(vmem_limit_bytes=room * 1024 * 1024),
    )(place, *operands)


def swap(value):
    return lax.ppermute(value, "core", [(0, 1), (1, 0)])


def from_x(value, steps):
    return lax.ppermute(value, "x", [((i + steps) % 4, i) for i in range(4)])


def from_y(value, steps):
    return lax.ppermute(value, "tensor", [((i + steps) % 4, i) for i in range(4)])


def from_z(value, steps):
    return lax.ppermute(value, "dp", [((i + steps) % 8, i) for i in range(8)])


def after(value, *others):
    return lax.optimization_barrier((value, *others))[0]


def code(total):
    high = total.astype(BF16)
    rest = total - high.astype(F32)
    middle = rest.astype(BF16)
    low = (rest - middle.astype(F32)).astype(BF16)
    lane = lax.broadcasted_iota(jnp.int32, total.shape, 1)
    return jnp.where(
        lane == 0,
        high.astype(F32),
        jnp.where(
            lane == 1, middle.astype(F32), jnp.where(lane == 2, low.astype(F32), jnp.zeros_like(total))
        ),
    ).astype(BF16)


def mm(a, b, contract_a=1, contract_b=0):
    return lax.dot_general(
        a, b, (((contract_a,), (contract_b,)), ((), ())), preferred_element_type=F32
    )


def norm_body(place, permute, gain, inputs, normed, n0, q1, q2, q3, moved, inverse, moved_gain):
    x, y = place[0], place[2]
    wide = gain[...]
    high = wide.astype(BF16)
    middle = (wide - high.astype(F32)).astype(BF16)
    low = (wide - high.astype(F32) - middle.astype(F32)).astype(BF16)
    moved_gain[...] = mm(high, permute[...]) + mm(middle, permute[...]) + mm(low, permute[...])
    rows = inputs[...].astype(F32)
    inv = lax.rsqrt(jnp.sum(rows * rows, -1, keepdims=True) * (1.0 / D) + EPSILON)
    inverse[...] = jnp.broadcast_to(inv, inverse.ref.shape)
    for slab in range(4):
        part = mm(inputs[:, slab * SLAB : (slab + 1) * SLAB], permute[...])
        moved[slab] = part.astype(BF16)
        normed[slab] = (part * inv * moved_gain[slab : slab + 1, :]).astype(BF16)
    normed.leave()
    quarter = pl.ds(pl.multiple_of(y * 64, 64), 64)
    for step, one in ((1, q1), (2, q2), (3, q3)):
        one[...] = normed[lax.rem(x + 4 - step, 4), quarter, :]
        one.leave()
    n0[...] = normed[x]


def stack_body(place, own, far, up2, down2, up, down, top, bottom, whole):
    z = place[3]

    def put(step, rows):
        at = lax.rem(z + step, 8) * 112
        whole[pl.ds(pl.multiple_of(at, 16), 112), :] = rows

    put(0, own[...])
    put(4, far[...])
    put(2, up2[...])
    put(6, down2[...])
    put(1, up[:112, :])
    put(5, up[112:, :])
    put(7, down[:112, :])
    put(3, down[112:, :])
    top[...] = whole[:CUT, :]
    bottom[...] = whole[CUT:, :]


def columns_body(place, *refs):
    own, other, mine, theirs, whole, rows = refs[0], refs[1], refs[2:6], refs[6:10], refs[10], refs[11]
    x, core, y = place[0], place[1], place[2]
    for first, block, parts in ((own, core, mine), (other, 1 - core, theirs)):
        rows[x, pl.ds(pl.multiple_of(block * TOK, TOK), TOK), :] = first[...]
        for turn in range(4):
            at = pl.ds(pl.multiple_of(block * TOK + lax.rem(y + turn, 4) * 64, 64), 64)
            for step in range(1, 4):
                rows[lax.rem(x + step, 4), at, :] = parts[turn][(step - 1) * 64 : step * 64, :]
    for slab in range(4):
        whole[slab] = rows[slab].T


def spin(value, cosine, sine, direction):
    first, second = value[:, :128], value[:, 128:]
    return jnp.concatenate(
        [first * cosine - direction * second * sine, second * cosine + direction * first * sine], -1
    )


PIECES = tuple((step, start, stop) for step in (0, 1, 3, 2) for start, stop in ((0, CUT), (CUT, SLAB)))


def project_body(place, own, s0, s1, other, s2, s3, s4, s5, total, last):
    x = place[0]
    for turn, ((step, start, stop), slab) in enumerate(zip(PIECES, (s0, s1, s2, s3, s4, s5))):
        here = lax.rem(x + step, 4)
        for half, rows in enumerate((own, other)):
            part = mm(rows[here, :, start:stop], slab[...])
            total[half] = part if turn == 0 else total[half] + part
    for half, rows in enumerate((own, other)):
        last[half] = rows[lax.rem(x + 2, 4)]


def finish_body(place, last, s6, s7, total, cos2, sin2, cos, sin, pair, query):
    core = place[1]
    sums = []
    for half in range(2):
        sums.append(total[half] + mm(last[half, :, :CUT], s6[...]) + mm(last[half, :, CUT:], s7[...]))
    for half, block in ((0, core), (1, 1 - core)):
        at = pl.ds(pl.multiple_of(block * TOK, TOK), TOK)
        pair[at, :] = spin(sums[half][:, HD:], cos2[at, :], sin2[at, :], 1.0).astype(BF16)
    pair.leave()
    for half, block in ((0, core), (1, 1 - core)):
        at = pl.ds(pl.multiple_of(block * TOK, TOK), TOK)
        query[at, :] = spin(sums[half][:, :HD], cos[at, :], sin[at, :], 1.0).astype(BF16)


def attend_body(place, query, mine, theirs, mine_before, theirs_before, cot, cos, sin,
                dquery, keep, keep_before, send, send_before, keys, values):
    first_core = place[1] == 0
    for at, a, b in ((0, mine_before, theirs_before), (TOK, mine, theirs)):
        rows = a.ref.shape[0]
        keys[at : at + rows, :] = jnp.where(first_core, a[...], b[...])
        values[at : at + rows, :] = jnp.where(first_core, b[...], a[...])
    scale = 1.0 / math.sqrt(HD)
    q_at = lax.broadcasted_iota(jnp.int32, (TOK, 2 * TOK), 0)
    k_at = lax.broadcasted_iota(jnp.int32, (TOK, 2 * TOK), 1)
    band = (k_at <= q_at + TOK) & (k_at > q_at)
    key_parts = []
    value_parts = []
    for block in range(2):
        here = slice(block * TOK, (block + 1) * TOK)
        seen = slice(block * TOK, (block + 2) * TOK)
        q, g = query[here, :], cot[here, :]
        k, v = keys[seen, :], values[seen, :]
        squash = jnp.tanh(mm(q, k, 1, 1) * (scale / SOFTCAP))
        allowed = band
        if block == 0:
            allowed = band & ((k_at >= TOK) | (place[0] > 0))
        terms = jnp.where(allowed, jnp.exp(SOFTCAP * squash), 0.0)
        probs = terms / jnp.sum(terms, -1, keepdims=True)
        dprobs = mm(g, v, 1, 1)
        value_parts.append(mm(probs.astype(BF16), g, 0, 0))
        delta = jnp.sum(probs * dprobs, -1, keepdims=True)
        dlogits = (probs * (dprobs - delta) * (1.0 - squash * squash) * scale).astype(BF16)
        dq = mm(dlogits, k)
        dquery[here, :] = spin(dq, cos[here, :], sin[here, :], -1.0).astype(BF16)
        key_parts.append(mm(dlogits, q, 0, 0))

    def place_out(dk, dv, keep_at, send_at, here):
        keep_at[here, :] = jnp.where(first_core, dk, dv)
        send_at[here, :] = jnp.where(first_core, dv, dk).astype(BF16)

    place_out(key_parts[0][:TOK], value_parts[0][:TOK], keep_before, send_before, slice(0, TOK))
    place_out(
        key_parts[0][TOK:] + key_parts[1][:TOK],
        value_parts[0][TOK:] + value_parts[1][:TOK],
        keep,
        send,
        slice(0, TOK),
    )
    place_out(key_parts[1][TOK:], value_parts[1][TOK:], keep, send, slice(TOK, 2 * TOK))


def halo_body(place, keep_before, got_before, out):
    out[...] = (keep_before[...] + got_before[...].astype(F32)).astype(BF16)


def pair_body(place, dquery, keep, got, cos2, sin2, back, dout):
    dout[:, :HD] = dquery[...]
    for block in range(2):
        here = slice(block * TOK, (block + 1) * TOK)
        total = keep[here, :] + got[here, :].astype(F32)
        if block == 1:
            total += back[...].astype(F32)
        dout[here, HD:] = spin(total, cos2[here, :], sin2[here, :], -1.0).astype(BF16)


def dnormed_body(
    place, dout, s0, s1, other, s2, s3, s4, s5, s6, s7, own, send, send_sum, keep, keep_sum
):
    x, core = place[0], place[1]
    for rows, block, out, sums in (
        (other, 1 - core, send, send_sum),
        (own, core, keep, keep_sum),
    ):
        d = dout[pl.ds(pl.multiple_of(block * TOK, TOK), TOK), :]
        total = jnp.zeros((TOK, 1), F32)
        for (step, start, stop), slab in zip(PIECES, (s0, s1, s2, s3, s4, s5, s6, s7)):
            here = lax.rem(x + step, 4)
            part = mm(d, slab[...], 1, 1)
            total += jnp.sum(part * rows[here, :, start:stop].astype(F32), -1, keepdims=True)
            out[here, :, start:stop] = part.astype(BF16)
        sums[...] = jnp.broadcast_to(total, sums.ref.shape)
        out.leave()
        sums.leave()


def split_body(place, keep, got, keep_sum, got_sum, m1, m2, m3, own, own_sum):
    y = place[2]
    total = keep_sum[...] + got_sum[...]
    own_sum[...] = total
    coded = code(total)
    for step, message in enumerate((m1, m2, m3)):
        at = lax.rem(y + 4 - (step + 1), 4)
        message[:, :SLAB] = (keep[at].astype(F32) + got[at].astype(F32)).astype(BF16)
        message[:, SLAB:] = coded
        message.leave()
    own[...] = keep[y].astype(F32) + got[y].astype(F32)


def input_body(place, own, own_sum, m1, m2, m3, moved, inverse, gain, permute, out):
    total = own[...]
    sums = own_sum[:, :1]
    for message in (m1, m2, m3):
        total += message[:, :SLAB].astype(F32)
        sums += jnp.sum(message[:, SLAB:].astype(F32), -1, keepdims=True)
    inv = inverse[:, :1]
    y = place[2]
    rows = moved[y].astype(F32)
    grad = inv * (gain[pl.ds(y, 1), :] * total) - rows * ((inv * inv) * (sums * (1.0 / D)))
    out[0] = mm(grad.astype(BF16), permute[...], 1, 1).astype(BF16)


def weights_body(place, d0, columns, d1, d3, d2a, d2b, squares, chunks):
    x, z = place[0], place[3]
    acc = mm(columns[x], d0[...])
    for step, d in ((1, d1), (3, d3)):
        acc += mm(columns[lax.rem(x + step, 4)], d[...])
    far = lax.rem(x + 2, 4)
    acc += mm(columns[far, :, :TOK], d2a[...]) + mm(columns[far, :, TOK:], d2b[...])
    for chunk in range(8):
        chunks[chunk] = acc[chunk * 112 : (chunk + 1) * 112, :].astype(BF16)
    chunks.leave()
    row = lax.broadcasted_iota(jnp.int32, (8, 128), 0)
    squares[...] = jnp.where(row == z, jnp.sum(acc * acc), 0.0)


def local(inputs, w_query, w_key, w_value, norm_gain, attn_grad):
    x = lax.axis_index("x").astype(jnp.int32)
    core = lax.axis_index("core").astype(jnp.int32)
    y = lax.axis_index("tensor").astype(jnp.int32)
    z = lax.axis_index("dp").astype(jnp.int32)
    place = jnp.stack([x, core, y, z])
    first = core == 0

    low, high = w_query[:, :HD], w_query[:, HD:]
    mine = jnp.concatenate([jnp.where(first, low, high), jnp.where(first, w_key, w_value)], 1)
    theirs = jnp.concatenate([jnp.where(first, high, low), jnp.where(first, w_value, w_key)], 1)
    got = swap(theirs)
    block = jnp.concatenate([jnp.where(first, mine, got), jnp.where(first, got, mine)], 0)
    index = np.arange(SLAB)
    natural = (index % 112) // ROWS * 448 + index // 112 * ROWS + index % ROWS
    permute = (
        lax.broadcasted_iota(jnp.int32, (SLAB, SLAB), 0) == jnp.asarray(natural, jnp.int32)[None, :]
    ).astype(BF16)
    cot_low, cot_high = attn_grad[0][:, :HD], attn_grad[0][:, HD:]
    cot_mine = jnp.where(first, cot_low, cot_high)
    cot_got = swap(jnp.where(first, cot_high, cot_low))
    gain_rows = norm_gain.reshape(4, SLAB)
    far = from_z(block, 4)
    up2, down2 = from_z(block, 2), from_z(block, -2)
    far, up2, down2, permute, cot_got, gain_rows, place = lax.optimization_barrier(
        (far, up2, down2, permute, cot_got, gain_rows, place)
    )
    both = jnp.concatenate([block, far], 0)
    up, down = from_z(both, 1), from_z(both, -1)

    normed, own_columns, *quarters, moved, inverse, gain = call(
        norm_body,
        [((4, TOK, SLAB), BF16), ((TOK, SLAB), BF16)]
        + [((TOK // 4, SLAB), BF16)] * 3
        + [((4, TOK, SLAB), BF16), ((TOK, 128), F32), ((4, SLAB), F32)],
        place,
        permute,
        gain_rows,
        after(inputs[0], far),
        room=60,
    )
    top, bottom = call(
        stack_body,
        [((CUT, 2 * HD), BF16), ((SLAB - CUT, 2 * HD), BF16)],
        place,
        after(block, normed),
        far,
        up2,
        down2,
        up,
        down,
        scratch=[pltpu.VMEM((SLAB, 2 * HD), BF16)],
    )
    *quarters, _, _ = lax.optimization_barrier((*quarters, up, down))
    quarters = [from_x(one, step + 1) for step, one in enumerate(quarters)]
    near = (from_x(top, 1), from_x(bottom, 1), from_x(top, -1), from_x(bottom, -1))
    near = lax.optimization_barrier(near)
    normed_other = swap(after(normed, *near))
    *quarters, normed_other = lax.optimization_barrier((*quarters, normed_other))
    bundle = jnp.concatenate(quarters, 0)
    slabs = (top, bottom, *near, from_x(near[0], 1), from_x(near[3], -1))
    bundles = (bundle, from_y(bundle, 1), from_y(bundle, 2), from_y(bundle, 3))
    theirs = [swap(one) for one in bundles]
    theirs_own = swap(own_columns)
    (columns,) = call(
        columns_body,
        [((4, SLAB, 2 * TOK), BF16)],
        place,
        own_columns,
        theirs_own,
        *bundles,
        *theirs,
        scratch=[pltpu.VMEM((4, 2 * TOK, SLAB), BF16)],
    )

    cot = jnp.concatenate(
        [jnp.where(first, cot_mine, cot_got), jnp.where(first, cot_got, cot_mine)], 0
    )

    positions = x * (2 * TOK) + jnp.arange(2 * TOK, dtype=jnp.int32)
    frequency = ROPE_BASE ** (-2.0 * jnp.arange(HD // 2).astype(F32) / HD)
    phases = positions.astype(F32)[:, None] * frequency[None, :]
    cos, sin = jnp.cos(phases), jnp.sin(phases)
    cos2, sin2 = jnp.where(first, cos, 1.0), jnp.where(first, sin, 0.0)

    normed_other, cos, sin, cos2, sin2 = lax.optimization_barrier(
        (normed_other, cos, sin, cos2, sin2)
    )
    cot = after(cot, *bundles)
    total, last = call(
        project_body,
        [((2, TOK, 2 * HD), F32), ((2, TOK, SLAB), BF16)],
        place,
        normed,
        *slabs[:2],
        normed_other,
        *slabs[2:6],
    )
    pair, query = call(
        finish_body,
        [((2 * TOK, HD), BF16), ((2 * TOK, HD), BF16)],
        place,
        last,
        *slabs[6:],
        after(total, bundles[1], bundles[3]),
        cos2,
        sin2,
        cos,
        sin,
    )
    pair_other = swap(pair)
    before = from_x(pair[TOK:], -1)
    before_other = swap(before)
    dquery, keep, keep_before, send, send_before = call(
        attend_body,
        [
            ((2 * TOK, HD), BF16),
            ((2 * TOK, HD), F32),
            ((TOK, HD), F32),
            ((2 * TOK, HD), BF16),
            ((TOK, HD), BF16),
        ],
        place,
        query,
        pair,
        pair_other,
        before,
        before_other,
        cot,
        cos,
        sin,
        scratch=[pltpu.VMEM((3 * TOK, HD), BF16), pltpu.VMEM((3 * TOK, HD), BF16)],
    )
    got_before = swap(send_before)
    got = after(swap(send), theirs_own, *theirs)
    (back,) = call(halo_body, [((TOK, HD), BF16)], place, keep_before, got_before)
    back = from_x(back, 1)
    (dout,) = call(
        pair_body, [((2 * TOK, 2 * HD), BF16)], place, dquery, keep, got, cos2, sin2, back
    )
    dout_1, dout_3 = lax.optimization_barrier((from_x(dout, 1), from_x(dout, 3)))
    dout_2 = (from_x(dout_1[:TOK], 1), from_x(dout_3[TOK:], -1))

    send_in, send_sum, keep_in, keep_sum = call(
        dnormed_body,
        [((4, TOK, SLAB), BF16), ((TOK, 128), F32)] * 2,
        place,
        dout,
        *slabs[:2],
        normed_other,
        *slabs[2:],
        normed,
    )
    got_in, got_sum = swap(send_in), swap(send_sum)
    *messages, own, own_sum = call(
        split_body,
        [((TOK, SLAB + 128), BF16)] * 3 + [((TOK, SLAB), F32), ((TOK, 128), F32)],
        place,
        keep_in,
        got_in,
        keep_sum,
        got_sum,
    )
    arrived = [from_y(message, step + 1) for step, message in enumerate(messages)]

    squares, chunks = call(
        weights_body,
        [((8, 128), F32), ((8, 112, 2 * HD), BF16)],
        place,
        dout,
        columns,
        dout_1,
        dout_3,
        *dout_2,
    )
    chunks = lax.all_to_all(after(chunks, *arrived), "dp", split_axis=0, concat_axis=0, tiled=True)
    for axis in ("core", "x", "tensor"):
        squares = lax.optimization_barrier(lax.psum(squares, axis))
    (input_grad,) = call(
        input_body,
        [((1, TOK, SLAB), BF16)],
        place,
        own,
        own_sum,
        *arrived,
        moved,
        inverse,
        gain,
        permute,
        room=60,
    )
    chunks, squares = lax.optimization_barrier((chunks, squares))
    spread = jnp.broadcast_to(squares[None], (8, 8, 128))
    spread = lax.all_to_all(spread, "dp", split_axis=0, concat_axis=0, tiled=True)
    squares = jnp.sum(after(spread, input_grad), 0)
    upper, lower = chunks[:, :ROWS], chunks[:, ROWS:]
    rms = jnp.sqrt(squares[:, :1] * (1.0 / (D * (H + 2 * KVH) * HD)) + EPSILON)
    factor = (CLIP_BOUND / jnp.maximum(rms, CLIP_BOUND))[:, :, None]
    mine_out = jnp.where(first, upper, lower)
    got_out = swap(jnp.where(first, lower, upper))
    mine_out, got_out = (
        jnp.sum(one.astype(F32) * factor, 0) for one in (mine_out, got_out)
    )
    zero = jnp.where(first, mine_out, got_out)
    one = jnp.where(first, got_out, mine_out)
    grad_query = jnp.concatenate([zero[:, :HD], one[:, :HD]], 1)
    grad_key, grad_value = zero[:, HD:], one[:, HD:]
    return grad_query, grad_key, grad_value, input_grad


def solution(mesh):
    chips = Mesh(mesh.devices.reshape(4, 2, 4, 8), ("x", "core", "tensor", "dp"))
    seq = ("x", "core")
    weight = P((*seq, "dp"), "tensor")
    return jax.shard_map(
        local,
        mesh=chips,
        in_specs=(P("dp", seq, None), weight, weight, weight, P(), P("dp", seq, "tensor")),
        out_specs=(weight, weight, weight, P("dp", seq, "tensor")),
        check_vma=False,
    )
```

```python
import math

import jax
import jax.numpy as jnp
import numpy as np
from jax import lax
from jax.experimental import pallas as pl
from jax.experimental.pallas import tpu as pltpu
from jax.sharding import Mesh
from jax.sharding import PartitionSpec as P

D = 3584
H = 8
KVH = 4
HD = 256
WINDOW = 256
SLAB = D // 4
ROWS = 56
TOK = 256
CUT = 384

EPSILON = 1e-06
SOFTCAP = 50.0
CLIP_BOUND = 1.0
ROPE_BASE = 10000.0

F32 = jnp.float32
BF16 = jnp.bfloat16
ANY = pl.BlockSpec(memory_space=pl.ANY)
SMEM = pl.BlockSpec(memory_space=pltpu.SMEM)


class Arriving:
    def __init__(self, copy, ref):
        self.copy, self.ref, self.here = copy, ref, False

    def wait(self):
        if not self.here:
            self.copy.wait()
            self.here = True

    def __getitem__(self, at):
        self.wait()
        return self.ref[at]


class Leaving:
    def __init__(self, copy, ref):
        self.copy, self.ref, self.gone = copy, ref, False

    def __getitem__(self, at):
        return self.ref[at]

    def __setitem__(self, at, value):
        self.ref[at] = value

    def leave(self):
        if not self.gone:
            self.copy.start()
            self.gone = True


def call(body, outs, place, *operands, scratch=(), room=16):
    count, made = len(operands), len(outs)

    def kernel(place_ref, *refs):
        held = refs[count + made : 2 * (count + made)]
        sems = refs[2 * (count + made)]
        rest = refs[2 * (count + made) + 1 :]
        arriving = []
        for k in range(count):
            copy = pltpu.make_async_copy(refs[k], held[k], sems.at[k])
            copy.start()
            arriving.append(Arriving(copy, held[k]))
        leaving = []
        for k in range(count, count + made):
            copy = pltpu.make_async_copy(held[k], refs[k], sems.at[k])
            leaving.append(Leaving(copy, held[k]))
        body(place_ref, *arriving, *leaving, *rest)
        for one in leaving:
            one.leave()
        for one in arriving:
            one.wait()
        for one in leaving:
            one.copy.wait()

    return pl.pallas_call(
        kernel,
        out_shape=[jax.ShapeDtypeStruct(shape, kind) for shape, kind in outs],
        in_specs=[SMEM] + [ANY] * count,
        out_specs=[ANY] * made,
        scratch_shapes=[pltpu.VMEM(one.shape, one.dtype) for one in operands]
        + [pltpu.VMEM(shape, kind) for shape, kind in outs]
        + [pltpu.SemaphoreType.DMA((count + made,))]
        + list(scratch),
        compiler_params=pltpu.CompilerParams(vmem_limit_bytes=room * 1024 * 1024),
    )(place, *operands)


def swap(value):
    return lax.ppermute(value, "core", [(0, 1), (1, 0)])


def from_x(value, steps):
    return lax.ppermute(value, "x", [((i + steps) % 4, i) for i in range(4)])


def from_y(value, steps):
    return lax.ppermute(value, "tensor", [((i + steps) % 4, i) for i in range(4)])


def from_z(value, steps):
    return lax.ppermute(value, "dp", [((i + steps) % 8, i) for i in range(8)])


def after(value, *others):
    return lax.optimization_barrier((value, *others))[0]


def code(total):
    high = total.astype(BF16)
    rest = total - high.astype(F32)
    middle = rest.astype(BF16)
    low = (rest - middle.astype(F32)).astype(BF16)
    lane = lax.broadcasted_iota(jnp.int32, total.shape, 1)
    return jnp.where(
        lane == 0,
        high.astype(F32),
        jnp.where(
            lane == 1, middle.astype(F32), jnp.where(lane == 2, low.astype(F32), jnp.zeros_like(total))
        ),
    ).astype(BF16)


def mm(a, b, contract_a=1, contract_b=0):
    return lax.dot_general(
        a, b, (((contract_a,), (contract_b,)), ((), ())), preferred_element_type=F32
    )


def norm_body(place, permute, gain, inputs, normed, n0, q1, q2, q3, moved, inverse, moved_gain):
    x, y = place[0], place[2]
    wide = gain[...]
    high = wide.astype(BF16)
    middle = (wide - high.astype(F32)).astype(BF16)
    low = (wide - high.astype(F32) - middle.astype(F32)).astype(BF16)
    moved_gain[...] = mm(high, permute[...]) + mm(middle, permute[...]) + mm(low, permute[...])
    rows = inputs[...].astype(F32)
    inv = lax.rsqrt(jnp.sum(rows * rows, -1, keepdims=True) * (1.0 / D) + EPSILON)
    inverse[...] = jnp.broadcast_to(inv, inverse.ref.shape)
    for slab in range(4):
        part = mm(inputs[:, slab * SLAB : (slab + 1) * SLAB], permute[...])
        moved[slab] = part.astype(BF16)
        normed[slab] = (part * inv * moved_gain[slab : slab + 1, :]).astype(BF16)
    normed.leave()
    quarter = pl.ds(pl.multiple_of(y * 64, 64), 64)
    for step, one in ((1, q1), (2, q2), (3, q3)):
        one[...] = normed[lax.rem(x + 4 - step, 4), quarter, :]
        one.leave()
    n0[...] = normed[x]


def stack_body(place, own, far, up2, down2, up, down, top, bottom, whole):
    z = place[3]

    def put(step, rows):
        at = lax.rem(z + step, 8) * 112
        whole[pl.ds(pl.multiple_of(at, 16), 112), :] = rows

    put(0, own[...])
    put(4, far[...])
    put(2, up2[...])
    put(6, down2[...])
    put(1, up[:112, :])
    put(5, up[112:, :])
    put(7, down[:112, :])
    put(3, down[112:, :])
    top[...] = whole[:CUT, :]
    bottom[...] = whole[CUT:, :]


def columns_body(place, *refs):
    own, other, mine, theirs, whole, rows = refs[0], refs[1], refs[2:6], refs[6:10], refs[10], refs[11]
    x, core, y = place[0], place[1], place[2]
    for first, block, parts in ((own, core, mine), (other, 1 - core, theirs)):
        rows[x, pl.ds(pl.multiple_of(block * TOK, TOK), TOK), :] = first[...]
        for turn in range(4):
            at = pl.ds(pl.multiple_of(block * TOK + lax.rem(y + turn, 4) * 64, 64), 64)
            for step in range(1, 4):
                rows[lax.rem(x + step, 4), at, :] = parts[turn][(step - 1) * 64 : step * 64, :]
    for slab in range(4):
        whole[slab] = rows[slab].T


def spin(value, cosine, sine, direction):
    first, second = value[:, :128], value[:, 128:]
    return jnp.concatenate(
        [first * cosine - direction * second * sine, second * cosine + direction * first * sine], -1
    )


PIECES = tuple((step, start, stop) for step in (0, 1, 3, 2) for start, stop in ((0, CUT), (CUT, SLAB)))


def project_body(place, own, s0, s1, other, s2, s3, s4, s5, total, last):
    x = place[0]
    for turn, ((step, start, stop), slab) in enumerate(zip(PIECES, (s0, s1, s2, s3, s4, s5))):
        here = lax.rem(x + step, 4)
        for half, rows in enumerate((own, other)):
            part = mm(rows[here, :, start:stop], slab[...])
            total[half] = part if turn == 0 else total[half] + part
    for half, rows in enumerate((own, other)):
        last[half] = rows[lax.rem(x + 2, 4)]


def finish_body(place, last, s6, s7, total, cos2, sin2, cos, sin, pair, query):
    core = place[1]
    sums = []
    for half in range(2):
        sums.append(total[half] + mm(last[half, :, :CUT], s6[...]) + mm(last[half, :, CUT:], s7[...]))
    for half, block in ((0, core), (1, 1 - core)):
        at = pl.ds(pl.multiple_of(block * TOK, TOK), TOK)
        pair[at, :] = spin(sums[half][:, HD:], cos2[at, :], sin2[at, :], 1.0).astype(BF16)
    pair.leave()
    for half, block in ((0, core), (1, 1 - core)):
        at = pl.ds(pl.multiple_of(block * TOK, TOK), TOK)
        query[at, :] = spin(sums[half][:, :HD], cos[at, :], sin[at, :], 1.0).astype(BF16)


def attend_body(place, query, mine, theirs, mine_before, theirs_before, cot, cos, sin,
                dquery, keep, keep_before, send, send_before, keys, values):
    first_core = place[1] == 0
    for at, a, b in ((0, mine_before, theirs_before), (TOK, mine, theirs)):
        rows = a.ref.shape[0]
        keys[at : at + rows, :] = jnp.where(first_core, a[...], b[...])
        values[at : at + rows, :] = jnp.where(first_core, b[...], a[...])
    scale = 1.0 / math.sqrt(HD)
    q_at = lax.broadcasted_iota(jnp.int32, (TOK, 2 * TOK), 0)
    k_at = lax.broadcasted_iota(jnp.int32, (TOK, 2 * TOK), 1)
    band = (k_at <= q_at + TOK) & (k_at > q_at)
    key_parts = []
    value_parts = []
    for block in range(2):
        here = slice(block * TOK, (block + 1) * TOK)
        seen = slice(block * TOK, (block + 2) * TOK)
        q, g = query[here, :], cot[here, :]
        k, v = keys[seen, :], values[seen, :]
        squash = jnp.tanh(mm(q, k, 1, 1) * (scale / SOFTCAP))
        allowed = band
        if block == 0:
            allowed = band & ((k_at >= TOK) | (place[0] > 0))
        terms = jnp.where(allowed, jnp.exp(SOFTCAP * squash), 0.0)
        probs = terms / jnp.sum(terms, -1, keepdims=True)
        dprobs = mm(g, v, 1, 1)
        value_parts.append(mm(probs.astype(BF16), g, 0, 0))
        delta = jnp.sum(probs * dprobs, -1, keepdims=True)
        dlogits = (probs * (dprobs - delta) * (1.0 - squash * squash) * scale).astype(BF16)
        dq = mm(dlogits, k)
        dquery[here, :] = spin(dq, cos[here, :], sin[here, :], -1.0).astype(BF16)
        key_parts.append(mm(dlogits, q, 0, 0))

    def place_out(dk, dv, keep_at, send_at, here):
        keep_at[here, :] = jnp.where(first_core, dk, dv)
        send_at[here, :] = jnp.where(first_core, dv, dk).astype(BF16)

    place_out(key_parts[0][:TOK], value_parts[0][:TOK], keep_before, send_before, slice(0, TOK))
    place_out(
        key_parts[0][TOK:] + key_parts[1][:TOK],
        value_parts[0][TOK:] + value_parts[1][:TOK],
        keep,
        send,
        slice(0, TOK),
    )
    place_out(key_parts[1][TOK:], value_parts[1][TOK:], keep, send, slice(TOK, 2 * TOK))


def halo_body(place, keep_before, got_before, out):
    out[...] = (keep_before[...] + got_before[...].astype(F32)).astype(BF16)


def pair_body(place, dquery, keep, got, cos2, sin2, back, dout):
    dout[:, :HD] = dquery[...]
    for block in range(2):
        here = slice(block * TOK, (block + 1) * TOK)
        total = keep[here, :] + got[here, :].astype(F32)
        if block == 1:
            total += back[...].astype(F32)
        dout[here, HD:] = spin(total, cos2[here, :], sin2[here, :], -1.0).astype(BF16)


def dnormed_body(
    place, dout, s0, s1, other, s2, s3, s4, s5, s6, s7, own, send, send_sum, keep, keep_sum
):
    x, core = place[0], place[1]
    for rows, block, out, sums in (
        (other, 1 - core, send, send_sum),
        (own, core, keep, keep_sum),
    ):
        d = dout[pl.ds(pl.multiple_of(block * TOK, TOK), TOK), :]
        total = jnp.zeros((TOK, 1), F32)
        for (step, start, stop), slab in zip(PIECES, (s0, s1, s2, s3, s4, s5, s6, s7)):
            here = lax.rem(x + step, 4)
            part = mm(d, slab[...], 1, 1)
            total += jnp.sum(part * rows[here, :, start:stop].astype(F32), -1, keepdims=True)
            out[here, :, start:stop] = part.astype(BF16)
        sums[...] = jnp.broadcast_to(total, sums.ref.shape)
        out.leave()
        sums.leave()


def split_body(place, keep, got, keep_sum, got_sum, m1, m2, m3, own, own_sum):
    y = place[2]
    total = keep_sum[...] + got_sum[...]
    own_sum[...] = total
    coded = code(total)
    for step, message in enumerate((m1, m2, m3)):
        at = lax.rem(y + 4 - (step + 1), 4)
        message[:, :SLAB] = (keep[at].astype(F32) + got[at].astype(F32)).astype(BF16)
        message[:, SLAB:] = coded
        message.leave()
    own[...] = keep[y].astype(F32) + got[y].astype(F32)


def input_body(place, own, own_sum, m1, m2, m3, moved, inverse, gain, permute, out):
    total = own[...]
    sums = own_sum[:, :1]
    for message in (m1, m2, m3):
        total += message[:, :SLAB].astype(F32)
        sums += jnp.sum(message[:, SLAB:].astype(F32), -1, keepdims=True)
    inv = inverse[:, :1]
    y = place[2]
    rows = moved[y].astype(F32)
    grad = inv * (gain[pl.ds(y, 1), :] * total) - rows * ((inv * inv) * (sums * (1.0 / D)))
    out[0] = mm(grad.astype(BF16), permute[...], 1, 1).astype(BF16)


def weights_body(place, d0, columns, d1, d3, d2a, d2b, squares, chunks):
    x, z = place[0], place[3]
    acc = mm(columns[x], d0[...])
    for step, d in ((1, d1), (3, d3)):
        acc += mm(columns[lax.rem(x + step, 4)], d[...])
    far = lax.rem(x + 2, 4)
    acc += mm(columns[far, :, :TOK], d2a[...]) + mm(columns[far, :, TOK:], d2b[...])
    for chunk in range(8):
        chunks[chunk] = acc[chunk * 112 : (chunk + 1) * 112, :].astype(BF16)
    chunks.leave()
    row = lax.broadcasted_iota(jnp.int32, (8, 128), 0)
    squares[...] = jnp.where(row == z, jnp.sum(acc * acc), 0.0)


def local(inputs, w_query, w_key, w_value, norm_gain, attn_grad):
    x = lax.axis_index("x").astype(jnp.int32)
    core = lax.axis_index("core").astype(jnp.int32)
    y = lax.axis_index("tensor").astype(jnp.int32)
    z = lax.axis_index("dp").astype(jnp.int32)
    place = jnp.stack([x, core, y, z])
    first = core == 0

    low, high = w_query[:, :HD], w_query[:, HD:]
    mine = jnp.concatenate([jnp.where(first, low, high), jnp.where(first, w_key, w_value)], 1)
    theirs = jnp.concatenate([jnp.where(first, high, low), jnp.where(first, w_value, w_key)], 1)
    got = swap(theirs)
    block = jnp.concatenate([jnp.where(first, mine, got), jnp.where(first, got, mine)], 0)
    index = np.arange(SLAB)
    natural = (index % 112) // ROWS * 448 + index // 112 * ROWS + index % ROWS
    permute = (
        lax.broadcasted_iota(jnp.int32, (SLAB, SLAB), 0) == jnp.asarray(natural, jnp.int32)[None, :]
    ).astype(BF16)
    cot_low, cot_high = attn_grad[0][:, :HD], attn_grad[0][:, HD:]
    cot_mine = jnp.where(first, cot_low, cot_high)
    cot_got = swap(jnp.where(first, cot_high, cot_low))
    gain_rows = norm_gain.reshape(4, SLAB)
    far = from_z(block, 4)
    up2, down2 = from_z(block, 2), from_z(block, -2)
    far, up2, down2, permute, cot_got, gain_rows, place = lax.optimization_barrier(
        (far, up2, down2, permute, cot_got, gain_rows, place)
    )
    both = jnp.concatenate([block, far], 0)
    up, down = from_z(both, 1), from_z(both, -1)

    normed, own_columns, *quarters, moved, inverse, gain = call(
        norm_body,
        [((4, TOK, SLAB), BF16), ((TOK, SLAB), BF16)]
        + [((TOK // 4, SLAB), BF16)] * 3
        + [((4, TOK, SLAB), BF16), ((TOK, 128), F32), ((4, SLAB), F32)],
        place,
        permute,
        gain_rows,
        after(inputs[0], far),
        room=60,
    )
    top, bottom = call(
        stack_body,
        [((CUT, 2 * HD), BF16), ((SLAB - CUT, 2 * HD), BF16)],
        place,
        after(block, normed),
        far,
        up2,
        down2,
        up,
        down,
        scratch=[pltpu.VMEM((SLAB, 2 * HD), BF16)],
    )
    *quarters, _, _ = lax.optimization_barrier((*quarters, up, down))
    quarters = [from_x(one, step + 1) for step, one in enumerate(quarters)]
    near = (from_x(top, 1), from_x(bottom, 1), from_x(top, -1), from_x(bottom, -1))
    near = lax.optimization_barrier(near)
    normed_other = swap(after(normed, *near))
    *quarters, normed_other = lax.optimization_barrier((*quarters, normed_other))
    bundle = jnp.concatenate(quarters, 0)
    slabs = (top, bottom, *near, from_x(near[0], 1), from_x(near[3], -1))
    bundles = (bundle, from_y(bundle, 1), from_y(bundle, 2), from_y(bundle, 3))
    theirs = [swap(one) for one in bundles]
    theirs_own = swap(own_columns)
    (columns,) = call(
        columns_body,
        [((4, SLAB, 2 * TOK), BF16)],
        place,
        own_columns,
        theirs_own,
        *bundles,
        *theirs,
        scratch=[pltpu.VMEM((4, 2 * TOK, SLAB), BF16)],
    )

    cot = jnp.concatenate(
        [jnp.where(first, cot_mine, cot_got), jnp.where(first, cot_got, cot_mine)], 0
    )

    positions = x * (2 * TOK) + jnp.arange(2 * TOK, dtype=jnp.int32)
    frequency = ROPE_BASE ** (-2.0 * jnp.arange(HD // 2).astype(F32) / HD)
    phases = positions.astype(F32)[:, None] * frequency[None, :]
    cos, sin = jnp.cos(phases), jnp.sin(phases)
    cos2, sin2 = jnp.where(first, cos, 1.0), jnp.where(first, sin, 0.0)

    normed_other, cos, sin, cos2, sin2 = lax.optimization_barrier(
        (normed_other, cos, sin, cos2, sin2)
    )
    cot = after(cot, bundles[1], bundles[3])
    total, last = call(
        project_body,
        [((2, TOK, 2 * HD), F32), ((2, TOK, SLAB), BF16)],
        place,
        normed,
        *slabs[:2],
        normed_other,
        *slabs[2:6],
    )
    pair, query = call(
        finish_body,
        [((2 * TOK, HD), BF16), ((2 * TOK, HD), BF16)],
        place,
        last,
        *slabs[6:],
        total,
        cos2,
        sin2,
        cos,
        sin,
    )
    pair_other = swap(pair)
    before = from_x(pair[TOK:], -1)
    before_other = swap(before)
    dquery, keep, keep_before, send, send_before = call(
        attend_body,
        [
            ((2 * TOK, HD), BF16),
            ((2 * TOK, HD), F32),
            ((TOK, HD), F32),
            ((2 * TOK, HD), BF16),
            ((TOK, HD), BF16),
        ],
        place,
        query,
        pair,
        pair_other,
        before,
        before_other,
        cot,
        cos,
        sin,
        scratch=[pltpu.VMEM((3 * TOK, HD), BF16), pltpu.VMEM((3 * TOK, HD), BF16)],
    )
    got_before = swap(send_before)
    got = after(swap(send), theirs_own, *theirs)
    (back,) = call(halo_body, [((TOK, HD), BF16)], place, keep_before, got_before)
    back = from_x(back, 1)
    (dout,) = call(
        pair_body, [((2 * TOK, 2 * HD), BF16)], place, dquery, keep, got, cos2, sin2, back
    )
    dout_1, dout_3 = lax.optimization_barrier((from_x(dout, 1), from_x(dout, 3)))
    dout_2 = (from_x(dout_1[:TOK], 1), from_x(dout_3[TOK:], -1))

    send_in, send_sum, keep_in, keep_sum = call(
        dnormed_body,
        [((4, TOK, SLAB), BF16), ((TOK, 128), F32)] * 2,
        place,
        dout,
        *slabs[:2],
        normed_other,
        *slabs[2:],
        normed,
    )
    got_in, got_sum = swap(send_in), swap(send_sum)
    *messages, own, own_sum = call(
        split_body,
        [((TOK, SLAB + 128), BF16)] * 3 + [((TOK, SLAB), F32), ((TOK, 128), F32)],
        place,
        keep_in,
        got_in,
        keep_sum,
        got_sum,
    )
    arrived = [from_y(message, step + 1) for step, message in enumerate(messages)]

    squares, chunks = call(
        weights_body,
        [((8, 128), F32), ((8, 112, 2 * HD), BF16)],
        place,
        dout,
        columns,
        dout_1,
        dout_3,
        *dout_2,
    )
    chunks = lax.all_to_all(after(chunks, *arrived), "dp", split_axis=0, concat_axis=0, tiled=True)
    for axis in ("core", "x", "tensor"):
        squares = lax.optimization_barrier(lax.psum(squares, axis))
    (input_grad,) = call(
        input_body,
        [((1, TOK, SLAB), BF16)],
        place,
        own,
        own_sum,
        *arrived,
        moved,
        inverse,
        gain,
        permute,
        room=60,
    )
    chunks, squares = lax.optimization_barrier((chunks, squares))
    spread = jnp.broadcast_to(squares[None], (8, 8, 128))
    spread = lax.all_to_all(spread, "dp", split_axis=0, concat_axis=0, tiled=True)
    squares = jnp.sum(after(spread, input_grad), 0)
    upper, lower = chunks[:, :ROWS], chunks[:, ROWS:]
    rms = jnp.sqrt(squares[:, :1] * (1.0 / (D * (H + 2 * KVH) * HD)) + EPSILON)
    factor = (CLIP_BOUND / jnp.maximum(rms, CLIP_BOUND))[:, :, None]
    mine_out = jnp.where(first, upper, lower)
    got_out = swap(jnp.where(first, lower, upper))
    mine_out, got_out = (
        jnp.sum(one.astype(F32) * factor, 0) for one in (mine_out, got_out)
    )
    zero = jnp.where(first, mine_out, got_out)
    one = jnp.where(first, got_out, mine_out)
    grad_query = jnp.concatenate([zero[:, :HD], one[:, :HD]], 1)
    grad_key, grad_value = zero[:, HD:], one[:, HD:]
    return grad_query, grad_key, grad_value, input_grad


def solution(mesh):
    chips = Mesh(mesh.devices.reshape(4, 2, 4, 8), ("x", "core", "tensor", "dp"))
    seq = ("x", "core")
    weight = P((*seq, "dp"), "tensor")
    return jax.shard_map(
        local,
        mesh=chips,
        in_specs=(P("dp", seq, None), weight, weight, weight, P(), P("dp", seq, "tensor")),
        out_specs=(weight, weight, weight, P("dp", seq, "tensor")),
        check_vma=False,
    )
```

```python
import math

import jax
import jax.numpy as jnp
import numpy as np
from jax import lax
from jax.experimental import pallas as pl
from jax.experimental.pallas import tpu as pltpu
from jax.sharding import Mesh
from jax.sharding import PartitionSpec as P

D = 3584
H = 8
KVH = 4
HD = 256
WINDOW = 256
SLAB = D // 4
ROWS = 56
TOK = 256
CUT = 384

EPSILON = 1e-06
SOFTCAP = 50.0
CLIP_BOUND = 1.0
ROPE_BASE = 10000.0

F32 = jnp.float32
BF16 = jnp.bfloat16
ANY = pl.BlockSpec(memory_space=pl.ANY)
SMEM = pl.BlockSpec(memory_space=pltpu.SMEM)


class Arriving:
    def __init__(self, copy, ref):
        self.copy, self.ref, self.here = copy, ref, False

    def wait(self):
        if not self.here:
            self.copy.wait()
            self.here = True

    def __getitem__(self, at):
        self.wait()
        return self.ref[at]


class Leaving:
    def __init__(self, copy, ref):
        self.copy, self.ref, self.gone = copy, ref, False

    def __getitem__(self, at):
        return self.ref[at]

    def __setitem__(self, at, value):
        self.ref[at] = value

    def leave(self):
        if not self.gone:
            self.copy.start()
            self.gone = True


def call(body, outs, place, *operands, scratch=(), room=16):
    count, made = len(operands), len(outs)

    def kernel(place_ref, *refs):
        held = refs[count + made : 2 * (count + made)]
        sems = refs[2 * (count + made)]
        rest = refs[2 * (count + made) + 1 :]
        arriving = []
        for k in range(count):
            copy = pltpu.make_async_copy(refs[k], held[k], sems.at[k])
            copy.start()
            arriving.append(Arriving(copy, held[k]))
        leaving = []
        for k in range(count, count + made):
            copy = pltpu.make_async_copy(held[k], refs[k], sems.at[k])
            leaving.append(Leaving(copy, held[k]))
        body(place_ref, *arriving, *leaving, *rest)
        for one in leaving:
            one.leave()
        for one in arriving:
            one.wait()
        for one in leaving:
            one.copy.wait()

    return pl.pallas_call(
        kernel,
        out_shape=[jax.ShapeDtypeStruct(shape, kind) for shape, kind in outs],
        in_specs=[SMEM] + [ANY] * count,
        out_specs=[ANY] * made,
        scratch_shapes=[pltpu.VMEM(one.shape, one.dtype) for one in operands]
        + [pltpu.VMEM(shape, kind) for shape, kind in outs]
        + [pltpu.SemaphoreType.DMA((count + made,))]
        + list(scratch),
        compiler_params=pltpu.CompilerParams(vmem_limit_bytes=room * 1024 * 1024),
    )(place, *operands)


def swap(value):
    return lax.ppermute(value, "core", [(0, 1), (1, 0)])


def from_x(value, steps):
    return lax.ppermute(value, "x", [((i + steps) % 4, i) for i in range(4)])


def from_y(value, steps):
    return lax.ppermute(value, "tensor", [((i + steps) % 4, i) for i in range(4)])


def from_z(value, steps):
    return lax.ppermute(value, "dp", [((i + steps) % 8, i) for i in range(8)])


def after(value, *others):
    return lax.optimization_barrier((value, *others))[0]


def code(total):
    high = total.astype(BF16)
    rest = total - high.astype(F32)
    middle = rest.astype(BF16)
    low = (rest - middle.astype(F32)).astype(BF16)
    lane = lax.broadcasted_iota(jnp.int32, total.shape, 1)
    return jnp.where(
        lane == 0,
        high.astype(F32),
        jnp.where(
            lane == 1, middle.astype(F32), jnp.where(lane == 2, low.astype(F32), jnp.zeros_like(total))
        ),
    ).astype(BF16)


def mm(a, b, contract_a=1, contract_b=0):
    return lax.dot_general(
        a, b, (((contract_a,), (contract_b,)), ((), ())), preferred_element_type=F32
    )


def norm_body(place, permute, gain, inputs, normed, n0, q1, q2, q3, moved, inverse, moved_gain):
    x, y = place[0], place[2]
    wide = gain[...]
    high = wide.astype(BF16)
    middle = (wide - high.astype(F32)).astype(BF16)
    low = (wide - high.astype(F32) - middle.astype(F32)).astype(BF16)
    moved_gain[...] = mm(high, permute[...]) + mm(middle, permute[...]) + mm(low, permute[...])
    rows = inputs[...].astype(F32)
    inv = lax.rsqrt(jnp.sum(rows * rows, -1, keepdims=True) * (1.0 / D) + EPSILON)
    inverse[...] = jnp.broadcast_to(inv, inverse.ref.shape)
    for slab in range(4):
        part = mm(inputs[:, slab * SLAB : (slab + 1) * SLAB], permute[...])
        moved[slab] = part.astype(BF16)
        normed[slab] = (part * inv * moved_gain[slab : slab + 1, :]).astype(BF16)
    normed.leave()
    quarter = pl.ds(pl.multiple_of(y * 64, 64), 64)
    for step, one in ((1, q1), (2, q2), (3, q3)):
        one[...] = normed[lax.rem(x + 4 - step, 4), quarter, :]
        one.leave()
    n0[...] = normed[x]


def stack_body(place, own, far, up2, down2, up, down, top, bottom, whole):
    z = place[3]

    def put(step, rows):
        at = lax.rem(z + step, 8) * 112
        whole[pl.ds(pl.multiple_of(at, 16), 112), :] = rows

    put(0, own[...])
    put(4, far[...])
    put(2, up2[...])
    put(6, down2[...])
    put(1, up[:112, :])
    put(5, up[112:, :])
    put(7, down[:112, :])
    put(3, down[112:, :])
    top[...] = whole[:CUT, :]
    bottom[...] = whole[CUT:, :]


def columns_body(place, *refs):
    own, other, mine, theirs, whole, rows = refs[0], refs[1], refs[2:6], refs[6:10], refs[10], refs[11]
    x, core, y = place[0], place[1], place[2]
    for first, block, parts in ((own, core, mine), (other, 1 - core, theirs)):
        rows[x, pl.ds(pl.multiple_of(block * TOK, TOK), TOK), :] = first[...]
        for turn in range(4):
            at = pl.ds(pl.multiple_of(block * TOK + lax.rem(y + turn, 4) * 64, 64), 64)
            for step in range(1, 4):
                rows[lax.rem(x + step, 4), at, :] = parts[turn][(step - 1) * 64 : step * 64, :]
    for slab in range(4):
        whole[slab] = rows[slab].T


def spin(value, cosine, sine, direction):
    first, second = value[:, :128], value[:, 128:]
    return jnp.concatenate(
        [first * cosine - direction * second * sine, second * cosine + direction * first * sine], -1
    )


PIECES = tuple((step, start, stop) for step in (0, 1, 3, 2) for start, stop in ((0, CUT), (CUT, SLAB)))


def project_body(place, own, s0, s1, other, s2, s3, s4, s5, total, last):
    x = place[0]
    for turn, ((step, start, stop), slab) in enumerate(zip(PIECES, (s0, s1, s2, s3, s4, s5))):
        here = lax.rem(x + step, 4)
        for half, rows in enumerate((own, other)):
            part = mm(rows[here, :, start:stop], slab[...])
            total[half] = part if turn == 0 else total[half] + part
    for half, rows in enumerate((own, other)):
        last[half] = rows[lax.rem(x + 2, 4)]


def finish_body(place, last, s6, s7, total, cos2, sin2, cos, sin, pair, query):
    core = place[1]
    sums = []
    for half in range(2):
        sums.append(total[half] + mm(last[half, :, :CUT], s6[...]) + mm(last[half, :, CUT:], s7[...]))
    for half, block in ((0, core), (1, 1 - core)):
        at = pl.ds(pl.multiple_of(block * TOK, TOK), TOK)
        pair[at, :] = spin(sums[half][:, HD:], cos2[at, :], sin2[at, :], 1.0).astype(BF16)
    pair.leave()
    for half, block in ((0, core), (1, 1 - core)):
        at = pl.ds(pl.multiple_of(block * TOK, TOK), TOK)
        query[at, :] = spin(sums[half][:, :HD], cos[at, :], sin[at, :], 1.0).astype(BF16)


def attend_body(place, query, mine, theirs, mine_before, theirs_before, cot, cos, sin,
                dquery, keep, keep_before, send, send_before, keys, values):
    first_core = place[1] == 0
    for at, a, b in ((0, mine_before, theirs_before), (TOK, mine, theirs)):
        rows = a.ref.shape[0]
        keys[at : at + rows, :] = jnp.where(first_core, a[...], b[...])
        values[at : at + rows, :] = jnp.where(first_core, b[...], a[...])
    scale = 1.0 / math.sqrt(HD)
    q_at = lax.broadcasted_iota(jnp.int32, (TOK, 2 * TOK), 0)
    k_at = lax.broadcasted_iota(jnp.int32, (TOK, 2 * TOK), 1)
    band = (k_at <= q_at + TOK) & (k_at > q_at)
    key_parts = []
    value_parts = []
    for block in range(2):
        here = slice(block * TOK, (block + 1) * TOK)
        seen = slice(block * TOK, (block + 2) * TOK)
        q, g = query[here, :], cot[here, :]
        k, v = keys[seen, :], values[seen, :]
        squash = jnp.tanh(mm(q, k, 1, 1) * (scale / SOFTCAP))
        allowed = band
        if block == 0:
            allowed = band & ((k_at >= TOK) | (place[0] > 0))
        terms = jnp.where(allowed, jnp.exp(SOFTCAP * squash), 0.0)
        probs = terms / jnp.sum(terms, -1, keepdims=True)
        dprobs = mm(g, v, 1, 1)
        value_parts.append(mm(probs.astype(BF16), g, 0, 0))
        delta = jnp.sum(probs * dprobs, -1, keepdims=True)
        dlogits = (probs * (dprobs - delta) * (1.0 - squash * squash) * scale).astype(BF16)
        dq = mm(dlogits, k)
        dquery[here, :] = spin(dq, cos[here, :], sin[here, :], -1.0).astype(BF16)
        key_parts.append(mm(dlogits, q, 0, 0))

    def place_out(dk, dv, keep_at, send_at, here):
        keep_at[here, :] = jnp.where(first_core, dk, dv)
        send_at[here, :] = jnp.where(first_core, dv, dk).astype(BF16)

    place_out(key_parts[0][:TOK], value_parts[0][:TOK], keep_before, send_before, slice(0, TOK))
    place_out(
        key_parts[0][TOK:] + key_parts[1][:TOK],
        value_parts[0][TOK:] + value_parts[1][:TOK],
        keep,
        send,
        slice(0, TOK),
    )
    place_out(key_parts[1][TOK:], value_parts[1][TOK:], keep, send, slice(TOK, 2 * TOK))


def halo_body(place, keep_before, got_before, out):
    out[...] = (keep_before[...] + got_before[...].astype(F32)).astype(BF16)


def pair_body(place, dquery, keep, got, cos2, sin2, back, dout):
    dout[:, :HD] = dquery[...]
    for block in range(2):
        here = slice(block * TOK, (block + 1) * TOK)
        total = keep[here, :] + got[here, :].astype(F32)
        if block == 1:
            total += back[...].astype(F32)
        dout[here, HD:] = spin(total, cos2[here, :], sin2[here, :], -1.0).astype(BF16)


def dnormed_body(
    place, dout, s0, s1, other, s2, s3, s4, s5, s6, s7, own, send, send_sum, keep, keep_sum
):
    x, core = place[0], place[1]
    for rows, block, out, sums in (
        (other, 1 - core, send, send_sum),
        (own, core, keep, keep_sum),
    ):
        d = dout[pl.ds(pl.multiple_of(block * TOK, TOK), TOK), :]
        total = jnp.zeros((TOK, 1), F32)
        for (step, start, stop), slab in zip(PIECES, (s0, s1, s2, s3, s4, s5, s6, s7)):
            here = lax.rem(x + step, 4)
            part = mm(d, slab[...], 1, 1)
            total += jnp.sum(part * rows[here, :, start:stop].astype(F32), -1, keepdims=True)
            out[here, :, start:stop] = part.astype(BF16)
        sums[...] = jnp.broadcast_to(total, sums.ref.shape)
        out.leave()
        sums.leave()


def split_body(place, keep, got, keep_sum, got_sum, m1, m2, m3, own, own_sum):
    y = place[2]
    total = keep_sum[...] + got_sum[...]
    own_sum[...] = total
    coded = code(total)
    for step, message in enumerate((m1, m2, m3)):
        at = lax.rem(y + 4 - (step + 1), 4)
        message[:, :SLAB] = (keep[at].astype(F32) + got[at].astype(F32)).astype(BF16)
        message[:, SLAB:] = coded
        message.leave()
    own[...] = keep[y].astype(F32) + got[y].astype(F32)


def input_body(place, own, own_sum, m1, m2, m3, moved, inverse, gain, permute, out):
    total = own[...]
    sums = own_sum[:, :1]
    for message in (m1, m2, m3):
        total += message[:, :SLAB].astype(F32)
        sums += jnp.sum(message[:, SLAB:].astype(F32), -1, keepdims=True)
    inv = inverse[:, :1]
    y = place[2]
    rows = moved[y].astype(F32)
    grad = inv * (gain[pl.ds(y, 1), :] * total) - rows * ((inv * inv) * (sums * (1.0 / D)))
    out[0] = mm(grad.astype(BF16), permute[...], 1, 1).astype(BF16)


def weights_body(place, d0, columns, d1, d3, d2a, d2b, squares, chunks):
    x, z = place[0], place[3]
    acc = mm(columns[x], d0[...])
    for step, d in ((1, d1), (3, d3)):
        acc += mm(columns[lax.rem(x + step, 4)], d[...])
    far = lax.rem(x + 2, 4)
    acc += mm(columns[far, :, :TOK], d2a[...]) + mm(columns[far, :, TOK:], d2b[...])
    for chunk in range(8):
        chunks[chunk] = acc[chunk * 112 : (chunk + 1) * 112, :].astype(BF16)
    chunks.leave()
    row = lax.broadcasted_iota(jnp.int32, (8, 128), 0)
    squares[...] = jnp.where(row == z, jnp.sum(acc * acc), 0.0)


def local(inputs, w_query, w_key, w_value, norm_gain, attn_grad):
    x = lax.axis_index("x").astype(jnp.int32)
    core = lax.axis_index("core").astype(jnp.int32)
    y = lax.axis_index("tensor").astype(jnp.int32)
    z = lax.axis_index("dp").astype(jnp.int32)
    place = jnp.stack([x, core, y, z])
    first = core == 0

    low, high = w_query[:, :HD], w_query[:, HD:]
    mine = jnp.concatenate([jnp.where(first, low, high), jnp.where(first, w_key, w_value)], 1)
    theirs = jnp.concatenate([jnp.where(first, high, low), jnp.where(first, w_value, w_key)], 1)
    got = swap(theirs)
    block = jnp.concatenate([jnp.where(first, mine, got), jnp.where(first, got, mine)], 0)
    index = np.arange(SLAB)
    natural = (index % 112) // ROWS * 448 + index // 112 * ROWS + index % ROWS
    permute = (
        lax.broadcasted_iota(jnp.int32, (SLAB, SLAB), 0) == jnp.asarray(natural, jnp.int32)[None, :]
    ).astype(BF16)
    cot_low, cot_high = attn_grad[0][:, :HD], attn_grad[0][:, HD:]
    cot_mine = jnp.where(first, cot_low, cot_high)
    cot_got = swap(jnp.where(first, cot_high, cot_low))
    gain_rows = norm_gain.reshape(4, SLAB)
    far = from_z(block, 4)
    up2, down2 = from_z(block, 2), from_z(block, -2)
    far, up2, down2, permute, cot_got, gain_rows, place = lax.optimization_barrier(
        (far, up2, down2, permute, cot_got, gain_rows, place)
    )
    both = jnp.concatenate([block, far], 0)
    up, down = from_z(both, 1), from_z(both, -1)

    normed, own_columns, *quarters, moved, inverse, gain = call(
        norm_body,
        [((4, TOK, SLAB), BF16), ((TOK, SLAB), BF16)]
        + [((TOK // 4, SLAB), BF16)] * 3
        + [((4, TOK, SLAB), BF16), ((TOK, 128), F32), ((4, SLAB), F32)],
        place,
        permute,
        gain_rows,
        after(inputs[0], far),
        room=60,
    )
    top, bottom = call(
        stack_body,
        [((CUT, 2 * HD), BF16), ((SLAB - CUT, 2 * HD), BF16)],
        place,
        after(block, normed),
        far,
        up2,
        down2,
        up,
        down,
        scratch=[pltpu.VMEM((SLAB, 2 * HD), BF16)],
    )
    *quarters, _, _ = lax.optimization_barrier((*quarters, up, down))
    quarters = [from_x(one, step + 1) for step, one in enumerate(quarters)]
    near = (from_x(top, 1), from_x(bottom, 1), from_x(top, -1), from_x(bottom, -1))
    near = lax.optimization_barrier(near)
    normed_other = swap(after(normed, *near))
    *quarters, normed_other = lax.optimization_barrier((*quarters, normed_other))
    bundle = jnp.concatenate(quarters, 0)
    slabs = (top, bottom, *near, from_x(near[0], 1), from_x(near[3], -1))
    bundles = (bundle, from_y(bundle, 1), from_y(bundle, 2), from_y(bundle, 3))
    theirs = [swap(one) for one in (bundles[0], bundles[1], bundles[3])]
    theirs_own = swap(own_columns)

    cot = jnp.concatenate(
        [jnp.where(first, cot_mine, cot_got), jnp.where(first, cot_got, cot_mine)], 0
    )

    positions = x * (2 * TOK) + jnp.arange(2 * TOK, dtype=jnp.int32)
    frequency = ROPE_BASE ** (-2.0 * jnp.arange(HD // 2).astype(F32) / HD)
    phases = positions.astype(F32)[:, None] * frequency[None, :]
    cos, sin = jnp.cos(phases), jnp.sin(phases)
    cos2, sin2 = jnp.where(first, cos, 1.0), jnp.where(first, sin, 0.0)

    normed_other, cos, sin, cos2, sin2 = lax.optimization_barrier(
        (normed_other, cos, sin, cos2, sin2)
    )
    total, last = call(
        project_body,
        [((2, TOK, 2 * HD), F32), ((2, TOK, SLAB), BF16)],
        place,
        normed,
        *slabs[:2],
        normed_other,
        *slabs[2:6],
    )
    pair, query = call(
        finish_body,
        [((2 * TOK, HD), BF16), ((2 * TOK, HD), BF16)],
        place,
        last,
        *slabs[6:],
        after(total, bundles[1], bundles[3]),
        cos2,
        sin2,
        cos,
        sin,
    )
    pair_other = swap(pair)
    before = from_x(pair[TOK:], -1)
    before_other = swap(before)
    dquery, keep, keep_before, send, send_before = call(
        attend_body,
        [
            ((2 * TOK, HD), BF16),
            ((2 * TOK, HD), F32),
            ((TOK, HD), F32),
            ((2 * TOK, HD), BF16),
            ((TOK, HD), BF16),
        ],
        place,
        query,
        pair,
        pair_other,
        before,
        before_other,
        cot,
        cos,
        sin,
        scratch=[pltpu.VMEM((3 * TOK, HD), BF16), pltpu.VMEM((3 * TOK, HD), BF16)],
    )
    got_before = swap(send_before)
    got = swap(send)
    (back,) = call(halo_body, [((TOK, HD), BF16)], place, keep_before, got_before)
    back = from_x(back, 1)
    theirs.insert(2, swap(after(bundles[2], back)))
    (columns,) = call(
        columns_body,
        [((4, SLAB, 2 * TOK), BF16)],
        place,
        own_columns,
        theirs_own,
        *bundles,
        *theirs,
        scratch=[pltpu.VMEM((4, 2 * TOK, SLAB), BF16)],
    )
    (dout,) = call(
        pair_body, [((2 * TOK, 2 * HD), BF16)], place, dquery, keep, got, cos2, sin2, back
    )
    dout_1, dout_3 = lax.optimization_barrier((from_x(dout, 1), from_x(dout, 3)))
    dout_2 = (from_x(dout_1[:TOK], 1), from_x(dout_3[TOK:], -1))

    send_in, send_sum, keep_in, keep_sum = call(
        dnormed_body,
        [((4, TOK, SLAB), BF16), ((TOK, 128), F32)] * 2,
        place,
        dout,
        *slabs[:2],
        normed_other,
        *slabs[2:],
        after(normed, theirs_own, *theirs),
    )
    got_in, got_sum = swap(send_in), swap(send_sum)
    *messages, own, own_sum = call(
        split_body,
        [((TOK, SLAB + 128), BF16)] * 3 + [((TOK, SLAB), F32), ((TOK, 128), F32)],
        place,
        keep_in,
        got_in,
        keep_sum,
        got_sum,
    )
    arrived = [from_y(message, step + 1) for step, message in enumerate(messages)]

    squares, chunks = call(
        weights_body,
        [((8, 128), F32), ((8, 112, 2 * HD), BF16)],
        place,
        dout,
        columns,
        dout_1,
        dout_3,
        *dout_2,
    )
    chunks = lax.all_to_all(after(chunks, *arrived), "dp", split_axis=0, concat_axis=0, tiled=True)
    for axis in ("core", "x", "tensor"):
        squares = lax.optimization_barrier(lax.psum(squares, axis))
    (input_grad,) = call(
        input_body,
        [((1, TOK, SLAB), BF16)],
        place,
        own,
        own_sum,
        *arrived,
        moved,
        inverse,
        gain,
        permute,
        room=60,
    )
    chunks, squares = lax.optimization_barrier((chunks, squares))
    spread = jnp.broadcast_to(squares[None], (8, 8, 128))
    spread = lax.all_to_all(spread, "dp", split_axis=0, concat_axis=0, tiled=True)
    squares = jnp.sum(after(spread, input_grad), 0)
    upper, lower = chunks[:, :ROWS], chunks[:, ROWS:]
    rms = jnp.sqrt(squares[:, :1] * (1.0 / (D * (H + 2 * KVH) * HD)) + EPSILON)
    factor = (CLIP_BOUND / jnp.maximum(rms, CLIP_BOUND))[:, :, None]
    mine_out = jnp.where(first, upper, lower)
    got_out = swap(jnp.where(first, lower, upper))
    mine_out, got_out = (
        jnp.sum(one.astype(F32) * factor, 0) for one in (mine_out, got_out)
    )
    zero = jnp.where(first, mine_out, got_out)
    one = jnp.where(first, got_out, mine_out)
    grad_query = jnp.concatenate([zero[:, :HD], one[:, :HD]], 1)
    grad_key, grad_value = zero[:, HD:], one[:, HD:]
    return grad_query, grad_key, grad_value, input_grad


def solution(mesh):
    chips = Mesh(mesh.devices.reshape(4, 2, 4, 8), ("x", "core", "tensor", "dp"))
    seq = ("x", "core")
    weight = P((*seq, "dp"), "tensor")
    return jax.shard_map(
        local,
        mesh=chips,
        in_specs=(P("dp", seq, None), weight, weight, weight, P(), P("dp", seq, "tensor")),
        out_specs=(weight, weight, weight, P("dp", seq, "tensor")),
        check_vma=False,
    )
```
